256 devices in a mesh: node: 32 (over y, x, core), dev: 8 (over z).
Axes of the slice: x: 4, y: 4, z: 8, core: 2. Of those that a mesh axis runs over, the one named last changes fastest.
Arguments:
- element_load: float32 [8, 8, 8, 8, 64, 128], P(None, None, None, 'dev', 'node'), may hold values from -4 to 5
- diffusivity: float32 [8, 64, 128], P('dev', 'node'), may hold values from 0.2 to 5
Outputs:
- solution: float32 [8, 8, 8, 8, 64, 128], P(None, None, None, 'dev', 'node')
The draws below stay inside these ranges and needn't reach their ends.
All inputs are finite; a program needn't handle non-finite values.
Results may differ from the reference program's by a relative error of at most 0.0003.
Values sent between devices are 32-bit elements; how exact they have to be, the bound alone decides.
A program may use at most 128 MiB of HBM per device.

```python
import math
import jax
import jax.numpy as jnp
import numpy as np
from jax import lax

PF = 8
PM = 4
PC = 2
SMOOTH_FINE = 3
SMOOTH_MID = 3
COARSE_ITERS = 5
EX = 8
EY = 128
EZ = 64


def draw_element_load(key, part):
    key = jax.random.fold_in(key, 7)
    first_key = jax.random.fold_in(key, 0)
    full_shape = (PF, PF, PF, EX, EZ, EY)
    random_part = jax.random.truncated_normal(first_key, -4.0, 4.0, full_shape, jnp.float32)
    return random_part


def block_levels(stream_key, dims, cuts, low, high):
    level = 1.0
    for position, shards_of in cuts:
        draws = jax.random.uniform(jax.random.fold_in(jax.random.fold_in(stream_key, 6), position), (shards_of,), jnp.float32, low / len(cuts), high / len(cuts))
        level = level * jnp.repeat(jnp.exp(draws), dims[position] // shards_of).reshape((-1,) + (1,) * (len(dims) - 1 - position))
    return level


def setup_inputs(seed: int = 0) -> dict:
    key_of = jax.random.split(jax.random.key(seed), 3)
    return {
        "element_load": draw_element_load(jax.random.fold_in(key_of[2], 71), 0),
        "diffusivity": jnp.clip(jnp.exp(math.log(5.0) - 3.218876 * jax.random.uniform(key_of[1], (EX, EZ, EY), jnp.float32) ** block_levels(key_of[1], (EX, EZ, EY), ((0, 8), (1, 32)), -0.2, 0.2)), 0.2, 5.0),
    }


SHIFT_MASS = 0.05
FACE_ELEM = (2, 4, 3)

def legendre_values(points, poly_order):
    columns = [points * 0.0 + 1.0, points]
    for degree in range(2, poly_order + 1):
        columns.append(((2 * degree - 1) * points * columns[degree - 1] - (degree - 1) * columns[degree - 2]) / degree)
    return np.stack(columns[:poly_order + 1], axis=1)

def largest_eigen(matrix):
    size_n = matrix.shape[0]
    vector = np.cos(2.7 * np.arange(size_n) + 0.3)
    for power_step in range(4000):
        vector = matrix @ vector
        vector = vector / np.sqrt(np.sum(vector * vector))
    return float(vector @ (matrix @ vector))

def gll_level(poly_order):
    point_count = poly_order + 1
    gll_nodes = np.cos(np.pi * np.arange(point_count) / poly_order)
    for newton_step in range(60):
        values = legendre_values(gll_nodes, poly_order)
        gll_nodes = gll_nodes - (gll_nodes * values[:, poly_order] - values[:, poly_order - 1]) / (point_count * values[:, poly_order])
    gll_nodes = np.sort(gll_nodes)
    values = legendre_values(gll_nodes, poly_order)
    top_value = values[:, poly_order]
    weights = 2.0 / (poly_order * point_count * top_value ** 2)
    deriv_matrix = np.zeros((point_count, point_count))
    for row_index in range(point_count):
        for col_index in range(point_count):
            if row_index != col_index:
                deriv_matrix[row_index, col_index] = top_value[row_index] / (top_value[col_index] * (gll_nodes[row_index] - gll_nodes[col_index]))
    deriv_matrix[0, 0] = -poly_order * point_count / 4.0
    deriv_matrix[poly_order, poly_order] = poly_order * point_count / 4.0
    stiffness = deriv_matrix.T @ (weights[:, None] * deriv_matrix)
    diag_ids = np.arange(point_count)
    stiff_diag = stiffness[diag_ids, diag_ids]
    diag_scale = 1.0 / np.sqrt(stiff_diag)
    eig_bound = largest_eigen(diag_scale[:, None] * stiffness * diag_scale[None, :])
    return (gll_nodes, weights, deriv_matrix, stiff_diag, eig_bound)

def interp_table(fine_nodes, coarse_nodes):
    interp_mat = np.ones((fine_nodes.shape[0], coarse_nodes.shape[0]))
    for col_index in range(coarse_nodes.shape[0]):
        for other_index in range(coarse_nodes.shape[0]):
            if other_index != col_index:
                interp_mat[:, col_index] *= (fine_nodes - coarse_nodes[other_index]) / (coarse_nodes[col_index] - coarse_nodes[other_index])
    return jnp.asarray(interp_mat, jnp.float32)

def level_data(poly_order):
    gll_nodes, weights, deriv_matrix, stiff_diag, eig_bound = gll_level(poly_order)
    return (gll_nodes, jnp.asarray(weights, jnp.float32), jnp.asarray(deriv_matrix, jnp.float32), jnp.asarray(stiff_diag, jnp.float32), eig_bound)

def apply_along(matrix, values, axis_index):
    einsum_forms = ('ia,abcxyz->ibcxyz', 'jb,abcxyz->ajcxyz', 'kc,abcxyz->abkxyz')
    return jnp.einsum(einsum_forms[axis_index], matrix, values, precision=lax.Precision.HIGHEST)

def tensor_weights(weights):
    return (weights[:, None, None] * weights[None, :, None] * weights[None, None, :])[:, :, :, None, None, None]

def local_operator(values, diffusivity, deriv_matrix, weights):
    volume = tensor_weights(weights)
    scaled = volume * diffusivity[None, None, None]
    summed = SHIFT_MASS * volume * values
    for axis_index in range(3):
        summed = summed + apply_along(deriv_matrix.T, scaled * apply_along(deriv_matrix, values, axis_index), axis_index)
    return summed

def diag_local(diffusivity, weights, stiff_diag):
    wgt = weights
    pattern = stiff_diag[:, None, None] * wgt[None, :, None] * wgt[None, None, :] + wgt[:, None, None] * stiff_diag[None, :, None] * wgt[None, None, :] + wgt[:, None, None] * wgt[None, :, None] * stiff_diag[None, None, :]
    return diffusivity[None, None, None] * pattern[:, :, :, None, None, None] + SHIFT_MASS * tensor_weights(weights)

def face_sums(values, point_axis, side_fn):
    point_count = values.shape[point_axis]
    elem_axis = FACE_ELEM[point_axis]
    lower_face = lax.index_in_dim(values, 0, point_axis, keepdims=False)
    upper_face = lax.index_in_dim(values, point_count - 1, point_axis, keepdims=False)
    left_upper, right_lower = side_fn(lower_face, upper_face, elem_axis)
    shared = jnp.concatenate([left_upper, upper_face], elem_axis) + jnp.concatenate([lower_face, right_lower], elem_axis)
    blocks = lower_face.shape[elem_axis]
    new_lower = lax.slice_in_dim(shared, 0, blocks, axis=elem_axis)
    new_upper = lax.slice_in_dim(shared, 1, blocks + 1, axis=elem_axis)
    middle = lax.slice_in_dim(values, 1, point_count - 1, axis=point_axis)
    return jnp.concatenate([jnp.expand_dims(new_lower, point_axis), middle, jnp.expand_dims(new_upper, point_axis)], point_axis)

def closed_side(lower_face, upper_face, elem_axis):
    return (jnp.zeros_like(lax.slice_in_dim(upper_face, 0, 1, axis=elem_axis)), jnp.zeros_like(lax.slice_in_dim(lower_face, 0, 1, axis=elem_axis)))

def periodic_side(lower_face, upper_face, elem_axis):
    blocks = upper_face.shape[elem_axis]
    return (lax.slice_in_dim(upper_face, blocks - 1, blocks, axis=elem_axis), lax.slice_in_dim(lower_face, 0, 1, axis=elem_axis))

def assemble(values, x_side, y_side, z_side):
    values = face_sums(values, 0, x_side)
    values = face_sums(values, 1, y_side)
    return face_sums(values, 2, z_side)

def inverse_copies(points, count_x, count_y, x_start, y_start, x_total, y_total):
    point_ids = jnp.arange(points, dtype=jnp.int32)
    first_point = point_ids == 0
    last_point = point_ids == points - 1
    x_global = x_start + jnp.arange(count_x, dtype=jnp.int32)
    y_global = y_start + jnp.arange(count_y, dtype=jnp.int32)
    mult_x = 1 + (first_point[:, None] & (x_global > 0)[None, :]).astype(jnp.int32) + (last_point[:, None] & (x_global < x_total - 1)[None, :]).astype(jnp.int32)
    mult_y = 1 + (first_point[:, None] & (y_global > 0)[None, :]).astype(jnp.int32) + (last_point[:, None] & (y_global < y_total - 1)[None, :]).astype(jnp.int32)
    mult_z = 1 + first_point.astype(jnp.int32) + last_point.astype(jnp.int32)
    copies = mult_x[:, None, None, :, None, None] * mult_y[None, :, None, None, None, :] * mult_z[None, None, :, None, None, None]
    return 1.0 / copies.astype(jnp.float32)

def chebyshev(operator, right_side, initial, inverse_diag, eig_bound, step_count):
    lower_bound = 0.1 * eig_bound
    upper_bound = 1.1 * eig_bound
    center = 0.5 * (upper_bound + lower_bound)
    radius = 0.5 * (upper_bound - lower_bound)
    ratio_sig = center / radius
    rho_prev = 1.0 / ratio_sig
    if initial is None:
        iterate = jnp.zeros_like(right_side)
        residual = right_side
    else:
        iterate = initial
        residual = right_side - operator(initial)
    update = inverse_diag * residual / center
    for step_index in range(step_count):
        iterate = iterate + update
        if step_index + 1 < step_count:
            residual = residual - operator(update)
            rho_next = 1.0 / (2.0 * ratio_sig - rho_prev)
            update = rho_next * rho_prev * update + 2.0 * rho_next / radius * inverse_diag * residual
            rho_prev = rho_next
    return iterate

def conj_grad(operator, right_side, dot_global, iter_count):
    iterate = jnp.zeros_like(right_side)
    residual = right_side
    direction = right_side
    norm_now = dot_global(residual, residual)
    for step_index in range(iter_count):
        image_vec = operator(direction)
        step_len = norm_now / dot_global(direction, image_vec)
        iterate = iterate + step_len * direction
        residual = residual - step_len * image_vec
        norm_next = dot_global(residual, residual)
        direction = residual + norm_next / norm_now * direction
        norm_now = norm_next
    return iterate

def restrict(matrix, values):
    for axis_index in range(3):
        values = apply_along(matrix.T, values, axis_index)
    return values

def prolong(matrix, values):
    for axis_index in range(3):
        values = apply_along(matrix, values, axis_index)
    return values

def reference(element_load, diffusivity):
    nodes_fine, w_fine, d_fine, k_fine, bound_fine = level_data(PF - 1)
    nodes_mid, w_mid, d_mid, k_mid, bound_mid = level_data(PM - 1)
    nodes_low, w_low, d_low, k_low, bound_low = level_data(PC - 1)
    j_fine = interp_table(nodes_fine, nodes_mid)
    j_mid = interp_table(nodes_mid, nodes_low)

    def gather_sum(values):
        return assemble(values, closed_side, closed_side, periodic_side)

    def op_fine(values):
        return gather_sum(local_operator(values, diffusivity, d_fine, w_fine))

    def op_mid(values):
        return gather_sum(local_operator(values, diffusivity, d_mid, w_mid))

    def op_low(values):
        return gather_sum(local_operator(values, diffusivity, d_low, w_low))
    inv_fine = inverse_copies(PF, EX, EY, 0, 0, EX, EY)
    inv_mid = inverse_copies(PM, EX, EY, 0, 0, EX, EY)
    inv_low = inverse_copies(PC, EX, EY, 0, 0, EX, EY)

    def dot_global(left_vec, right_vec):
        return jnp.sum(inv_low * left_vec * right_vec)
    forcing = gather_sum(element_load)
    dinv_fine = 1.0 / gather_sum(diag_local(diffusivity, w_fine, k_fine))
    dinv_mid = 1.0 / gather_sum(diag_local(diffusivity, w_mid, k_mid))
    x_fine = chebyshev(op_fine, forcing, None, dinv_fine, bound_fine, SMOOTH_FINE)
    rhs_mid = gather_sum(restrict(j_fine, inv_fine * (forcing - op_fine(x_fine))))
    x_mid = chebyshev(op_mid, rhs_mid, None, dinv_mid, bound_mid, SMOOTH_MID)
    rhs_low = gather_sum(restrict(j_mid, inv_mid * (rhs_mid - op_mid(x_mid))))
    x_low = conj_grad(op_low, rhs_low, dot_global, COARSE_ITERS)
    x_mid = chebyshev(op_mid, rhs_mid, x_mid + prolong(j_mid, x_low), dinv_mid, bound_mid, SMOOTH_MID)
    return chebyshev(op_fine, forcing, x_fine + prolong(j_fine, x_mid), dinv_fine, bound_fine, SMOOTH_FINE)
```

```python
import jax
import jax.numpy as jnp
import numpy as np
from jax import lax
from jax.experimental import pallas as pl
from jax.experimental.pallas import tpu as pltpu
from jax.sharding import PartitionSpec as P

PF = 8
PM = 4
PC = 2
SMOOTH_FINE = 3
SMOOTH_MID = 3
COARSE_ITERS = 5
SHIFT_MASS = 0.05
LANES = 128
SUB = 8
MESH = pl.DeviceIdType.MESH

def legendre_values(points, poly_order):
    columns = [points * 0.0 + 1.0, points]
    for degree in range(2, poly_order + 1):
        columns.append(
            ((2 * degree - 1) * points * columns[degree - 1] - (degree - 1) * columns[degree - 2])
            / degree
        )
    return np.stack(columns[: poly_order + 1], axis=1)


def largest_eigen(matrix):
    size_n = matrix.shape[0]
    vector = np.cos(2.7 * np.arange(size_n) + 0.3)
    for power_step in range(4000):
        vector = matrix @ vector
        vector = vector / np.sqrt(np.sum(vector * vector))
    return float(vector @ (matrix @ vector))


def gll_level(poly_order):
    point_count = poly_order + 1
    gll_nodes = np.cos(np.pi * np.arange(point_count) / poly_order)
    for newton_step in range(60):
        values = legendre_values(gll_nodes, poly_order)
        gll_nodes = gll_nodes - (gll_nodes * values[:, poly_order] - values[:, poly_order - 1]) / (
            point_count * values[:, poly_order]
        )
    gll_nodes = np.sort(gll_nodes)
    values = legendre_values(gll_nodes, poly_order)
    top_value = values[:, poly_order]
    weights = 2.0 / (poly_order * point_count * top_value**2)
    deriv_matrix = np.zeros((point_count, point_count))
    for row_index in range(point_count):
        for col_index in range(point_count):
            if row_index != col_index:
                deriv_matrix[row_index, col_index] = top_value[row_index] / (
                    top_value[col_index] * (gll_nodes[row_index] - gll_nodes[col_index])
                )
    deriv_matrix[0, 0] = -poly_order * point_count / 4.0
    deriv_matrix[poly_order, poly_order] = poly_order * point_count / 4.0
    stiffness = deriv_matrix.T @ (weights[:, None] * deriv_matrix)
    diag_ids = np.arange(point_count)
    stiff_diag = stiffness[diag_ids, diag_ids]
    diag_scale = 1.0 / np.sqrt(stiff_diag)
    eig_bound = largest_eigen(diag_scale[:, None] * stiffness * diag_scale[None, :])
    return (gll_nodes, weights, deriv_matrix, stiff_diag, eig_bound)


def interp_table(fine_nodes, coarse_nodes):
    interp_mat = np.ones((fine_nodes.shape[0], coarse_nodes.shape[0]))
    for col_index in range(coarse_nodes.shape[0]):
        for other_index in range(coarse_nodes.shape[0]):
            if other_index != col_index:
                interp_mat[:, col_index] *= (fine_nodes - coarse_nodes[other_index]) / (
                    coarse_nodes[col_index] - coarse_nodes[other_index]
                )
    return interp_mat


class Level:
    def __init__(self, points):
        nodes, w, deriv, stiff_diag, bound = gll_level(points - 1)
        self.points = points
        self.planes = 2 * points - 1
        self.rows = SUB * self.planes
        self.nodes = nodes
        self.w = w
        self.khat = (deriv.T @ (w[:, None] * deriv)) / w[:, None]
        self.kdiag = stiff_diag / w
        self.theta = 0.6 * bound
        self.delta = 0.5 * bound

    def steps(self, count):
        sig = self.theta / self.delta
        rho = 1.0 / sig
        out = []
        for _ in range(count - 1):
            rho_next = 1.0 / (2.0 * sig - rho)
            out.append((float(rho_next * rho), float(2.0 * rho_next / self.delta)))
            rho = rho_next
        return out


def roll_coefs(matrix):
    full = np.zeros((SUB, SUB))
    full[: matrix.shape[0], : matrix.shape[1]] = matrix
    i = np.arange(SUB)
    return [full[i, (i - s) % SUB] for s in range(SUB)]


def two_elements(matrix):
    n, m = matrix.shape
    out = np.zeros((2 * n - 1, 2 * m - 1))
    out[:n, :m] = matrix
    out[n - 1 :, m - 1 :] = matrix
    return out


def plane_sum(points):
    values = np.zeros((2 * points - 1,))
    values[:points] += 1
    values[points - 1 :] += 1
    return values


class Consts:
    def __init__(self):
        self.blocks = []
        self.at = {}
        self.row = 0

    def add(self, name, block):
        block = np.asarray(block, np.float64)
        if block.ndim == 1:
            block = np.broadcast_to(block[:, None], (block.shape[0], LANES))
        assert block.shape[0] % SUB == 0
        self.at[name] = (self.row, block.shape[0])
        self.blocks.append(block)
        self.row += block.shape[0]

    def array(self):
        return np.concatenate(self.blocks, 0).astype(np.float32)


FINE, MID, LOW = Level(PF), Level(PM), Level(PC)
J73 = interp_table(FINE.nodes, MID.nodes)
J31 = interp_table(MID.nodes, LOW.nodes)
R73 = (FINE.w[:, None] * J73 / MID.w[None, :]).T
R31 = (MID.w[:, None] * J31).T
R73Z = two_elements(FINE.w[:, None] * J73 / MID.w[None, :])
R73Z[PF - 1] = 0.0
R73Z[PF - 1, PM - 1] = FINE.w[0] / MID.w[0]
R31Z = two_elements(MID.w[:, None] * J31)
R31Z[PM - 1] = 0.0
R31Z[PM - 1, PC - 1] = MID.w[0]
J73Z = two_elements(J73)
J31Z = two_elements(J31)

CONSTS = Consts()
for tag, level in (("f", FINE), ("m", MID)):
    CONSTS.add("ky" + tag, np.concatenate(roll_coefs(level.khat)))
    kb = np.zeros(SUB)
    kb[: level.points] = level.kdiag
    kz = np.concatenate([level.kdiag, level.kdiag[1:]])
    CONSTS.add("kzb" + tag, (kz[:, None] + kb[None, :]).reshape(-1))
    ey = np.arange(LANES)
    my = np.ones((SUB, LANES))
    my[0] += ey > 0
    my[level.points - 1] += ey < LANES - 1
    mz = np.ones(level.planes)
    mz[[0, level.points - 1, -1]] = 2
    CONSTS.add("cnt" + tag, (SHIFT_MASS * mz[:, None, None] * my[None]).reshape(-1, LANES))
CONSTS.add("r73", np.concatenate(roll_coefs(R73)))
CONSTS.add("j73", np.concatenate(roll_coefs(J73)))
CONSTS.add("r31", np.concatenate(roll_coefs(R31)))
CONSTS.add("j31", np.concatenate([np.pad(J31[:, p], (0, SUB - PM)) for p in range(PC)]))
CONSTS.add("iwb", 1.0 / FINE.w)

DIRS = ((-1, 0), (1, 0), (0, -1), (0, 1), (-1, -1), (-1, 1), (1, -1), (1, 1))
OPP = tuple(DIRS.index((-dx, -dz)) for dx, dz in DIRS)
COEF = 1e-13


def mix(matrix, parts):
    out = []
    for row in np.asarray(matrix):
        acc = None
        for c, v in zip(row, parts):
            if abs(c) > COEF:
                term = v if abs(c - 1.0) < COEF else float(c) * v
                acc = term if acc is None else acc + term
        out.append(acc)
    return out


def mix_even_odd(matrix, parts):
    n = len(parts)
    h = n // 2
    flipped = matrix[:h, ::-1][:, :h]
    even = mix(0.5 * (matrix[:h, :h] + flipped), [parts[i] + parts[n - 1 - i] for i in range(h)])
    odd = mix(0.5 * (matrix[:h, :h] - flipped), [parts[i] - parts[n - 1 - i] for i in range(h)])
    low = [e + o for e, o in zip(even, odd)]
    high = [e - o for e, o in zip(even, odd)]
    return low + high[::-1]


def scratch_shapes(n_node, n_dev):
    f32 = jnp.float32
    low_rows = -(-(3 * (n_dev + 1) + 1) // SUB) * SUB
    shapes = {}
    for tag, level in (("f", FINE), ("m", MID)):
        p, rows = level.points, level.rows
        for name in ("loc", "rhs", "inv", "x", "r", "d", "l"):
            shapes[name + tag] = pltpu.VMEM((p, rows, LANES), f32)
        shapes["cls" + tag] = pltpu.VMEM((3, rows, LANES), f32)
        shapes["dz" + tag] = pltpu.VMEM((rows, LANES), f32)
        shapes["rx" + tag] = pltpu.VMEM((2, 2, rows, LANES), f32)
        shapes["rz" + tag] = pltpu.VMEM((2, 2, p, SUB, LANES), f32)
        shapes["rc" + tag] = pltpu.VMEM((2, 4, SUB, LANES), f32)
        shapes["ssem" + tag] = pltpu.SemaphoreType.DMA((8,))
        shapes["rsem" + tag] = pltpu.SemaphoreType.DMA((2, 8))
    shapes["tmpf"] = pltpu.VMEM((PF, MID.rows, LANES), f32)
    shapes["tmpm"] = pltpu.VMEM((PM, LOW.rows, LANES), f32)
    shapes["ein"] = pltpu.VMEM((PF * PF * PF * 2, LANES), f32)
    shapes["cst"] = pltpu.VMEM((CONSTS.row, LANES), f32)
    shapes["insem"] = pltpu.SemaphoreType.DMA((2,))
    shapes["dsrc"] = pltpu.VMEM((SUB, LANES), f32)
    shapes["dhalo"] = pltpu.VMEM((8, SUB, LANES), f32)
    shapes["dssem"] = pltpu.SemaphoreType.DMA((8,))
    shapes["drsem"] = pltpu.SemaphoreType.DMA((8,))
    shapes["da"] = pltpu.VMEM((n_dev, SUB, LANES), f32)
    shapes["db"] = pltpu.VMEM((n_node * 2 * n_dev, LANES), f32)
    shapes["ga"] = pltpu.VMEM((n_dev, SUB, LANES), f32)
    shapes["gb"] = pltpu.VMEM(((n_node + 1) * low_rows, LANES), f32)
    half = n_node // 2
    for tag in "dg":
        shapes[tag + "a_s"] = pltpu.SemaphoreType.DMA((n_dev,))
        shapes[tag + "a_r"] = pltpu.SemaphoreType.DMA((n_dev,))
        shapes[tag + "b_s"] = pltpu.SemaphoreType.DMA((half,))
        shapes[tag + "b_r"] = pltpu.SemaphoreType.DMA((half,))
        shapes[tag + "c_s"] = pltpu.SemaphoreType.DMA((half,))
        shapes[tag + "c_r"] = pltpu.SemaphoreType.DMA((half,))
    nx, nz = n_dev + 1, 2 * n_node
    for name in ("wx", "wxm", "wy", "wym", "wz", "wzm", "dg", "cx", "cr", "cq"):
        shapes["c_" + name] = pltpu.VMEM((nx, nz, 2 * LANES), f32)
    shapes["c_main"] = pltpu.VMEM((nz, LANES), f32)
    shapes["c_rest"] = pltpu.VMEM((nz, LANES), f32)
    shapes["c_p"] = pltpu.VMEM((nx, nz + 2 * SUB, 2 * LANES), f32)
    return shapes, low_rows


def make_kernel(n_node, n_dev, names, low_rows):
    half = n_node // 2
    nx, nz = n_dev + 1, 2 * n_node

    def kernel(ein_hbm, diff_ref, cst_hbm, out_ref, *scratch):
        s = dict(zip(names, scratch))
        node = lax.axis_index("node")
        dev = lax.axis_index("dev")
        sub = lax.broadcasted_iota(jnp.int32, (SUB, LANES), 0)
        lane = lax.broadcasted_iota(jnp.int32, (SUB, LANES), 1)
        has_lo, has_hi = dev > 0, dev < n_dev - 1

        load_in = pltpu.make_async_copy(ein_hbm, s["ein"], s["insem"].at[0])
        load_cst = pltpu.make_async_copy(cst_hbm, s["cst"], s["insem"].at[1])
        load_cst.start()
        load_in.start()

        def const(name, index=None):
            row, size = CONSTS.at[name]
            if index is None:
                return s["cst"][row : row + size, :]
            return s["cst"][row + SUB * index : row + SUB * index + SUB, :]

        def guarded(dx, fn):
            if dx == 0:
                fn()
            else:
                pl.when(has_lo if dx < 0 else has_hi)(fn)

        def neighbour(dx, dz):
            return (lax.rem(node + dz + n_node, n_node), dev + dx)

        sibling = (node + 1 - 2 * lax.rem(node, 2), dev)

        def same_core(k):
            return lax.rem(node + 2 * k, n_node)

        for tag in "fm":
            for name in ("rx", "rz", "rc"):
                s[name + tag][...] = jnp.zeros_like(s[name + tag])
        s["dhalo"][...] = jnp.zeros_like(s["dhalo"])
        s["dsrc"][...] = jnp.zeros_like(s["dsrc"])
        s["dsrc"][0:2, :] = diff_ref[...]
        s["da"][dev] = s["dsrc"][...]

        barrier = pltpu.get_barrier_semaphore()

        def greet(target):
            pl.semaphore_signal(barrier, inc=1, device_id=target, device_id_type=MESH)

        for dx, dz in DIRS:
            guarded(dx, lambda dx=dx, dz=dz: greet(neighbour(dx, dz)))
        far = lambda k: lax.rem(dev + k, n_dev)

        def greet_far(k, _):
            greet((node, lax.rem(dev + k, n_dev)))
            return 0

        def greet_cores(k, _):
            greet((same_core(k), dev))
            return 0

        lax.fori_loop(1, n_dev, greet_far, 0)
        lax.fori_loop(1, half, greet_cores, 0)
        ends = has_lo.astype(jnp.int32) + has_hi.astype(jnp.int32)
        pl.semaphore_wait(barrier, n_dev - 1 + half - 1 + 2 + 3 * ends)

        def face_copy(tag, par, i):
            level = FINE if tag == "f" else MID
            dx, dz = DIRS[i]
            j = OPP[i]
            a = 0 if dx < 0 else level.points - 1
            zrow = pl.ds(0 if dz < 0 else level.rows - SUB, SUB)
            buf = s["l" + tag]
            if dz == 0:
                src, dst = buf.at[a], s["rx" + tag].at[par, j]
            elif dx == 0:
                src, dst = buf.at[:, zrow], s["rz" + tag].at[par, j - 2]
            else:
                src, dst = buf.at[a, zrow], s["rc" + tag].at[par, j - 4]
            return pltpu.make_async_remote_copy(
                src_ref=src,
                dst_ref=dst,
                send_sem=s["ssem" + tag].at[i],
                recv_sem=s["rsem" + tag].at[par, j],
                device_id=neighbour(dx, dz),
                device_id_type=MESH,
            )

        def halo_copy(i):
            return pltpu.make_async_remote_copy(
                src_ref=s["dsrc"],
                dst_ref=s["dhalo"].at[OPP[i]],
                send_sem=s["dssem"].at[i],
                recv_sem=s["drsem"].at[OPP[i]],
                device_id=neighbour(*DIRS[i]),
                device_id_type=MESH,
            )

        def start_all(make):
            for i in range(8):
                guarded(DIRS[i][0], lambda i=i: make(i).start())

        def wait_all(make):
            for i in range(8):
                guarded(DIRS[i][0], lambda i=i: make(i).wait_send())
            for i in range(8):
                guarded(DIRS[OPP[i]][0], lambda i=i: make(i).wait_recv())

        parity = {"f": 0, "m": 0}

        def exchange(tag, between=None):
            level = FINE if tag == "f" else MID
            par = parity[tag]
            parity[tag] = 1 - par
            make = lambda i: face_copy(tag, par, i)
            start_all(make)
            if between is not None:
                between()
            wait_all(make)
            buf, rx, rz, rc = (s[n + tag] for n in ("l", "rx", "rz", "rc"))
            last, top = level.points - 1, level.rows - SUB
            buf[0] += rx[par, 0]
            buf[last] += rx[par, 1]
            buf[:, 0:SUB] += rz[par, 0]
            buf[:, top : top + SUB] += rz[par, 1]
            buf[0, 0:SUB] += rc[par, 0]
            buf[0, top : top + SUB] += rc[par, 1]
            buf[last, 0:SUB] += rc[par, 2]
            buf[last, top : top + SUB] += rc[par, 3]

        def sum_y(tag, a):
            level = FINE if tag == "f" else MID
            buf, n = s["l" + tag], level.planes
            rows_lo = pl.ds(0, n, stride=SUB)
            rows_hi = pl.ds(level.points - 1, n, stride=SUB)
            lo, hi = buf[a, rows_lo, :], buf[a, rows_hi, :]
            at = lax.broadcasted_iota(jnp.int32, (n, LANES), 1)
            buf[a, rows_lo, :] = lo + jnp.where(at > 0, pltpu.roll(hi, 1, 1), 0.0)
            buf[a, rows_hi, :] = hi + jnp.where(
                at < LANES - 1, pltpu.roll(lo, LANES - 1, 1), 0.0
            )

        def gather_a(tag, k):
            buf = s[tag + "a"]
            return pltpu.make_async_remote_copy(
                src_ref=buf.at[dev],
                dst_ref=buf.at[dev],
                send_sem=s[tag + "a_s"].at[k],
                recv_sem=s[tag + "a_r"].at[k],
                device_id=(node, far(k)),
                device_id_type=MESH,
            )

        block = {"d": 2 * n_dev, "g": low_rows}
        base = {"d": 0, "g": low_rows}

        def slot(tag, index):
            size = block[tag]
            return s[tag + "b"].at[pl.ds(pl.multiple_of(base[tag] + index * size, size), size)]

        def gather_b(tag, k):
            return pltpu.make_async_remote_copy(
                src_ref=slot(tag, node),
                dst_ref=slot(tag, node),
                send_sem=s[tag + "b_s"].at[k],
                recv_sem=s[tag + "b_r"].at[k],
                device_id=(same_core(k), dev),
                device_id_type=MESH,
            )

        def gather_c(tag, k):
            index = lax.rem(node - 2 * k + n_node, n_node)
            return pltpu.make_async_remote_copy(
                src_ref=slot(tag, index),
                dst_ref=slot(tag, index),
                send_sem=s[tag + "c_s"].at[k],
                recv_sem=s[tag + "c_r"].at[k],
                device_id=sibling,
                device_id_type=MESH,
            )

        def loop(lower, upper, fn):
            def step(k, _):
                fn(k)
                return 0

            lax.fori_loop(lower, upper, step, 0)

        def start_a(tag):
            loop(1, n_dev, lambda k: gather_a(tag, k).start())

        def wait_a(tag):
            loop(1, n_dev, lambda k: gather_a(tag, k).wait())

        def start_b(tag):
            loop(1, half, lambda k: gather_b(tag, k).start())
            gather_c(tag, 0).start()

        def forward_b(tag):
            def one(k):
                gather_b(tag, k).wait_recv()
                gather_c(tag, k).start()

            loop(1, half, one)

        def wait_b(tag):
            loop(1, half, lambda k: gather_b(tag, k).wait_send())
            loop(0, half, lambda k: gather_c(tag, k).wait())

        def apply(tag, src):
            level = FINE if tag == "f" else MID
            n, p = level.planes, level.points
            src, dst = s[src + tag], s["l" + tag]

            def plane(z):
                rows = pl.ds(pl.multiple_of(z * SUB, SUB), SUB)
                v = src[:, rows, :]
                acc = const("ky" + tag, 0) * v
                for shift in range(1, SUB):
                    if p == PF or shift < p or shift > SUB - p:
                        acc = acc + const("ky" + tag, shift) * pltpu.roll(v, shift, 1)
                along_x = mix_even_odd(level.khat, [v[a] for a in range(p)])
                weight = s["dz" + tag][rows, :]
                mass = jnp.where(z == p - 1, 2.0 * SHIFT_MASS, SHIFT_MASS)
                for a in range(p):
                    dst[a, rows, :] = weight * (acc[a] + along_x[a]) + mass * v[a]

            loop(0, n, plane)

            def line(a):
                v = src[a]
                parts = [v[SUB * i : SUB * i + SUB] for i in range(n)]
                low = mix_even_odd(level.khat, parts[:p])
                high = mix_even_odd(level.khat, parts[p - 1 :])
                first = s["dz" + tag][0:SUB, :]
                second = s["dz" + tag][level.rows - SUB : level.rows, :]
                out = [first * t for t in low[: p - 1]]
                out.append(first * low[p - 1] + second * high[0])
                out += [second * t for t in high[1:]]
                for i in range(n):
                    dst[a, SUB * i : SUB * i + SUB, :] += out[i]

            loop(0, p, line)

        def first_step(tag, from_zero, scale=False):
            level = FINE if tag == "f" else MID
            c = float(1.0 / level.theta)

            def one(a):
                sum_y(tag, a)
                if from_zero:
                    res = s["l" + tag][a]
                    s["rhs" + tag][a] = res
                else:
                    res = s["rhs" + tag][a] - s["l" + tag][a]
                s["r" + tag][a] = res
                upd = c * s["inv" + tag][a] * res
                s["d" + tag][a] = upd
                s["x" + tag][a] = upd if from_zero else s["x" + tag][a] + upd

            loop(0, level.points, one)

        def next_step(tag, c1, c2, last):
            level = FINE if tag == "f" else MID

            def one(a):
                sum_y(tag, a)
                res = s["r" + tag][a] - s["l" + tag][a]
                upd = c1 * s["d" + tag][a] + c2 * s["inv" + tag][a] * res
                if not last:
                    s["r" + tag][a] = res
                    s["d" + tag][a] = upd
                s["x" + tag][a] += upd

            loop(0, level.points, one)

        def smooth(tag, count, from_zero, between=None):
            exchange(tag, None if between is None else between[0])
            first_step(tag, from_zero)
            coefs = (FINE if tag == "f" else MID).steps(count)
            for index, (c1, c2) in enumerate(coefs):
                apply(tag, "d")
                exchange(tag, None if between is None else between[index + 1])
                next_step(tag, c1, c2, index == count - 2)

        def diagonals():
            ones = [has_lo.astype(jnp.float32), 1.0, has_hi.astype(jnp.float32)]
            halo, own = s["dhalo"], s["dsrc"]

            def patch(dx):
                at = lambda dz: halo.at[DIRS.index((dx, dz))]
                mid = own if dx == 0 else at(0)
                return [at(-1)[1:2, :], mid[0:1, :], mid[1:2, :], at(1)[0:1, :]]

            p_lo, p_own, p_hi = patch(-1), patch(0), patch(1)
            xs = [
                [u + v for u, v in zip(p_lo, p_own)],
                p_own,
                [u + v for u, v in zip(p_own, p_hi)],
            ]
            copies = [1.0 + ones[0], 1.0, 1.0 + ones[2]]
            for xc in range(3):
                q = xs[xc]
                kinds = [q[0] + q[1], q[1], q[1] + q[2], q[2], q[2] + q[3]]
                kinds = [jnp.broadcast_to(k, (SUB, LANES)) for k in kinds]
                lows = [k + jnp.where(lane > 0, pltpu.roll(k, 1, 1), 0.0) for k in kinds]
                highs = [
                    k + jnp.where(lane < LANES - 1, pltpu.roll(k, LANES - 1, 1), 0.0)
                    for k in kinds
                ]
                for tag, level in (("f", FINE), ("m", MID)):
                    p = level.points
                    full = [
                        jnp.where(sub == 0, lo, jnp.where(sub == p - 1, hi, k))
                        for lo, hi, k in zip(lows, highs, kinds)
                    ]
                    for z in range(level.planes):
                        kind = {0: 0, p - 1: 2, 2 * p - 2: 4}.get(z, 1 if z < p else 3)
                        s["cls" + tag][xc, SUB * z : SUB * z + SUB, :] = full[kind]
                        if xc == 1 and kind in (1, 2, 3):
                            s["dz" + tag][SUB * z : SUB * z + SUB, :] = kinds[kind]
                    if xc == 1:
                        s["dz" + tag][0:SUB, :] = kinds[1]
                        s["dz" + tag][level.rows - SUB : level.rows, :] = kinds[3]
            for tag, level in (("f", FINE), ("m", MID)):
                p = level.points
                for a in range(p):
                    xc = 0 if a == 0 else 2 if a == p - 1 else 1
                    diag = (float(level.kdiag[a]) + const("kzb" + tag)) * s["cls" + tag][xc]
                    diag = diag + copies[xc] * const("cnt" + tag)
                    s["inv" + tag][a] = 1.0 / diag

        def restrict_fine():
            def line(a):
                res = s["locf"][a] - s["lf"][a]
                parts = [res[SUB * i : SUB * i + SUB] for i in range(FINE.planes)]
                for i, t in enumerate(mix(R73Z.T, parts)):
                    s["tmpf"][a, SUB * i : SUB * i + SUB, :] = t

            loop(0, PF, line)

            def plane(z):
                rows = pl.ds(pl.multiple_of(z * SUB, SUB), SUB)
                v = s["tmpf"][:, rows, :]
                t = jnp.stack(mix(R73, [v[a] for a in range(PF)]))
                acc = const("r73", 0) * t
                for shift in range(1, SUB):
                    acc = acc + const("r73", shift) * pltpu.roll(t, shift, 1)
                s["locm"][:, rows, :] = acc
                s["lm"][:, rows, :] = acc

            loop(0, MID.planes, plane)

        def prolong_fine():
            def plane(z):
                rows = pl.ds(pl.multiple_of(z * SUB, SUB), SUB)
                v = s["xm"][:, rows, :]
                acc = const("j73", 0) * v
                for shift in range(1, SUB):
                    acc = acc + const("j73", shift) * pltpu.roll(v, shift, 1)
                for a, t in enumerate(mix(J73, [acc[i] for i in range(PM)])):
                    s["tmpf"][a, rows, :] = t

            loop(0, MID.planes, plane)

            def line(a):
                v = s["tmpf"][a]
                parts = [v[SUB * i : SUB * i + SUB] for i in range(MID.planes)]
                for i, t in enumerate(mix(J73Z, parts)):
                    s["xf"][a, SUB * i : SUB * i + SUB, :] += t

            loop(0, PF, line)

        def restrict_mid():
            for a in range(PM):
                res = s["locm"][a] - s["lm"][a]
                parts = [res[SUB * i : SUB * i + SUB] for i in range(MID.planes)]
                for i, t in enumerate(mix(R31Z.T, parts)):
                    s["tmpm"][a, SUB * i : SUB * i + SUB, :] = t
            spare = jnp.zeros((SUB, LANES), jnp.float32)
            for z in range(3):
                v = s["tmpm"][:, SUB * z : SUB * z + SUB, :]
                for a, t in enumerate(mix(R31, [v[i] for i in range(PM)])):
                    acc = const("r31", 0) * t
                    for shift in (1, 5, 6, 7):
                        acc = acc + const("r31", shift) * pltpu.roll(t, shift, 0)
                    up = pltpu.roll(pltpu.roll(acc, 1, 1), SUB - 1, 0)
                    node_row = acc + jnp.where(lane > 0, up, 0.0)
                    s["ga"][dev, 3 * a + z : 3 * a + z + 1, :] = node_row[0:1, :]
                    spare = spare + jnp.where(lane == z * nx + dev + a, up[0:1, 0:1], 0.0)
            s["ga"][dev, 6:7, :] = spare[0:1, :]
            s["ga"][dev, 7:8, :] = jnp.zeros((1, LANES), jnp.float32)

        def sum_x_low():
            flat = s["ga"]
            g = jnp.zeros((low_rows, LANES), jnp.float32)
            pad = lambda rows, before: jnp.pad(
                rows, ((before, low_rows - before - rows.shape[0]), (0, 0))
            )
            mine = s["gb"].at[
                pl.ds(pl.multiple_of(low_rows + node * low_rows, low_rows), low_rows)
            ]
            mine[...] = g
            for z in range(3):
                mine[z * nx : z * nx + n_dev, :] = flat[:, z, :]
                mine[z * nx + 1 : z * nx + nx, :] += flat[:, 3 + z, :]
            mine[3 * nx : 3 * nx + 1, :] = jnp.sum(flat[:, 6, :], axis=0, keepdims=True)

        def wide(rows):
            return jnp.concatenate([rows, jnp.zeros_like(rows)], axis=1)

        def low_weights():
            up_y = lambda v: pltpu.roll(v, 1, 1)
            up_z = lambda v: pltpu.roll(v, 1, 0)
            elem = lambda x: s["db"][pl.ds(x, nz, stride=n_dev), :]
            zero = jnp.zeros((nz, 2 * LANES), jnp.float32)
            lanes = lax.broadcasted_iota(jnp.int32, (nz, 2 * LANES), 1)
            inside = (lanes <= LANES).astype(jnp.float32)
            y_copies = (
                inside + ((lanes > 0) & (lanes < LANES)).astype(jnp.float32)
            )
            for x in range(nx):
                lo = wide(elem(x - 1)) if x > 0 else zero
                hi = wide(elem(x)) if x < n_dev else zero
                both = lo + hi
                wy = 0.5 * (both + up_z(both))
                wz = 0.5 * (both + up_y(both))
                s["c_wy"][x] = wy
                s["c_wym"][x] = up_y(wy)
                s["c_wz"][x] = wz
                s["c_wzm"][x] = up_z(wz)
                hz = hi + up_z(hi)
                wx = 0.5 * (hz + up_y(hz))
                s["c_wx"][x] = wx
                wxm = s["c_wx"][x - 1] if x > 0 else zero
                x_copies = 1.0 if x in (0, n_dev) else 2.0
                s["c_dg"][x] = (
                    wx + wxm + wy + s["c_wym"][x] + wz + s["c_wzm"][x]
                    + 2.0 * SHIFT_MASS * x_copies * y_copies
                )

        def low_rhs():
            buf = s["gb"]
            buf[0:low_rows, :] = buf[n_node * low_rows : (n_node + 1) * low_rows, :]
            own = lambda row: buf[pl.ds(low_rows + row, n_node, stride=low_rows), :]
            before = lambda row: buf[pl.ds(row, n_node, stride=low_rows), :]
            at = lax.broadcasted_iota(jnp.int32, (n_node, LANES), 1)
            spare, spare_before = own(3 * nx), before(3 * nx)

            def pick(rows, lane_index):
                moved = rows if lane_index == 0 else pltpu.roll(rows, LANES - lane_index, 1)
                return jnp.where(at == 0, moved, 0.0)

            even, odd = pl.ds(0, n_node, stride=2), pl.ds(1, n_node, stride=2)
            left, right = pl.ds(0, LANES), pl.ds(LANES, LANES)
            res, main, rest = s["c_cr"], s["c_main"], s["c_rest"]
            for x in range(nx):
                main[even, :] = own(x) + before(2 * nx + x)
                main[odd, :] = own(nx + x)
                rest[even, :] = pick(spare, x) + pick(spare_before, 2 * nx + x)
                rest[odd, :] = pick(spare, nx + x)
                res[x, :, left] = main[...]
                res[x, :, right] = rest[...]

        def fold(v):
            parts = [v[i : i + SUB] for i in range(0, v.shape[0], SUB)]
            while len(parts) > 1:
                parts = [u + w for u, w in zip(parts[::2], parts[1::2])] + (
                    [parts[-1]] if len(parts) % 2 else []
                )
            return parts[0][:, :LANES] + parts[0][:, LANES:]

        def total(v):
            return jnp.sum(v, axis=(0, 1), keepdims=True)

        def set_direction(x, value):
            p = s["c_p"]
            p[x, SUB : SUB + nz, :] = value
            p[x, 0:SUB, :] = value[nz - SUB : nz]
            p[x, SUB + nz : 2 * SUB + nz, :] = value[0:SUB]

        def coarse_solve():
            p, q, res, sol = s["c_p"], s["c_cq"], s["c_cr"], s["c_cx"]
            wide_lanes = 2 * LANES
            here = pl.ds(SUB, nz)
            norm = jnp.zeros((SUB, LANES), jnp.float32)
            for x in range(nx):
                v = res[x]
                set_direction(x, v)
                sol[x] = jnp.zeros_like(v)
                norm = norm + fold(v * v)

            def iteration(_, now):
                dot = jnp.zeros((SUB, LANES), jnp.float32)
                for x in range(nx):
                    v = p[x, here, :]
                    out = s["c_dg"][x] * v
                    if x > 0:
                        out = out - s["c_wx"][x - 1] * p[x - 1, here, :]
                    if x < nx - 1:
                        out = out - s["c_wx"][x] * p[x + 1, here, :]
                    out = out - s["c_wy"][x] * pltpu.roll(v, wide_lanes - 1, 1)
                    out = out - s["c_wym"][x] * pltpu.roll(v, 1, 1)
                    out = out - s["c_wz"][x] * p[x, SUB + 1 : SUB + 1 + nz, :]
                    out = out - s["c_wzm"][x] * p[x, SUB - 1 : SUB - 1 + nz, :]
                    q[x] = out
                    dot = dot + fold(v * out)
                alpha = now / total(dot)
                norm = jnp.zeros((SUB, LANES), jnp.float32)
                for x in range(nx):
                    sol[x] += alpha * p[x, here, :]
                    v = res[x] - alpha * q[x]
                    res[x] = v
                    norm = norm + fold(v * v)
                new = total(norm)
                beta = new / now
                for x in range(nx):
                    set_direction(x, res[x] + beta * p[x, here, :])
                return new

            lax.fori_loop(0, COARSE_ITERS, iteration, total(norm))

        def prolong_mid():
            spread = {}
            for a in range(2):
                for z in range(3):
                    index = lax.rem(2 * node + z, nz)
                    row = s["c_cx"][dev + a, pl.ds(index, 1), :]
                    row = jnp.broadcast_to(row, (SUB, 2 * LANES))
                    low = row[:, :LANES]
                    high = pltpu.roll(row, 2 * LANES - 1, 1)[:, :LANES]
                    spread[a, z] = const("j31", 0) * low + const("j31", 1) * high
            for a in range(PM):
                parts = [
                    mix(J31[a : a + 1], [spread[0, z], spread[1, z]])[0] for z in range(3)
                ]
                for i, t in enumerate(mix(J31Z, parts)):
                    s["xm"][a, SUB * i : SUB * i + SUB, :] += t

        start_all(halo_copy)
        start_a("d")
        load_cst.wait()
        load_in.wait()

        def load_line(a):
            planes = []
            for e in range(2):
                for c in range(PF):
                    start = a * (PF * PF * 2) + 2 * c + e
                    planes.append(s["ein"][pl.ds(start, SUB, stride=2 * PF), :])
            merged = planes[: PF - 1] + [planes[PF - 1] + planes[PF]] + planes[PF + 1 :]
            wz = np.concatenate([FINE.w, FINE.w[1:]])
            for z, v in enumerate(merged):
                t = const("iwb") * v * float(1.0 / wz[z])
                s["locf"][a, SUB * z : SUB * z + SUB, :] = t

        loop(0, PF, load_line)
        for a in range(PF):
            t = s["locf"][a] * float(1.0 / FINE.w[a])
            s["locf"][a] = t
            s["lf"][a] = t

        def setup():
            wait_all(halo_copy)
            diagonals()

        def diff_stage_b():
            wait_a("d")
            mine = slot("d", node)
            for e in range(2):
                mine[e * n_dev : (e + 1) * n_dev, :] = s["da"][:, e, :]
            start_b("d")

        smooth("f", SMOOTH_FINE, True, [setup, diff_stage_b, lambda: forward_b("d")])
        apply("f", "x")
        restrict_fine()

        def weights():
            wait_b("d")
            low_weights()

        smooth("m", SMOOTH_MID, True, [weights, None, None])
        apply("m", "x")
        restrict_mid()
        start_a("g")
        wait_a("g")
        sum_x_low()
        start_b("g")
        forward_b("g")
        wait_b("g")
        low_rhs()
        coarse_solve()
        prolong_mid()
        apply("m", "x")
        smooth("m", SMOOTH_MID, False)
        prolong_fine()
        apply("f", "x")
        smooth("f", SMOOTH_FINE, False)

        def store_line(a):
            for e in range(2):
                for c in range(PF):
                    z = e * (PF - 1) + c
                    start = a * (PF * PF * 2) + 2 * c + e
                    out_ref[pl.ds(start, SUB, stride=2 * PF), :] = s["xf"][
                        a, SUB * z : SUB * z + SUB, :
                    ]

        loop(0, PF, store_line)

    return kernel


def solution(mesh):
    n_node, n_dev = mesh.shape["node"], mesh.shape["dev"]
    shapes, low_rows = scratch_shapes(n_node, n_dev)
    kernel = make_kernel(n_node, n_dev, list(shapes), low_rows)
    rows = PF * PF * PF * 2

    def local(element_load, diffusivity):
        out = pl.pallas_call(
            kernel,
            out_shape=jax.ShapeDtypeStruct((rows, LANES), jnp.float32),
            in_specs=[
                pl.BlockSpec(memory_space=pl.ANY),
                pl.BlockSpec(memory_space=pltpu.VMEM),
                pl.BlockSpec(memory_space=pl.ANY),
            ],
            out_specs=pl.BlockSpec(memory_space=pltpu.VMEM),
            scratch_shapes=list(shapes.values()),
            compiler_params=pltpu.CompilerParams(
                collective_id=0, has_side_effects=True, vmem_limit_bytes=48 * 1024 * 1024
            ),
        )(
            element_load.reshape(rows, LANES),
            diffusivity.reshape(2, LANES),
            jnp.asarray(CONSTS.array()),
        )
        return out.reshape(element_load.shape)

    return jax.shard_map(
        local,
        mesh=mesh,
        in_specs=(P(None, None, None, "dev", "node", None), P("dev", "node", None)),
        out_specs=P(None, None, None, "dev", "node", None),
        check_vma=False,
    )
```

```python
import jax
import jax.numpy as jnp
import numpy as np
from jax import lax
from jax.experimental import pallas as pl
from jax.experimental.pallas import tpu as pltpu
from jax.sharding import PartitionSpec as P

PF = 8
PM = 4
PC = 2
SMOOTH_FINE = 3
SMOOTH_MID = 3
COARSE_ITERS = 5
SHIFT_MASS = 0.05
LANES = 128
SUB = 8
MESH = pl.DeviceIdType.MESH

def legendre_values(points, poly_order):
    columns = [points * 0.0 + 1.0, points]
    for degree in range(2, poly_order + 1):
        columns.append(
            ((2 * degree - 1) * points * columns[degree - 1] - (degree - 1) * columns[degree - 2])
            / degree
        )
    return np.stack(columns[: poly_order + 1], axis=1)


def largest_eigen(matrix):
    size_n = matrix.shape[0]
    vector = np.cos(2.7 * np.arange(size_n) + 0.3)
    for power_step in range(4000):
        vector = matrix @ vector
        vector = vector / np.sqrt(np.sum(vector * vector))
    return float(vector @ (matrix @ vector))


def gll_level(poly_order):
    point_count = poly_order + 1
    gll_nodes = np.cos(np.pi * np.arange(point_count) / poly_order)
    for newton_step in range(60):
        values = legendre_values(gll_nodes, poly_order)
        gll_nodes = gll_nodes - (gll_nodes * values[:, poly_order] - values[:, poly_order - 1]) / (
            point_count * values[:, poly_order]
        )
    gll_nodes = np.sort(gll_nodes)
    values = legendre_values(gll_nodes, poly_order)
    top_value = values[:, poly_order]
    weights = 2.0 / (poly_order * point_count * top_value**2)
    deriv_matrix = np.zeros((point_count, point_count))
    for row_index in range(point_count):
        for col_index in range(point_count):
            if row_index != col_index:
                deriv_matrix[row_index, col_index] = top_value[row_index] / (
                    top_value[col_index] * (gll_nodes[row_index] - gll_nodes[col_index])
                )
    deriv_matrix[0, 0] = -poly_order * point_count / 4.0
    deriv_matrix[poly_order, poly_order] = poly_order * point_count / 4.0
    stiffness = deriv_matrix.T @ (weights[:, None] * deriv_matrix)
    diag_ids = np.arange(point_count)
    stiff_diag = stiffness[diag_ids, diag_ids]
    diag_scale = 1.0 / np.sqrt(stiff_diag)
    eig_bound = largest_eigen(diag_scale[:, None] * stiffness * diag_scale[None, :])
    return (gll_nodes, weights, deriv_matrix, stiff_diag, eig_bound)


def interp_table(fine_nodes, coarse_nodes):
    interp_mat = np.ones((fine_nodes.shape[0], coarse_nodes.shape[0]))
    for col_index in range(coarse_nodes.shape[0]):
        for other_index in range(coarse_nodes.shape[0]):
            if other_index != col_index:
                interp_mat[:, col_index] *= (fine_nodes - coarse_nodes[other_index]) / (
                    coarse_nodes[col_index] - coarse_nodes[other_index]
                )
    return interp_mat


class Level:
    def __init__(self, points):
        nodes, w, deriv, stiff_diag, bound = gll_level(points - 1)
        self.points = points
        self.planes = 2 * points - 1
        self.rows = SUB * self.planes
        self.x_rows = SUB * (self.planes if points == SUB else -(-self.planes // 2))
        self.z_rows = SUB * (points if points == SUB else -(-points // 2))
        self.nodes = nodes
        self.w = w
        self.khat = (deriv.T @ (w[:, None] * deriv)) / w[:, None]
        self.kdiag = stiff_diag / w
        self.theta = 0.6 * bound
        self.delta = 0.5 * bound

    def steps(self, count):
        sig = self.theta / self.delta
        rho = 1.0 / sig
        out = []
        for _ in range(count - 1):
            rho_next = 1.0 / (2.0 * sig - rho)
            out.append((float(rho_next * rho), float(2.0 * rho_next / self.delta)))
            rho = rho_next
        return out


def roll_coefs(matrix):
    full = np.zeros((SUB, SUB))
    full[: matrix.shape[0], : matrix.shape[1]] = matrix
    i = np.arange(SUB)
    return [full[i, (i - s) % SUB] for s in range(SUB)]


def two_elements(matrix):
    n, m = matrix.shape
    out = np.zeros((2 * n - 1, 2 * m - 1))
    out[:n, :m] = matrix
    out[n - 1 :, m - 1 :] = matrix
    return out


def plane_sum(points):
    values = np.zeros((2 * points - 1,))
    values[:points] += 1
    values[points - 1 :] += 1
    return values


class Consts:
    def __init__(self):
        self.blocks = []
        self.at = {}
        self.row = 0

    def add(self, name, block):
        block = np.asarray(block, np.float64)
        if block.ndim == 1:
            block = np.broadcast_to(block[:, None], (block.shape[0], LANES))
        assert block.shape[0] % SUB == 0
        self.at[name] = (self.row, block.shape[0])
        self.blocks.append(block)
        self.row += block.shape[0]

    def array(self):
        return np.concatenate(self.blocks, 0).astype(np.float32)


FINE, MID, LOW = Level(PF), Level(PM), Level(PC)
J73 = interp_table(FINE.nodes, MID.nodes)
J31 = interp_table(MID.nodes, LOW.nodes)
R73 = (FINE.w[:, None] * J73 / MID.w[None, :]).T
R31 = (MID.w[:, None] * J31).T
R73Z = two_elements(FINE.w[:, None] * J73 / MID.w[None, :])
R73Z[PF - 1] = 0.0
R73Z[PF - 1, PM - 1] = FINE.w[0] / MID.w[0]
R31Z = two_elements(MID.w[:, None] * J31)
R31Z[PM - 1] = 0.0
R31Z[PM - 1, PC - 1] = MID.w[0]
J73Z = two_elements(J73)
J31Z = two_elements(J31)

CONSTS = Consts()
for tag, level in (("f", FINE), ("m", MID)):
    CONSTS.add("ky" + tag, np.concatenate(roll_coefs(level.khat)))
    kb = np.zeros(SUB)
    kb[: level.points] = level.kdiag
    kz = np.concatenate([level.kdiag, level.kdiag[1:]])
    CONSTS.add("kzb" + tag, (kz[:, None] + kb[None, :]).reshape(-1))
    ey = np.arange(LANES)
    my = np.ones((SUB, LANES))
    my[0] += ey > 0
    my[level.points - 1] += ey < LANES - 1
    mz = np.ones(level.planes)
    mz[[0, level.points - 1, -1]] = 2
    CONSTS.add("cnt" + tag, (SHIFT_MASS * mz[:, None, None] * my[None]).reshape(-1, LANES))
    CONSTS.add("mz" + tag, np.repeat(SHIFT_MASS * plane_sum(level.points), SUB))
CONSTS.add("r73", np.concatenate(roll_coefs(R73)))
CONSTS.add("j73", np.concatenate(roll_coefs(J73)))
CONSTS.add("r31", np.concatenate(roll_coefs(R31)))
CONSTS.add("j31", np.concatenate([np.pad(J31[:, p], (0, SUB - PM)) for p in range(PC)]))
CONSTS.add("iwb", 1.0 / FINE.w)

DIRS = ((-1, 0), (1, 0), (0, -1), (0, 1), (-1, -1), (-1, 1), (1, -1), (1, 1))
OPP = tuple(DIRS.index((-dx, -dz)) for dx, dz in DIRS)
COEF = 1e-13


def mix(matrix, parts):
    out = []
    for row in np.asarray(matrix):
        acc = None
        for c, v in zip(row, parts):
            if abs(c) > COEF:
                term = v if abs(c - 1.0) < COEF else float(c) * v
                acc = term if acc is None else acc + term
        out.append(acc)
    return out


def mix_even_odd(matrix, parts):
    n = len(parts)
    h = n // 2
    flipped = matrix[:h, ::-1][:, :h]
    even = mix(0.5 * (matrix[:h, :h] + flipped), [parts[i] + parts[n - 1 - i] for i in range(h)])
    odd = mix(0.5 * (matrix[:h, :h] - flipped), [parts[i] - parts[n - 1 - i] for i in range(h)])
    low = [e + o for e, o in zip(even, odd)]
    high = [e - o for e, o in zip(even, odd)]
    return low + high[::-1]


def scratch_shapes(n_node, n_dev):
    f32 = jnp.float32
    low_rows = -(-(3 * (n_dev + 1) + 1) // SUB) * SUB
    shapes = {}
    for tag, level in (("f", FINE), ("m", MID)):
        p, rows = level.points, level.rows
        for name in ("loc", "rhs", "inv", "x", "r", "d", "l"):
            shapes[name + tag] = pltpu.VMEM((p, rows, LANES), f32)
        shapes["cls" + tag] = pltpu.VMEM((3, rows, LANES), f32)
        shapes["dz" + tag] = pltpu.VMEM((rows, LANES), f32)
        shapes["rx" + tag] = pltpu.VMEM((2, 2, level.x_rows, LANES), f32)
        shapes["rz" + tag] = pltpu.VMEM((2, 2, level.z_rows, LANES), f32)
        shapes["sx" + tag] = pltpu.VMEM((2, level.x_rows, LANES), f32)
        shapes["sz" + tag] = pltpu.VMEM((2, level.z_rows, LANES), f32)
        shapes["rc" + tag] = pltpu.VMEM((2, 4, SUB, LANES), f32)
        shapes["ssem" + tag] = pltpu.SemaphoreType.DMA((8,))
        shapes["rsem" + tag] = pltpu.SemaphoreType.DMA((2, 8))
    shapes["tmpf"] = pltpu.VMEM((PF, MID.rows, LANES), f32)
    shapes["tmpm"] = pltpu.VMEM((PM, LOW.rows, LANES), f32)
    shapes["ein"] = pltpu.VMEM((PF * PF * PF * 2, LANES), f32)
    shapes["cst"] = pltpu.VMEM((CONSTS.row, LANES), f32)
    shapes["insem"] = pltpu.SemaphoreType.DMA((3,))
    shapes["eout"] = pltpu.VMEM((PF * PF * PF * 2, LANES), f32)
    shapes["outsem"] = pltpu.SemaphoreType.DMA((PF,))
    shapes["side"] = pltpu.VMEM((6, SUB, LANES), f32)
    shapes["dsrc"] = pltpu.VMEM((SUB, LANES), f32)
    shapes["dhalo"] = pltpu.VMEM((8, SUB, LANES), f32)
    shapes["dssem"] = pltpu.SemaphoreType.DMA((8,))
    shapes["drsem"] = pltpu.SemaphoreType.DMA((8,))
    shapes["da"] = pltpu.VMEM((n_dev, SUB, LANES), f32)
    shapes["db"] = pltpu.VMEM((n_node * 2 * n_dev, LANES), f32)
    shapes["ga"] = pltpu.VMEM((n_dev, SUB, LANES), f32)
    shapes["gb"] = pltpu.VMEM(((n_node + 1) * low_rows, LANES), f32)
    half = n_node // 2
    for tag in "dg":
        shapes[tag + "a_s"] = pltpu.SemaphoreType.DMA((n_dev,))
        shapes[tag + "a_r"] = pltpu.SemaphoreType.DMA((n_dev,))
        shapes[tag + "b_s"] = pltpu.SemaphoreType.DMA((half,))
        shapes[tag + "b_r"] = pltpu.SemaphoreType.DMA((half,))
        shapes[tag + "c_s"] = pltpu.SemaphoreType.DMA((half,))
        shapes[tag + "c_r"] = pltpu.SemaphoreType.DMA((half,))
    nx, nz = n_dev + 1, 2 * n_node
    for name in ("wx", "wxm", "wy", "wym", "wz", "wzm", "dg", "cx", "cr", "cq"):
        shapes["c_" + name] = pltpu.VMEM((nx, nz, 2 * LANES), f32)
    shapes["c_main"] = pltpu.VMEM((nz, LANES), f32)
    shapes["c_rest"] = pltpu.VMEM((nz, LANES), f32)
    shapes["c_p"] = pltpu.VMEM((nx, nz + 2 * SUB, 2 * LANES), f32)
    return shapes, low_rows


def make_kernel(n_node, n_dev, names, low_rows):
    half = n_node // 2
    nx, nz = n_dev + 1, 2 * n_node

    def kernel(ein_hbm, diff_hbm, cst_hbm, out_hbm, *scratch):
        s = dict(zip(names, scratch))
        node = lax.axis_index("node")
        dev = lax.axis_index("dev")
        sub = lax.broadcasted_iota(jnp.int32, (SUB, LANES), 0)
        lane = lax.broadcasted_iota(jnp.int32, (SUB, LANES), 1)
        has_lo, has_hi = dev > 0, dev < n_dev - 1

        s["dsrc"][...] = jnp.zeros_like(s["dsrc"])
        load_diff = pltpu.make_async_copy(
            diff_hbm, s["dsrc"].at[pl.ds(0, 2)], s["insem"].at[2]
        )
        load_in = pltpu.make_async_copy(ein_hbm, s["ein"], s["insem"].at[0])
        load_cst = pltpu.make_async_copy(cst_hbm, s["cst"], s["insem"].at[1])
        load_diff.start()
        load_in.start()
        load_cst.start()

        def const(name, index=None):
            row, size = CONSTS.at[name]
            if index is None:
                return s["cst"][row : row + size, :]
            return s["cst"][row + SUB * index : row + SUB * index + SUB, :]

        def guarded(dx, fn):
            if dx == 0:
                fn()
            else:
                pl.when(has_lo if dx < 0 else has_hi)(fn)

        def neighbour(dx, dz):
            return (lax.rem(node + dz + n_node, n_node), dev + dx)

        sibling = (node + 1 - 2 * lax.rem(node, 2), dev)

        def same_core(k):
            return lax.rem(node + 2 * k, n_node)

        for tag in "fm":
            for name in ("rx", "rz", "rc"):
                s[name + tag][...] = jnp.zeros_like(s[name + tag])
        s["dhalo"][...] = jnp.zeros_like(s["dhalo"])

        barrier = pltpu.get_barrier_semaphore()

        def greet(target):
            pl.semaphore_signal(barrier, inc=1, device_id=target, device_id_type=MESH)

        for dx, dz in DIRS:
            guarded(dx, lambda dx=dx, dz=dz: greet(neighbour(dx, dz)))
        far = lambda k: lax.rem(dev + k, n_dev)

        def greet_far(k, _):
            greet((node, lax.rem(dev + k, n_dev)))
            return 0

        def greet_cores(k, _):
            greet((same_core(k), dev))
            return 0

        lax.fori_loop(1, n_dev, greet_far, 0)
        lax.fori_loop(1, half, greet_cores, 0)
        ends = has_lo.astype(jnp.int32) + has_hi.astype(jnp.int32)

        def wait_barrier():
            pl.semaphore_wait(barrier, n_dev - 1 + half - 1 + 2 + 3 * ends)

        def face_copy(tag, par, i):
            level = FINE if tag == "f" else MID
            dx, dz = DIRS[i]
            j = OPP[i]
            if dz == 0:
                src, dst = s["sx" + tag].at[i], s["rx" + tag].at[par, j]
            elif dx == 0:
                src, dst = s["sz" + tag].at[i - 2], s["rz" + tag].at[par, j - 2]
            else:
                a = 0 if dx < 0 else level.points - 1
                zrow = pl.ds(0 if dz < 0 else level.rows - SUB, SUB)
                src, dst = s["loc" + tag].at[a, zrow], s["rc" + tag].at[par, j - 4]
            return pltpu.make_async_remote_copy(
                src_ref=src,
                dst_ref=dst,
                send_sem=s["ssem" + tag].at[i],
                recv_sem=s["rsem" + tag].at[par, j],
                device_id=neighbour(dx, dz),
                device_id_type=MESH,
            )

        def halo_copy(i):
            return pltpu.make_async_remote_copy(
                src_ref=s["dsrc"],
                dst_ref=s["dhalo"].at[OPP[i]],
                send_sem=s["dssem"].at[i],
                recv_sem=s["drsem"].at[OPP[i]],
                device_id=neighbour(*DIRS[i]),
                device_id_type=MESH,
            )

        def start_some(make, which):
            for i in which:
                guarded(DIRS[i][0], lambda i=i: make(i).start())

        def wait_some(make, which):
            for i in which:
                guarded(DIRS[i][0], lambda i=i: make(i).wait_send())
            for i in which:
                guarded(DIRS[OPP[i]][0], lambda i=i: make(i).wait_recv())

        X_DIRS, Z_DIRS, EDGE_DIRS = (0, 1), (2, 3), (4, 5, 6, 7)
        parity = {"f": 0, "m": 0}

        def start_faces(tag, which):
            start_some(lambda i: face_copy(tag, parity[tag], i), which)

        def pack(tag, parts):
            if tag == "f":
                return parts
            h = -(-len(parts) // 2)
            return [
                parts[i] + pltpu.roll(parts[i + h], PM, 0) if i + h < len(parts) else parts[i]
                for i in range(h)
            ]

        def unpack(tag, v, count):
            parts = [v[SUB * i : SUB * i + SUB] for i in range(v.shape[0] // SUB)]
            if tag == "f":
                return parts
            out = parts + [pltpu.roll(t, PM, 0) for t in parts]
            return [jnp.where(sub < PM, t, 0.0) for t in out[:count]]

        def put(ref, index, parts):
            for i, t in enumerate(parts):
                ref[index, SUB * i : SUB * i + SUB, :] = t

        def add_faces(tag, edges):
            level = FINE if tag == "f" else MID
            par = parity[tag]
            parity[tag] = 1 - par
            which = X_DIRS + Z_DIRS + (EDGE_DIRS if edges else ())
            wait_some(lambda i: face_copy(tag, par, i), which)
            buf, rx, rz, rc = (s[n + tag] for n in ("l", "rx", "rz", "rc"))
            last, top = level.points - 1, level.rows - SUB
            for side, a in ((0, 0), (1, last)):
                for z, t in enumerate(unpack(tag, rx[par, side], level.planes)):
                    buf[a, SUB * z : SUB * z + SUB, :] += t
            for side, row in ((0, 0), (1, top)):
                for a, t in enumerate(unpack(tag, rz[par, side], level.points)):
                    buf[a, row : row + SUB, :] += t
            if edges:
                for k, (a, row) in enumerate(((0, 0), (0, top), (last, 0), (last, top))):
                    buf[a, row : row + SUB, :] += rc[par, k]

        def sum_y(tag, a, first=0, count=None):
            level = FINE if tag == "f" else MID
            n = level.planes if count is None else count
            buf = s["l" + tag]
            rows_lo = pl.ds(SUB * first, n, stride=SUB)
            rows_hi = pl.ds(SUB * first + level.points - 1, n, stride=SUB)
            lo, hi = buf[a, rows_lo, :], buf[a, rows_hi, :]
            at = lax.broadcasted_iota(jnp.int32, (n, LANES), 1)
            buf[a, rows_lo, :] = lo + jnp.where(at > 0, pltpu.roll(hi, 1, 1), 0.0)
            buf[a, rows_hi, :] = hi + jnp.where(
                at < LANES - 1, pltpu.roll(lo, LANES - 1, 1), 0.0
            )

        def sum_y_planes(tag, row):
            p = (FINE if tag == "f" else MID).points
            sel = (slice(1, p - 1), slice(row, row + SUB))
            t = s["l" + tag][sel]
            up = pltpu.roll(pltpu.roll(t, 1, 2), SUB - p + 1, 1)
            down = pltpu.roll(pltpu.roll(t, LANES - 1, 2), p - 1, 1)
            t = t + jnp.where((sub == 0) & (lane > 0), up, 0.0)
            t = t + jnp.where((sub == p - 1) & (lane < LANES - 1), down, 0.0)
            s["l" + tag][sel] = t

        def gather_a(tag, k):
            buf = s[tag + "a"]
            return pltpu.make_async_remote_copy(
                src_ref=buf.at[dev],
                dst_ref=buf.at[dev],
                send_sem=s[tag + "a_s"].at[k],
                recv_sem=s[tag + "a_r"].at[k],
                device_id=(node, far(k)),
                device_id_type=MESH,
            )

        block = {"d": 2 * n_dev, "g": low_rows}
        base = {"d": 0, "g": low_rows}

        def slot(tag, index):
            size = block[tag]
            return s[tag + "b"].at[pl.ds(pl.multiple_of(base[tag] + index * size, size), size)]

        def gather_b(tag, k):
            return pltpu.make_async_remote_copy(
                src_ref=slot(tag, node),
                dst_ref=slot(tag, node),
                send_sem=s[tag + "b_s"].at[k],
                recv_sem=s[tag + "b_r"].at[k],
                device_id=(same_core(k), dev),
                device_id_type=MESH,
            )

        def gather_c(tag, k):
            index = lax.rem(node - 2 * k + n_node, n_node)
            return pltpu.make_async_remote_copy(
                src_ref=slot(tag, index),
                dst_ref=slot(tag, index),
                send_sem=s[tag + "c_s"].at[k],
                recv_sem=s[tag + "c_r"].at[k],
                device_id=sibling,
                device_id_type=MESH,
            )

        def loop(lower, upper, fn):
            def step(k, _):
                fn(k)
                return 0

            lax.fori_loop(lower, upper, step, 0)

        def start_a(tag):
            loop(1, n_dev, lambda k: gather_a(tag, k).start())

        def wait_a(tag):
            loop(1, n_dev, lambda k: gather_a(tag, k).wait())

        def start_b(tag):
            loop(1, half, lambda k: gather_b(tag, k).start())
            gather_c(tag, 0).start()

        def forward_b(tag):
            def one(k):
                gather_b(tag, k).wait_recv()
                gather_c(tag, k).start()

            loop(1, half, one)

        def wait_b(tag):
            loop(1, half, lambda k: gather_b(tag, k).wait_send())
            loop(0, half, lambda k: gather_c(tag, k).wait())

        def along_y(tag, v):
            p = (FINE if tag == "f" else MID).points
            acc = const("ky" + tag, 0) * v
            for shift in range(1, SUB):
                if p == PF or shift < p or shift > SUB - p:
                    acc = acc + const("ky" + tag, shift) * pltpu.roll(v, shift, 1)
            return acc

        def along_z(tag, v):
            level = FINE if tag == "f" else MID
            n, p = level.planes, level.points
            parts = [v[SUB * i : SUB * i + SUB] for i in range(n)]
            low = mix_even_odd(level.khat, parts[:p])
            high = mix_even_odd(level.khat, parts[p - 1 :])
            first = s["dz" + tag][0:SUB, :]
            second = s["dz" + tag][level.rows - SUB : level.rows, :]
            out = [first * t for t in low[: p - 1]]
            out.append(first * low[p - 1] + second * high[0])
            out += [second * t for t in high[1:]]
            return out, low[0], high[-1]

        def faces(tag, name):
            level = FINE if tag == "f" else MID
            n, p, top = level.planes, level.points, level.rows - SUB
            src, dst, dz = s[name + tag], s["l" + tag], s["dz" + tag]
            mass_row, _ = CONSTS.at["mz" + tag]
            has = (has_lo.astype(jnp.float32), has_hi.astype(jnp.float32))
            ends = (0, p - 1)
            even_row = 0.5 * (level.khat[0:1] + level.khat[0:1, ::-1])[:, : p // 2]
            odd_row = 0.5 * (level.khat[0:1] - level.khat[0:1, ::-1])[:, : p // 2]
            x_edge, z_edge = {}, {}
            chunk = 5 if tag == "f" else n
            for z0 in range(0, n, chunk):
                rows = slice(SUB * z0, SUB * (z0 + chunk))
                v = [src[a, rows, :] for a in range(p)]
                even = mix(even_row, [v[i] + v[p - 1 - i] for i in range(p // 2)])[0]
                odd = mix(odd_row, [v[i] - v[p - 1 - i] for i in range(p // 2)])[0]
                for f, xt in ((0, even + odd), (1, even - odd)):
                    if z0 == 0:
                        x_edge[f, 0] = xt[0:SUB]
                    if z0 + chunk == n:
                        x_edge[f, 1] = xt[-SUB:]
                    u = v[ends[f]]
                    yt = along_y(tag, u.reshape(chunk, SUB, LANES)).reshape(chunk * SUB, LANES)
                    mass = s["cst"][mass_row + SUB * z0 : mass_row + SUB * (z0 + chunk), :]
                    dst[ends[f], rows, :] = dz[rows, :] * (xt + yt) + mass * u
            for f, a in enumerate(ends):
                out, z_edge[f, 0], z_edge[f, 1] = along_z(tag, src[a])
                out = [t + dst[a, SUB * z : SUB * z + SUB, :] for z, t in enumerate(out)]
                put(dst, a, out)
                out[0] = out[0] + s["side"][4] * x_edge[f, 0]
                out[-1] = out[-1] + s["side"][5] * x_edge[f, 1]
                put(s["sx" + tag], f, pack(tag, out))
            start_faces(tag, X_DIRS)
            for side, row in ((0, 0), (1, top)):
                rows = slice(row, row + SUB)
                v = src[:, rows, :]
                yt = along_y(tag, v)
                xt = mix_even_odd(level.khat, [v[a] for a in range(p)])
                plane0 = 0 if side == 0 else p - 1
                zt = mix(
                    level.khat[p - 1 : p] if side else level.khat[0:1],
                    [
                        src[1 : p - 1, SUB * (plane0 + c) : SUB * (plane0 + c) + SUB, :]
                        for c in range(p)
                    ],
                )[0]
                weight = dz[rows, :]
                out = [None] * p
                for a in range(1, p - 1):
                    out[a] = weight * (xt[a] + yt[a] + zt[a - 1]) + SHIFT_MASS * v[a]
                    dst[a, rows, :] = out[a]
                for f, a in enumerate(ends):
                    out[a] = (
                        dst[a, rows, :]
                        + s["side"][2 * f + side] * (z_edge[f, side] + yt[a])
                        + (SHIFT_MASS * has[f]) * v[a]
                    )
                put(s["sz" + tag], side, pack(tag, out))
            start_faces(tag, Z_DIRS)

        def interior(tag, name, after=None):
            level = FINE if tag == "f" else MID
            n, p = level.planes, level.points
            src, dst = s[name + tag], s["l" + tag]

            def plane(z):
                rows = pl.ds(pl.multiple_of(z * SUB, SUB), SUB)
                v = src[:, rows, :]
                acc = along_y(tag, v[1 : p - 1])
                along_x = mix_even_odd(level.khat, [v[a] for a in range(p)])
                weight = s["dz" + tag][rows, :]
                mass = jnp.where(z == p - 1, 2.0 * SHIFT_MASS, SHIFT_MASS)
                for a in range(1, p - 1):
                    dst[a, rows, :] = weight * (acc[a - 1] + along_x[a]) + mass * v[a]

            loop(1, n - 1, plane)

            def line(a):
                out, _, _ = along_z(tag, src[a])
                for i in range(1, n - 1):
                    dst[a, SUB * i : SUB * i + SUB, :] += out[i]
                if after is not None:
                    after(a)

            loop(1, p - 1, line)

        def apply(tag, name):
            level = FINE if tag == "f" else MID
            n, p = level.planes, level.points
            src, dst = s[name + tag], s["l" + tag]

            def plane(z):
                rows = pl.ds(pl.multiple_of(z * SUB, SUB), SUB)
                v = src[:, rows, :]
                acc = along_y(tag, v)
                along_x = mix_even_odd(level.khat, [v[a] for a in range(p)])
                weight = s["dz" + tag][rows, :]
                mass = jnp.where(z == p - 1, 2.0 * SHIFT_MASS, SHIFT_MASS)
                for a in range(p):
                    dst[a, rows, :] = weight * (acc[a] + along_x[a]) + mass * v[a]

            loop(0, n, plane)

            def line(a):
                out, _, _ = along_z(tag, src[a])
                for i in range(n):
                    dst[a, SUB * i : SUB * i + SUB, :] += out[i]

            loop(0, p, line)

        def update(tag, kind, c1=0.0, c2=0.0, last=False, residual="r"):
            level = FINE if tag == "f" else MID
            c = float(1.0 / level.theta)
            l, rhs, inv, x, r, d = (s[k + tag] for k in ("l", "rhs", "inv", "x", "r", "d"))
            old = s[residual + tag]

            def on(*sel):
                if kind == "zero":
                    res = l[sel]
                    rhs[sel] = res
                    upd = c * inv[sel] * res
                    d[sel] = upd
                    x[sel] = upd
                elif kind == "first":
                    res = rhs[sel] - l[sel]
                    r[sel] = res
                    upd = c * inv[sel] * res
                    d[sel] = upd
                    x[sel] = x[sel] + upd
                else:
                    res = old[sel] - l[sel]
                    upd = c1 * d[sel] + c2 * inv[sel] * res
                    if not last:
                        r[sel] = res
                        d[sel] = upd
                    x[sel] = x[sel] + upd

            return on

        def inner_update(tag, on):
            level = FINE if tag == "f" else MID

            def one(a):
                sum_y(tag, a, 1, level.planes - 2)
                on(a, slice(SUB, level.rows - SUB))

            return one

        def face_update(tag, on, edges=False):
            level = FINE if tag == "f" else MID
            add_faces(tag, edges)
            for a in (0, level.points - 1):
                sum_y(tag, a)
                on(a, slice(0, level.rows))
            for row in (0, level.rows - SUB):
                sum_y_planes(tag, row)
                on(slice(1, level.points - 1), slice(row, row + SUB))

        def raw_round(tag, on, before_inner, before_faces):
            level = FINE if tag == "f" else MID
            buf, last, top = s["l" + tag], level.points - 1, level.rows - SUB
            start_faces(tag, EDGE_DIRS)
            for f, a in ((0, 0), (1, last)):
                put(
                    s["sx" + tag],
                    f,
                    pack(tag, [buf[a, SUB * z : SUB * z + SUB, :] for z in range(level.planes)]),
                )
            start_faces(tag, X_DIRS)
            for side, row in ((0, 0), (1, top)):
                put(
                    s["sz" + tag],
                    side,
                    pack(tag, [buf[a, row : row + SUB, :] for a in range(level.points)]),
                )
            start_faces(tag, Z_DIRS)
            before_inner()
            loop(1, last, inner_update(tag, on))
            before_faces()
            face_update(tag, on, True)

        def steps(tag, count, residual, between):
            coefs = (FINE if tag == "f" else MID).steps(count)
            for index, (c1, c2) in enumerate(coefs):
                on = update(tag, "next", c1, c2, index == count - 2, residual)
                residual = "r"
                faces(tag, "d")
                interior(tag, "d", inner_update(tag, on))
                between[index]()
                face_update(tag, on)

        ones = [has_lo.astype(jnp.float32), 1.0, has_hi.astype(jnp.float32)]
        copies = [1.0 + ones[0], 1.0, 1.0 + ones[2]]
        levels = (("f", FINE), ("m", MID))

        def spread_row(row):
            return jnp.broadcast_to(row, (SUB, LANES))

        def patch(dx):
            at = lambda dz: s["dhalo"].at[DIRS.index((dx, dz))]
            mid = s["dsrc"] if dx == 0 else at(0)
            rows = [at(-1)[1:2, :], mid[0:1, :], mid[1:2, :], at(1)[0:1, :]]
            return [spread_row(row) for row in rows]

        def kinds_of(q):
            return [q[0] + q[1], q[1], q[1] + q[2], q[2], q[2] + q[3]]

        def kind_of(z, p):
            return {0: 0, p - 1: 2, 2 * p - 2: 4}.get(z, 1 if z < p else 3)

        def nodal(k, p):
            lo = k + jnp.where(lane > 0, pltpu.roll(k, 1, 1), 0.0)
            hi = k + jnp.where(lane < LANES - 1, pltpu.roll(k, LANES - 1, 1), 0.0)
            return jnp.where(sub == 0, lo, jnp.where(sub == p - 1, hi, k))

        def set_inverse(tag, level, a, xc, rows):
            row_k, _ = CONSTS.at["kzb" + tag]
            row_c, _ = CONSTS.at["cnt" + tag]
            kzb = s["cst"][row_k + rows.start : row_k + rows.stop, :]
            cnt = s["cst"][row_c + rows.start : row_c + rows.stop, :]
            diag = (float(level.kdiag[a]) + kzb) * s["cls" + tag][xc, rows, :]
            s["inv" + tag][a, rows, :] = 1.0 / (diag + copies[xc] * cnt)

        def diagonals_inside():
            first, second = spread_row(s["dsrc"][0:1, :]), spread_row(s["dsrc"][1:2, :])
            kinds = [first, first, first + second, second, second]
            for tag, level in levels:
                p = level.points
                full = [nodal(k, p) for k in kinds]
                for z in range(level.planes):
                    rows = slice(SUB * z, SUB * z + SUB)
                    s["dz" + tag][rows, :] = kinds[kind_of(z, p)]
                    s["cls" + tag][1, rows, :] = full[kind_of(z, p)]
                for a in range(1, p - 1):
                    set_inverse(tag, level, a, 1, slice(SUB, level.rows - SUB))

        def diagonals_faces():
            q = [patch(-1), patch(0), patch(1)]
            for side in range(2):
                s["side"][side] = q[0][1 + side]
                s["side"][2 + side] = q[2][1 + side]
                s["side"][4 + side] = q[1][3 * side]
            xs = [[u + v for u, v in zip(q[0], q[1])], q[1], [u + v for u, v in zip(q[1], q[2])]]
            for xc in range(3):
                kinds = kinds_of(xs[xc])
                for tag, level in levels:
                    p = level.points
                    full = [
                        None if xc == 1 and i in (1, 2, 3) else nodal(k, p)
                        for i, k in enumerate(kinds)
                    ]
                    for z in range(level.planes):
                        value = full[kind_of(z, p)]
                        if value is not None:
                            s["cls" + tag][xc, SUB * z : SUB * z + SUB, :] = value
            for tag, level in levels:
                p, n = level.points, level.rows
                set_inverse(tag, level, 0, 0, slice(0, n))
                set_inverse(tag, level, p - 1, 2, slice(0, n))
                for a in range(1, p - 1):
                    set_inverse(tag, level, a, 1, slice(0, SUB))
                    set_inverse(tag, level, a, 1, slice(n - SUB, n))

        def restrict_fine():
            def line(a):
                res = s["locf"][a] - s["lf"][a]
                parts = [res[SUB * i : SUB * i + SUB] for i in range(FINE.planes)]
                for i, t in enumerate(mix(R73Z.T, parts)):
                    s["tmpf"][a, SUB * i : SUB * i + SUB, :] = t

            loop(0, PF, line)

            def plane(z):
                rows = pl.ds(pl.multiple_of(z * SUB, SUB), SUB)
                v = s["tmpf"][:, rows, :]
                t = jnp.stack(mix(R73, [v[a] for a in range(PF)]))
                acc = const("r73", 0) * t
                for shift in range(1, SUB):
                    acc = acc + const("r73", shift) * pltpu.roll(t, shift, 1)
                s["locm"][:, rows, :] = acc
                s["lm"][:, rows, :] = acc

            loop(0, MID.planes, plane)

        def prolong_fine():
            def plane(z):
                rows = pl.ds(pl.multiple_of(z * SUB, SUB), SUB)
                v = s["xm"][:, rows, :]
                acc = const("j73", 0) * v
                for shift in range(1, SUB):
                    acc = acc + const("j73", shift) * pltpu.roll(v, shift, 1)
                for a, t in enumerate(mix(J73, [acc[i] for i in range(PM)])):
                    s["tmpf"][a, rows, :] = t

            loop(0, MID.planes, plane)

            def line(a):
                v = s["tmpf"][a]
                parts = [v[SUB * i : SUB * i + SUB] for i in range(MID.planes)]
                for i, t in enumerate(mix(J73Z, parts)):
                    s["xf"][a, SUB * i : SUB * i + SUB, :] += t

            loop(0, PF, line)

        def restrict_mid():
            for a in range(PM):
                res = s["locm"][a] - s["lm"][a]
                parts = [res[SUB * i : SUB * i + SUB] for i in range(MID.planes)]
                for i, t in enumerate(mix(R31Z.T, parts)):
                    s["tmpm"][a, SUB * i : SUB * i + SUB, :] = t
            spare = jnp.zeros((SUB, LANES), jnp.float32)
            for z in range(3):
                v = s["tmpm"][:, SUB * z : SUB * z + SUB, :]
                for a, t in enumerate(mix(R31, [v[i] for i in range(PM)])):
                    acc = const("r31", 0) * t
                    for shift in (1, 5, 6, 7):
                        acc = acc + const("r31", shift) * pltpu.roll(t, shift, 0)
                    up = pltpu.roll(pltpu.roll(acc, 1, 1), SUB - 1, 0)
                    node_row = acc + jnp.where(lane > 0, up, 0.0)
                    s["ga"][dev, 3 * a + z : 3 * a + z + 1, :] = node_row[0:1, :]
                    spare = spare + jnp.where(lane == z * nx + dev + a, up[0:1, 0:1], 0.0)
            s["ga"][dev, 6:7, :] = spare[0:1, :]
            s["ga"][dev, 7:8, :] = jnp.zeros((1, LANES), jnp.float32)

        def sum_x_low():
            flat = s["ga"]
            g = jnp.zeros((low_rows, LANES), jnp.float32)
            pad = lambda rows, before: jnp.pad(
                rows, ((before, low_rows - before - rows.shape[0]), (0, 0))
            )
            mine = s["gb"].at[
                pl.ds(pl.multiple_of(low_rows + node * low_rows, low_rows), low_rows)
            ]
            mine[...] = g
            for z in range(3):
                mine[z * nx : z * nx + n_dev, :] = flat[:, z, :]
                mine[z * nx + 1 : z * nx + nx, :] += flat[:, 3 + z, :]
            mine[3 * nx : 3 * nx + 1, :] = jnp.sum(flat[:, 6, :], axis=0, keepdims=True)

        def wide(rows):
            return jnp.concatenate([rows, jnp.zeros_like(rows)], axis=1)

        def low_weights():
            up_y = lambda v: pltpu.roll(v, 1, 1)
            up_z = lambda v: pltpu.roll(v, 1, 0)
            elem = lambda x: s["db"][pl.ds(x, nz, stride=n_dev), :]
            zero = jnp.zeros((nz, 2 * LANES), jnp.float32)
            lanes = lax.broadcasted_iota(jnp.int32, (nz, 2 * LANES), 1)
            inside = (lanes <= LANES).astype(jnp.float32)
            y_copies = (
                inside + ((lanes > 0) & (lanes < LANES)).astype(jnp.float32)
            )
            for x in range(nx):
                lo = wide(elem(x - 1)) if x > 0 else zero
                hi = wide(elem(x)) if x < n_dev else zero
                both = lo + hi
                wy = 0.5 * (both + up_z(both))
                wz = 0.5 * (both + up_y(both))
                s["c_wy"][x] = wy
                s["c_wym"][x] = up_y(wy)
                s["c_wz"][x] = wz
                s["c_wzm"][x] = up_z(wz)
                hz = hi + up_z(hi)
                wx = 0.5 * (hz + up_y(hz))
                s["c_wx"][x] = wx
                wxm = s["c_wx"][x - 1] if x > 0 else zero
                x_copies = 1.0 if x in (0, n_dev) else 2.0
                s["c_dg"][x] = (
                    wx + wxm + wy + s["c_wym"][x] + wz + s["c_wzm"][x]
                    + 2.0 * SHIFT_MASS * x_copies * y_copies
                )

        def low_rhs():
            buf = s["gb"]
            buf[0:low_rows, :] = buf[n_node * low_rows : (n_node + 1) * low_rows, :]
            own = lambda row: buf[pl.ds(low_rows + row, n_node, stride=low_rows), :]
            before = lambda row: buf[pl.ds(row, n_node, stride=low_rows), :]
            at = lax.broadcasted_iota(jnp.int32, (n_node, LANES), 1)
            spare, spare_before = own(3 * nx), before(3 * nx)

            def pick(rows, lane_index):
                moved = rows if lane_index == 0 else pltpu.roll(rows, LANES - lane_index, 1)
                return jnp.where(at == 0, moved, 0.0)

            even, odd = pl.ds(0, n_node, stride=2), pl.ds(1, n_node, stride=2)
            left, right = pl.ds(0, LANES), pl.ds(LANES, LANES)
            res, main, rest = s["c_cr"], s["c_main"], s["c_rest"]
            for x in range(nx):
                main[even, :] = own(x) + before(2 * nx + x)
                main[odd, :] = own(nx + x)
                rest[even, :] = pick(spare, x) + pick(spare_before, 2 * nx + x)
                rest[odd, :] = pick(spare, nx + x)
                res[x, :, left] = main[...]
                res[x, :, right] = rest[...]

        def fold(v):
            parts = [v[i : i + SUB] for i in range(0, v.shape[0], SUB)]
            while len(parts) > 1:
                parts = [u + w for u, w in zip(parts[::2], parts[1::2])] + (
                    [parts[-1]] if len(parts) % 2 else []
                )
            return parts[0][:, :LANES] + parts[0][:, LANES:]

        def total(v):
            return jnp.sum(v, axis=(0, 1), keepdims=True)

        def set_direction(x, value):
            p = s["c_p"]
            p[x, SUB : SUB + nz, :] = value
            p[x, 0:SUB, :] = value[nz - SUB : nz]
            p[x, SUB + nz : 2 * SUB + nz, :] = value[0:SUB]

        def coarse_solve():
            p, q, res, sol = s["c_p"], s["c_cq"], s["c_cr"], s["c_cx"]
            wide_lanes = 2 * LANES
            here = pl.ds(SUB, nz)
            norm = jnp.zeros((SUB, LANES), jnp.float32)
            for x in range(nx):
                v = res[x]
                set_direction(x, v)
                sol[x] = jnp.zeros_like(v)
                norm = norm + fold(v * v)

            def iteration(_, now):
                dot = jnp.zeros((SUB, LANES), jnp.float32)
                for x in range(nx):
                    v = p[x, here, :]
                    out = s["c_dg"][x] * v
                    if x > 0:
                        out = out - s["c_wx"][x - 1] * p[x - 1, here, :]
                    if x < nx - 1:
                        out = out - s["c_wx"][x] * p[x + 1, here, :]
                    out = out - s["c_wy"][x] * pltpu.roll(v, wide_lanes - 1, 1)
                    out = out - s["c_wym"][x] * pltpu.roll(v, 1, 1)
                    out = out - s["c_wz"][x] * p[x, SUB + 1 : SUB + 1 + nz, :]
                    out = out - s["c_wzm"][x] * p[x, SUB - 1 : SUB - 1 + nz, :]
                    q[x] = out
                    dot = dot + fold(v * out)
                alpha = now / total(dot)
                norm = jnp.zeros((SUB, LANES), jnp.float32)
                for x in range(nx):
                    sol[x] += alpha * p[x, here, :]
                    v = res[x] - alpha * q[x]
                    res[x] = v
                    norm = norm + fold(v * v)
                new = total(norm)
                beta = new / now
                for x in range(nx):
                    set_direction(x, res[x] + beta * p[x, here, :])
                return new

            lax.fori_loop(0, COARSE_ITERS, iteration, total(norm))

        def add_low():
            p, n = PM, MID.planes
            h = float((MID.khat @ J31)[0, 0])
            spread = {}
            for i in range(4):
                for k in range(5):
                    if i in (0, 3) and k in (0, 4):
                        continue
                    x = jnp.clip(dev + i - 1, 0, n_dev)
                    z = lax.rem(2 * node + k - 1 + nz, nz)
                    row = s["c_cx"][x, pl.ds(z, 1), :]
                    row = jnp.broadcast_to(row, (SUB, 2 * LANES))
                    low = row[:, :LANES]
                    high = pltpu.roll(row, 2 * LANES - 1, 1)[:, :LANES]
                    spread[i, k] = const("j31", 0) * low + const("j31", 1) * high
            left = mix(J31Z, [spread[0, k] for k in (1, 2, 3)])
            right = mix(J31Z, [spread[3, k] for k in (1, 2, 3)])
            inner = [
                mix(J31, [spread[1, k], spread[2, k]]) for k in range(5)
            ]
            q = [patch(-1), patch(0), patch(1)]
            xs = [[u + v for u, v in zip(q[0], q[1])], q[1], [u + v for u, v in zip(q[1], q[2])]]
            along_x = [kinds_of(v) for v in q]
            lines = [mix(J31Z, [inner[k][a] for k in (1, 2, 3)]) for a in range(p)]
            for a in range(p):
                xc = 0 if a == 0 else 2 if a == p - 1 else 1
                w, u = xs[xc], lines[a]
                kinds = kinds_of(w)
                ends = (0, p - 1, n - 1)
                slope = [u[0] - inner[0][a], u[p - 1] - u[0], u[n - 1] - u[p - 1], inner[4][a] - u[n - 1]]
                flow = [v * t for v, t in zip(w, slope)]
                for z in range(n):
                    rows = slice(SUB * z, SUB * z + SUB)
                    kind = kind_of(z, p)
                    copies_z = 2.0 if z in ends else 1.0
                    out = kinds[kind] * along_y("m", u[z][None])[0]
                    out = out + (SHIFT_MASS * copies_z * copies[xc]) * u[z]
                    if z in ends:
                        k = ends.index(z)
                        out = out + h * (flow[k] - flow[k + 1])
                    if a == 0:
                        out = out + h * (
                            along_x[0][kind] * (u[z] - left[z])
                            + along_x[1][kind] * (u[z] - lines[p - 1][z])
                        )
                    if a == p - 1:
                        out = out + h * (
                            along_x[1][kind] * (u[z] - lines[0][z])
                            + along_x[2][kind] * (u[z] - right[z])
                        )
                    s["lm"][a, rows, :] += out
                    s["xm"][a, rows, :] += u[z]

        nothing = lambda: None
        load_diff.wait()
        s["da"][dev] = s["dsrc"][...]
        wait_barrier()
        start_some(halo_copy, range(8))
        load_cst.wait()
        load_in.wait()
        wz = np.concatenate([FINE.w, FINE.w[1:]])

        def load_line(a):
            planes = []
            for e in range(2):
                for c in range(PF):
                    start = a * (PF * PF * 2) + 2 * c + e
                    planes.append(s["ein"][pl.ds(start, SUB, stride=2 * PF), :])
            merged = planes[: PF - 1] + [planes[PF - 1] + planes[PF]] + planes[PF + 1 :]
            scale = const("iwb") * wa_inverse(a)
            for z, v in enumerate(merged):
                t = scale * v * float(1.0 / wz[z])
                s["locf"][a, SUB * z : SUB * z + SUB, :] = t
                s["lf"][a, SUB * z : SUB * z + SUB, :] = t

        def wa_inverse(a):
            value = jnp.float32(1.0 / FINE.w[0])
            for i in range(1, PF // 2):
                value = jnp.where((a == i) | (a == PF - 1 - i), 1.0 / FINE.w[i], value)
            return value

        loop(0, PF, load_line)

        def halo_done():
            start_a("d")
            wait_some(halo_copy, range(8))
            diagonals_faces()

        def diff_stage_b():
            wait_a("d")
            mine = slot("d", node)
            for e in range(2):
                mine[e * n_dev : (e + 1) * n_dev, :] = s["da"][:, e, :]
            start_b("d")

        raw_round("f", update("f", "zero"), diagonals_inside, halo_done)
        steps("f", SMOOTH_FINE, "rhs", [diff_stage_b, lambda: forward_b("d")])
        apply("f", "x")
        restrict_fine()

        def weights():
            wait_b("d")
            low_weights()

        raw_round("m", update("m", "zero"), nothing, weights)
        steps("m", SMOOTH_MID, "rhs", [nothing, nothing])
        faces("m", "x")
        interior("m", "x")
        restrict_mid()
        start_a("g")
        add_faces("m", False)
        wait_a("g")
        sum_x_low()
        start_b("g")
        forward_b("g")
        wait_b("g")
        low_rhs()
        coarse_solve()
        add_low()
        first = update("m", "first")

        def first_mid(a):
            sum_y("m", a)
            first(a, slice(0, MID.rows))

        loop(0, PM, first_mid)
        steps("m", SMOOTH_MID, "r", [nothing, nothing])
        prolong_fine()
        first = update("f", "first")
        faces("f", "x")
        interior("f", "x", inner_update("f", first))
        face_update("f", first)
        steps("f", SMOOTH_FINE, "r", [nothing, nothing])

        chunk = PF * PF * 2

        def out_copy(a):
            rows = pl.ds(pl.multiple_of(a * chunk, chunk), chunk)
            return pltpu.make_async_copy(
                s["eout"].at[rows], out_hbm.at[rows], s["outsem"].at[a]
            )

        def store_line(a):
            for e in range(2):
                for c in range(PF):
                    z = e * (PF - 1) + c
                    start = a * chunk + 2 * c + e
                    s["eout"][pl.ds(start, SUB, stride=2 * PF), :] = s["xf"][
                        a, SUB * z : SUB * z + SUB, :
                    ]
            out_copy(a).start()

        loop(0, PF, store_line)
        loop(0, PF, lambda a: out_copy(a).wait())

    return kernel


def solution(mesh):
    n_node, n_dev = mesh.shape["node"], mesh.shape["dev"]
    shapes, low_rows = scratch_shapes(n_node, n_dev)
    kernel = make_kernel(n_node, n_dev, list(shapes), low_rows)
    rows = PF * PF * PF * 2

    def local(element_load, diffusivity):
        out = pl.pallas_call(
            kernel,
            out_shape=jax.ShapeDtypeStruct((rows, LANES), jnp.float32),
            in_specs=[pl.BlockSpec(memory_space=pltpu.HBM)] * 3,
            out_specs=pl.BlockSpec(memory_space=pltpu.HBM),
            scratch_shapes=list(shapes.values()),
            compiler_params=pltpu.CompilerParams(
                collective_id=0, has_side_effects=True, vmem_limit_bytes=48 * 1024 * 1024
            ),
        )(
            element_load.reshape(rows, LANES),
            diffusivity.reshape(2, LANES),
            jnp.asarray(CONSTS.array()),
        )
        return out.reshape(element_load.shape)

    return jax.shard_map(
        local,
        mesh=mesh,
        in_specs=(P(None, None, None, "dev", "node", None), P("dev", "node", None)),
        out_specs=P(None, None, None, "dev", "node", None),
        check_vma=False,
    )
```

```python
import jax
import jax.numpy as jnp
import numpy as np
from jax import lax
from jax.experimental import pallas as pl
from jax.experimental.pallas import tpu as pltpu
from jax.sharding import PartitionSpec as P

PF = 8
PM = 4
PC = 2
SMOOTH_FINE = 3
SMOOTH_MID = 3
COARSE_ITERS = 5
SHIFT_MASS = 0.05
LANES = 128
SUB = 8
MESH = pl.DeviceIdType.MESH

def legendre_values(points, poly_order):
    columns = [points * 0.0 + 1.0, points]
    for degree in range(2, poly_order + 1):
        columns.append(
            ((2 * degree - 1) * points * columns[degree - 1] - (degree - 1) * columns[degree - 2])
            / degree
        )
    return np.stack(columns[: poly_order + 1], axis=1)


def largest_eigen(matrix):
    size_n = matrix.shape[0]
    vector = np.cos(2.7 * np.arange(size_n) + 0.3)
    for power_step in range(4000):
        vector = matrix @ vector
        vector = vector / np.sqrt(np.sum(vector * vector))
    return float(vector @ (matrix @ vector))


def gll_level(poly_order):
    point_count = poly_order + 1
    gll_nodes = np.cos(np.pi * np.arange(point_count) / poly_order)
    for newton_step in range(60):
        values = legendre_values(gll_nodes, poly_order)
        gll_nodes = gll_nodes - (gll_nodes * values[:, poly_order] - values[:, poly_order - 1]) / (
            point_count * values[:, poly_order]
        )
    gll_nodes = np.sort(gll_nodes)
    values = legendre_values(gll_nodes, poly_order)
    top_value = values[:, poly_order]
    weights = 2.0 / (poly_order * point_count * top_value**2)
    deriv_matrix = np.zeros((point_count, point_count))
    for row_index in range(point_count):
        for col_index in range(point_count):
            if row_index != col_index:
                deriv_matrix[row_index, col_index] = top_value[row_index] / (
                    top_value[col_index] * (gll_nodes[row_index] - gll_nodes[col_index])
                )
    deriv_matrix[0, 0] = -poly_order * point_count / 4.0
    deriv_matrix[poly_order, poly_order] = poly_order * point_count / 4.0
    stiffness = deriv_matrix.T @ (weights[:, None] * deriv_matrix)
    diag_ids = np.arange(point_count)
    stiff_diag = stiffness[diag_ids, diag_ids]
    diag_scale = 1.0 / np.sqrt(stiff_diag)
    eig_bound = largest_eigen(diag_scale[:, None] * stiffness * diag_scale[None, :])
    return (gll_nodes, weights, deriv_matrix, stiff_diag, eig_bound)


def interp_table(fine_nodes, coarse_nodes):
    interp_mat = np.ones((fine_nodes.shape[0], coarse_nodes.shape[0]))
    for col_index in range(coarse_nodes.shape[0]):
        for other_index in range(coarse_nodes.shape[0]):
            if other_index != col_index:
                interp_mat[:, col_index] *= (fine_nodes - coarse_nodes[other_index]) / (
                    coarse_nodes[col_index] - coarse_nodes[other_index]
                )
    return interp_mat


class Level:
    def __init__(self, points):
        nodes, w, deriv, stiff_diag, bound = gll_level(points - 1)
        self.points = points
        self.planes = 2 * points - 1
        self.rows = SUB * self.planes
        self.x_rows = SUB * (self.planes if points == SUB else -(-self.planes // 2))
        self.z_rows = SUB * (points if points == SUB else -(-points // 2))
        self.nodes = nodes
        self.w = w
        self.khat = (deriv.T @ (w[:, None] * deriv)) / w[:, None]
        self.kdiag = stiff_diag / w
        self.theta = 0.6 * bound
        self.delta = 0.5 * bound

    def steps(self, count):
        sig = self.theta / self.delta
        rho = 1.0 / sig
        out = []
        for _ in range(count - 1):
            rho_next = 1.0 / (2.0 * sig - rho)
            out.append((float(rho_next * rho), float(2.0 * rho_next / self.delta)))
            rho = rho_next
        return out


def roll_coefs(matrix):
    full = np.zeros((SUB, SUB))
    full[: matrix.shape[0], : matrix.shape[1]] = matrix
    i = np.arange(SUB)
    return [full[i, (i - s) % SUB] for s in range(SUB)]


def two_elements(matrix):
    n, m = matrix.shape
    out = np.zeros((2 * n - 1, 2 * m - 1))
    out[:n, :m] = matrix
    out[n - 1 :, m - 1 :] = matrix
    return out


def plane_sum(points):
    values = np.zeros((2 * points - 1,))
    values[:points] += 1
    values[points - 1 :] += 1
    return values


class Consts:
    def __init__(self):
        self.blocks = []
        self.at = {}
        self.row = 0

    def add(self, name, block):
        block = np.asarray(block, np.float64)
        if block.ndim == 1:
            block = np.broadcast_to(block[:, None], (block.shape[0], LANES))
        assert block.shape[0] % SUB == 0
        self.at[name] = (self.row, block.shape[0])
        self.blocks.append(block)
        self.row += block.shape[0]

    def array(self):
        return np.concatenate(self.blocks, 0).astype(np.float32)


FINE, MID, LOW = Level(PF), Level(PM), Level(PC)
J73 = interp_table(FINE.nodes, MID.nodes)
J31 = interp_table(MID.nodes, LOW.nodes)
R73 = (FINE.w[:, None] * J73 / MID.w[None, :]).T
R31 = (MID.w[:, None] * J31).T
R73Z = two_elements(FINE.w[:, None] * J73 / MID.w[None, :])
R73Z[PF - 1] = 0.0
R73Z[PF - 1, PM - 1] = FINE.w[0] / MID.w[0]
R31Z = two_elements(MID.w[:, None] * J31)
R31Z[PM - 1] = 0.0
R31Z[PM - 1, PC - 1] = MID.w[0]
J73Z = two_elements(J73)
J31Z = two_elements(J31)

CONSTS = Consts()
for tag, level in (("f", FINE), ("m", MID)):
    CONSTS.add("ky" + tag, np.concatenate(roll_coefs(level.khat)))
    kb = np.zeros(SUB)
    kb[: level.points] = level.kdiag
    kz = np.concatenate([level.kdiag, level.kdiag[1:]])
    CONSTS.add("kzb" + tag, (kz[:, None] + kb[None, :]).reshape(-1))
    ey = np.arange(LANES)
    my = np.ones((SUB, LANES))
    my[0] += ey > 0
    my[level.points - 1] += ey < LANES - 1
    mz = np.ones(level.planes)
    mz[[0, level.points - 1, -1]] = 2
    CONSTS.add("cnt" + tag, (SHIFT_MASS * mz[:, None, None] * my[None]).reshape(-1, LANES))
    CONSTS.add("mz" + tag, np.repeat(SHIFT_MASS * plane_sum(level.points), SUB))
CONSTS.add("r73", np.concatenate(roll_coefs(R73)))
CONSTS.add("j73", np.concatenate(roll_coefs(J73)))
CONSTS.add("r31", np.concatenate(roll_coefs(R31)))
CONSTS.add("j31", np.concatenate([np.pad(J31[:, p], (0, SUB - PM)) for p in range(PC)]))
CONSTS.add("iwb", 1.0 / FINE.w)

DIRS = ((-1, 0), (1, 0), (0, -1), (0, 1), (-1, -1), (-1, 1), (1, -1), (1, 1))
OPP = tuple(DIRS.index((-dx, -dz)) for dx, dz in DIRS)
COEF = 1e-13


def mix(matrix, parts):
    out = []
    for row in np.asarray(matrix):
        acc = None
        for c, v in zip(row, parts):
            if abs(c) > COEF:
                term = v if abs(c - 1.0) < COEF else float(c) * v
                acc = term if acc is None else acc + term
        out.append(acc)
    return out


def mix_even_odd(matrix, parts):
    n = len(parts)
    h = n // 2
    flipped = matrix[:h, ::-1][:, :h]
    even = mix(0.5 * (matrix[:h, :h] + flipped), [parts[i] + parts[n - 1 - i] for i in range(h)])
    odd = mix(0.5 * (matrix[:h, :h] - flipped), [parts[i] - parts[n - 1 - i] for i in range(h)])
    low = [e + o for e, o in zip(even, odd)]
    high = [e - o for e, o in zip(even, odd)]
    return low + high[::-1]


def scratch_shapes(n_node, n_dev):
    f32 = jnp.float32
    low_rows = -(-(3 * (n_dev + 1) + 1) // SUB) * SUB
    shapes = {}
    for tag, level in (("f", FINE), ("m", MID)):
        p, rows = level.points, level.rows
        for name in ("loc", "rhs", "inv", "x", "r", "d", "l"):
            shapes[name + tag] = pltpu.VMEM((p, rows, LANES), f32)
        shapes["cls" + tag] = pltpu.VMEM((3, rows, LANES), f32)
        shapes["dz" + tag] = pltpu.VMEM((rows, LANES), f32)
        shapes["rx" + tag] = pltpu.VMEM((2, 2, level.x_rows, LANES), f32)
        shapes["rz" + tag] = pltpu.VMEM((2, 2, level.z_rows, LANES), f32)
        shapes["sx" + tag] = pltpu.VMEM((2, level.x_rows, LANES), f32)
        shapes["sz" + tag] = pltpu.VMEM((2, level.z_rows, LANES), f32)
        shapes["rc" + tag] = pltpu.VMEM((2, 4, SUB, LANES), f32)
        shapes["ssem" + tag] = pltpu.SemaphoreType.DMA((8,))
        shapes["rsem" + tag] = pltpu.SemaphoreType.DMA((2, 8))
    shapes["tmpf"] = pltpu.VMEM((PF, MID.rows, LANES), f32)
    shapes["tmpm"] = pltpu.VMEM((PM, LOW.rows, LANES), f32)
    shapes["ein"] = pltpu.VMEM((PF * PF * PF * 2, LANES), f32)
    shapes["cst"] = pltpu.VMEM((CONSTS.row, LANES), f32)
    shapes["insem"] = pltpu.SemaphoreType.DMA((3,))
    shapes["side"] = pltpu.VMEM((6, SUB, LANES), f32)
    shapes["dsrc"] = pltpu.VMEM((SUB, LANES), f32)
    shapes["dhalo"] = pltpu.VMEM((8, SUB, LANES), f32)
    shapes["dssem"] = pltpu.SemaphoreType.DMA((8,))
    shapes["drsem"] = pltpu.SemaphoreType.DMA((8,))
    shapes["da"] = pltpu.VMEM((n_dev, SUB, LANES), f32)
    shapes["db"] = pltpu.VMEM((n_node * 2 * n_dev, LANES), f32)
    shapes["ga"] = pltpu.VMEM((n_dev, SUB, LANES), f32)
    shapes["gb"] = pltpu.VMEM(((n_node + 1) * low_rows, LANES), f32)
    half = n_node // 2
    for tag in "dg":
        shapes[tag + "a_s"] = pltpu.SemaphoreType.DMA((n_dev,))
        shapes[tag + "a_r"] = pltpu.SemaphoreType.DMA((n_dev,))
        shapes[tag + "b_s"] = pltpu.SemaphoreType.DMA((half,))
        shapes[tag + "b_r"] = pltpu.SemaphoreType.DMA((half,))
        shapes[tag + "c_s"] = pltpu.SemaphoreType.DMA((half,))
        shapes[tag + "c_r"] = pltpu.SemaphoreType.DMA((half,))
    nx, nz = n_dev + 1, 2 * n_node
    for name in ("wx", "wy", "wym", "wz", "wzm", "dg", "cx", "cr", "cq"):
        shapes["c_" + name] = pltpu.VMEM((nx + 1, nz, LANES), f32)
    shapes["c_wxm"] = pltpu.VMEM((nz, LANES), f32)
    shapes["c_main"] = pltpu.VMEM((nz, LANES), f32)
    shapes["c_p"] = pltpu.VMEM((nx + 1, nz + 2 * SUB, LANES), f32)
    return shapes, low_rows


def make_kernel(n_node, n_dev, names, low_rows):
    half = n_node // 2
    nx, nz = n_dev + 1, 2 * n_node

    def kernel(ein_hbm, diff_hbm, cst_hbm, out_ref, *scratch):
        s = dict(zip(names, scratch))
        node = lax.axis_index("node")
        dev = lax.axis_index("dev")
        sub = lax.broadcasted_iota(jnp.int32, (SUB, LANES), 0)
        lane = lax.broadcasted_iota(jnp.int32, (SUB, LANES), 1)
        has_lo, has_hi = dev > 0, dev < n_dev - 1

        s["dsrc"][...] = jnp.zeros_like(s["dsrc"])
        load_diff = pltpu.make_async_copy(
            diff_hbm, s["dsrc"].at[pl.ds(0, 2)], s["insem"].at[2]
        )
        load_in = pltpu.make_async_copy(ein_hbm, s["ein"], s["insem"].at[0])
        load_cst = pltpu.make_async_copy(cst_hbm, s["cst"], s["insem"].at[1])
        load_diff.start()
        load_in.start()
        load_cst.start()

        def const(name, index=None):
            row, size = CONSTS.at[name]
            if index is None:
                return s["cst"][row : row + size, :]
            return s["cst"][row + SUB * index : row + SUB * index + SUB, :]

        def neighbour(dx, dz):
            return (lax.rem(node + dz + n_node, n_node), lax.rem(dev + dx + n_dev, n_dev))

        sibling = (node + 1 - 2 * lax.rem(node, 2), dev)

        def same_core(k):
            return lax.rem(node + 2 * k, n_node)

        barrier = pltpu.get_barrier_semaphore()

        def greet(target):
            pl.semaphore_signal(barrier, inc=1, device_id=target, device_id_type=MESH)

        for dx, dz in DIRS:
            greet(neighbour(dx, dz))
        far = lambda k: lax.rem(dev + k, n_dev)

        def greet_far(k, _):
            greet((node, lax.rem(dev + k, n_dev)))
            return 0

        def greet_cores(k, _):
            greet((same_core(k), dev))
            return 0

        lax.fori_loop(1, n_dev, greet_far, 0)
        lax.fori_loop(1, half, greet_cores, 0)

        def wait_barrier():
            pl.semaphore_wait(barrier, n_dev - 1 + half - 1 + len(DIRS))

        def face_copy(tag, par, i):
            level = FINE if tag == "f" else MID
            dx, dz = DIRS[i]
            j = OPP[i]
            if dz == 0:
                src, dst = s["sx" + tag].at[i], s["rx" + tag].at[par, j]
            elif dx == 0:
                src, dst = s["sz" + tag].at[i - 2], s["rz" + tag].at[par, j - 2]
            else:
                a = 0 if dx < 0 else level.points - 1
                zrow = pl.ds(0 if dz < 0 else level.rows - SUB, SUB)
                src, dst = s["loc" + tag].at[a, zrow], s["rc" + tag].at[par, j - 4]
            return pltpu.make_async_remote_copy(
                src_ref=src,
                dst_ref=dst,
                send_sem=s["ssem" + tag].at[i],
                recv_sem=s["rsem" + tag].at[par, j],
                device_id=neighbour(dx, dz),
                device_id_type=MESH,
            )

        def halo_copy(i):
            return pltpu.make_async_remote_copy(
                src_ref=s["dsrc"],
                dst_ref=s["dhalo"].at[OPP[i]],
                send_sem=s["dssem"].at[i],
                recv_sem=s["drsem"].at[OPP[i]],
                device_id=neighbour(*DIRS[i]),
                device_id_type=MESH,
            )

        def start_some(make, which):
            for i in which:
                make(i).start()

        def wait_some(make, which):
            for i in which:
                make(i).wait_send()
            for i in which:
                make(i).wait_recv()

        X_DIRS, Z_DIRS, EDGE_DIRS = (0, 1), (2, 3), (4, 5, 6, 7)
        parity = {"f": 0, "m": 0}

        def start_faces(tag, which):
            start_some(lambda i: face_copy(tag, parity[tag], i), which)

        def pack(tag, parts):
            if tag == "f":
                return parts
            h = -(-len(parts) // 2)
            return [
                parts[i] + pltpu.roll(parts[i + h], PM, 0) if i + h < len(parts) else parts[i]
                for i in range(h)
            ]

        def unpack(tag, v, count):
            parts = [v[SUB * i : SUB * i + SUB] for i in range(v.shape[0] // SUB)]
            if tag == "f":
                return parts
            out = parts + [pltpu.roll(t, PM, 0) for t in parts]
            return [jnp.where(sub < PM, t, 0.0) for t in out[:count]]

        def put(ref, index, parts):
            for i, t in enumerate(parts):
                ref[index, SUB * i : SUB * i + SUB, :] = t

        def add_faces(tag, edges):
            level = FINE if tag == "f" else MID
            par = parity[tag]
            parity[tag] = 1 - par
            which = X_DIRS + Z_DIRS + (EDGE_DIRS if edges else ())
            wait_some(lambda i: face_copy(tag, par, i), which)
            buf, rx, rz, rc = (s[n + tag] for n in ("l", "rx", "rz", "rc"))
            last, top = level.points - 1, level.rows - SUB
            has = (has_lo, has_hi)
            for side, a in ((0, 0), (1, last)):
                for z, t in enumerate(unpack(tag, rx[par, side], level.planes)):
                    t = jnp.where(has[side], t, 0.0)
                    buf[a, SUB * z : SUB * z + SUB, :] += t
            for side, row in ((0, 0), (1, top)):
                for a, t in enumerate(unpack(tag, rz[par, side], level.points)):
                    buf[a, row : row + SUB, :] += t
            if edges:
                for k, (a, row) in enumerate(((0, 0), (0, top), (last, 0), (last, top))):
                    t = jnp.where(has[0 if a == 0 else 1], rc[par, k], 0.0)
                    buf[a, row : row + SUB, :] += t

        def sum_y(tag, a, first=0, count=None):
            level = FINE if tag == "f" else MID
            n = level.planes if count is None else count
            buf = s["l" + tag]
            rows_lo = pl.ds(SUB * first, n, stride=SUB)
            rows_hi = pl.ds(SUB * first + level.points - 1, n, stride=SUB)
            lo, hi = buf[a, rows_lo, :], buf[a, rows_hi, :]
            at = lax.broadcasted_iota(jnp.int32, (n, LANES), 1)
            buf[a, rows_lo, :] = lo + jnp.where(at > 0, pltpu.roll(hi, 1, 1), 0.0)
            buf[a, rows_hi, :] = hi + jnp.where(
                at < LANES - 1, pltpu.roll(lo, LANES - 1, 1), 0.0
            )

        def sum_y_planes(tag, row):
            p = (FINE if tag == "f" else MID).points
            sel = (slice(1, p - 1), slice(row, row + SUB))
            t = s["l" + tag][sel]
            up = pltpu.roll(pltpu.roll(t, 1, 2), SUB - p + 1, 1)
            down = pltpu.roll(pltpu.roll(t, LANES - 1, 2), p - 1, 1)
            t = t + jnp.where((sub == 0) & (lane > 0), up, 0.0)
            t = t + jnp.where((sub == p - 1) & (lane < LANES - 1), down, 0.0)
            s["l" + tag][sel] = t

        def gather_a(tag, k):
            buf = s[tag + "a"]
            return pltpu.make_async_remote_copy(
                src_ref=buf.at[dev],
                dst_ref=buf.at[dev],
                send_sem=s[tag + "a_s"].at[k],
                recv_sem=s[tag + "a_r"].at[k],
                device_id=(node, far(k)),
                device_id_type=MESH,
            )

        block = {"d": 2 * n_dev, "g": low_rows}
        base = {"d": 0, "g": low_rows}

        def slot(tag, index):
            size = block[tag]
            return s[tag + "b"].at[pl.ds(pl.multiple_of(base[tag] + index * size, size), size)]

        def gather_b(tag, k):
            return pltpu.make_async_remote_copy(
                src_ref=slot(tag, node),
                dst_ref=slot(tag, node),
                send_sem=s[tag + "b_s"].at[k],
                recv_sem=s[tag + "b_r"].at[k],
                device_id=(same_core(k), dev),
                device_id_type=MESH,
            )

        def gather_c(tag, k):
            index = lax.rem(node - 2 * k + n_node, n_node)
            return pltpu.make_async_remote_copy(
                src_ref=slot(tag, index),
                dst_ref=slot(tag, index),
                send_sem=s[tag + "c_s"].at[k],
                recv_sem=s[tag + "c_r"].at[k],
                device_id=sibling,
                device_id_type=MESH,
            )

        def plane_rows(z):
            if isinstance(z, int):
                return slice(z * SUB, z * SUB + SUB)
            return pl.ds(pl.multiple_of(z * SUB, SUB), SUB)

        def each(tag, lower, upper, fn):
            if tag == "m":
                for k in range(lower, upper):
                    fn(k)
            else:
                loop(lower, upper, fn)

        def loop(lower, upper, fn):
            def step(k, _):
                fn(k)
                return 0

            lax.fori_loop(lower, upper, step, 0)

        def start_a(tag):
            loop(1, n_dev, lambda k: gather_a(tag, k).start())

        def wait_a(tag):
            loop(1, n_dev, lambda k: gather_a(tag, k).wait())

        def start_b(tag):
            loop(1, half, lambda k: gather_b(tag, k).start())
            gather_c(tag, 0).start()

        def forward_b(tag):
            def one(k):
                gather_b(tag, k).wait_recv()
                gather_c(tag, k).start()

            loop(1, half, one)

        def wait_b(tag):
            loop(1, half, lambda k: gather_b(tag, k).wait_send())
            loop(0, half, lambda k: gather_c(tag, k).wait())

        def along_y(tag, v):
            p = (FINE if tag == "f" else MID).points
            acc = const("ky" + tag, 0) * v
            for shift in range(1, SUB):
                if p == PF or shift < p or shift > SUB - p:
                    acc = acc + const("ky" + tag, shift) * pltpu.roll(v, shift, 1)
            return acc

        def along_z(tag, v):
            level = FINE if tag == "f" else MID
            n, p = level.planes, level.points
            parts = [v[SUB * i : SUB * i + SUB] for i in range(n)]
            low = mix_even_odd(level.khat, parts[:p])
            high = mix_even_odd(level.khat, parts[p - 1 :])
            first = s["dz" + tag][0:SUB, :]
            second = s["dz" + tag][level.rows - SUB : level.rows, :]
            out = [first * t for t in low[: p - 1]]
            out.append(first * low[p - 1] + second * high[0])
            out += [second * t for t in high[1:]]
            return out, low[0], high[-1]

        def faces(tag, name):
            level = FINE if tag == "f" else MID
            n, p, top = level.planes, level.points, level.rows - SUB
            src, dst, dz = s[name + tag], s["l" + tag], s["dz" + tag]
            mass_row, _ = CONSTS.at["mz" + tag]
            has = (has_lo.astype(jnp.float32), has_hi.astype(jnp.float32))
            ends = (0, p - 1)
            even_row = 0.5 * (level.khat[0:1] + level.khat[0:1, ::-1])[:, : p // 2]
            odd_row = 0.5 * (level.khat[0:1] - level.khat[0:1, ::-1])[:, : p // 2]
            x_edge, z_edge, x_out = {}, {}, []
            chunk = 5 if tag == "f" else n
            for z0 in range(0, n, chunk):
                rows = slice(SUB * z0, SUB * (z0 + chunk))
                v = [src[a, rows, :] for a in range(p)]
                even = mix(even_row, [v[i] + v[p - 1 - i] for i in range(p // 2)])[0]
                odd = mix(odd_row, [v[i] - v[p - 1 - i] for i in range(p // 2)])[0]
                for f, xt in ((0, even + odd), (1, even - odd)):
                    if z0 == 0:
                        x_edge[f, 0] = xt[0:SUB]
                    if z0 + chunk == n:
                        x_edge[f, 1] = xt[-SUB:]
                    u = v[ends[f]]
                    yt = along_y(tag, u.reshape(chunk, SUB, LANES)).reshape(chunk * SUB, LANES)
                    mass = s["cst"][mass_row + SUB * z0 : mass_row + SUB * (z0 + chunk), :]
                    dst[ends[f], rows, :] = dz[rows, :] * (xt + yt) + mass * u
            for f, a in enumerate(ends):
                out, z_edge[f, 0], z_edge[f, 1] = along_z(tag, src[a])
                out = [t + dst[a, SUB * z : SUB * z + SUB, :] for z, t in enumerate(out)]
                put(dst, a, out)
                out[0] = out[0] + s["side"][4] * x_edge[f, 0]
                out[-1] = out[-1] + s["side"][5] * x_edge[f, 1]
                x_out.append(out)
                if tag == "f":
                    put(s["sx" + tag], f, out)
            if tag == "f":
                start_faces(tag, X_DIRS)
            for side, row in ((0, 0), (1, top)):
                rows = slice(row, row + SUB)
                v = src[:, rows, :]
                yt = along_y(tag, v)
                xt = mix_even_odd(level.khat, [v[a] for a in range(p)])
                plane0 = 0 if side == 0 else p - 1
                zt = mix(
                    level.khat[p - 1 : p] if side else level.khat[0:1],
                    [
                        src[1 : p - 1, SUB * (plane0 + c) : SUB * (plane0 + c) + SUB, :]
                        for c in range(p)
                    ],
                )[0]
                weight = dz[rows, :]
                out = [None] * p
                for a in range(1, p - 1):
                    out[a] = weight * (xt[a] + yt[a] + zt[a - 1]) + SHIFT_MASS * v[a]
                    dst[a, rows, :] = out[a]
                for f, a in enumerate(ends):
                    out[a] = (
                        dst[a, rows, :]
                        + s["side"][2 * f + side] * (z_edge[f, side] + yt[a])
                        + (SHIFT_MASS * has[f]) * v[a]
                    )
                put(s["sz" + tag], side, pack(tag, out))
            start_faces(tag, Z_DIRS)
            if tag == "m":
                for f in range(2):
                    put(s["sx" + tag], f, pack(tag, x_out[f]))
                start_faces(tag, X_DIRS)

        def interior(tag, name, after=None):
            level = FINE if tag == "f" else MID
            n, p = level.planes, level.points
            src, dst = s[name + tag], s["l" + tag]

            def plane(z):
                rows = plane_rows(z)
                v = src[:, rows, :]
                acc = along_y(tag, v[1 : p - 1])
                along_x = mix_even_odd(level.khat, [v[a] for a in range(p)])
                weight = s["dz" + tag][rows, :]
                if isinstance(z, int):
                    mass = 2.0 * SHIFT_MASS if z == p - 1 else SHIFT_MASS
                else:
                    mass = jnp.where(z == p - 1, 2.0 * SHIFT_MASS, SHIFT_MASS)
                for a in range(1, p - 1):
                    dst[a, rows, :] = weight * (acc[a - 1] + along_x[a]) + mass * v[a]

            each(tag, 1, n - 1, plane)

            def line(a):
                out, _, _ = along_z(tag, src[a])
                for i in range(1, n - 1):
                    dst[a, SUB * i : SUB * i + SUB, :] += out[i]
                if after is not None:
                    after(a)

            each(tag, 1, p - 1, line)

        def apply(tag, name):
            level = FINE if tag == "f" else MID
            n, p = level.planes, level.points
            src, dst = s[name + tag], s["l" + tag]

            def plane(z):
                rows = plane_rows(z)
                v = src[:, rows, :]
                acc = along_y(tag, v)
                along_x = mix_even_odd(level.khat, [v[a] for a in range(p)])
                weight = s["dz" + tag][rows, :]
                mass = jnp.where(z == p - 1, 2.0 * SHIFT_MASS, SHIFT_MASS)
                for a in range(p):
                    dst[a, rows, :] = weight * (acc[a] + along_x[a]) + mass * v[a]

            loop(0, n, plane)

            def line(a):
                out, _, _ = along_z(tag, src[a])
                for i in range(n):
                    dst[a, SUB * i : SUB * i + SUB, :] += out[i]

            loop(0, p, line)

        def update(tag, kind, c1=0.0, c2=0.0, last=False, residual="r"):
            level = FINE if tag == "f" else MID
            c = float(1.0 / level.theta)
            l, rhs, inv, x, r, d = (s[k + tag] for k in ("l", "rhs", "inv", "x", "r", "d"))
            old = s[residual + tag]

            def on(*sel):
                if kind == "zero":
                    res = l[sel]
                    rhs[sel] = res
                    upd = c * inv[sel] * res
                    d[sel] = upd
                    x[sel] = upd
                elif kind == "first":
                    res = rhs[sel] - l[sel]
                    r[sel] = res
                    upd = c * inv[sel] * res
                    d[sel] = upd
                    x[sel] = x[sel] + upd
                else:
                    res = old[sel] - l[sel]
                    upd = c1 * d[sel] + c2 * inv[sel] * res
                    if not last:
                        r[sel] = res
                        d[sel] = upd
                    x[sel] = x[sel] + upd

            return on

        def inner_update(tag, on):
            level = FINE if tag == "f" else MID

            def one(a):
                sum_y(tag, a, 1, level.planes - 2)
                on(a, slice(SUB, level.rows - SUB))

            return one

        def face_update(tag, on, edges=False):
            level = FINE if tag == "f" else MID
            add_faces(tag, edges)
            for a in (0, level.points - 1):
                sum_y(tag, a)
                on(a, slice(0, level.rows))
            for row in (0, level.rows - SUB):
                sum_y_planes(tag, row)
                on(slice(1, level.points - 1), slice(row, row + SUB))

        def raw_round(tag, on, before_inner, before_faces):
            level = FINE if tag == "f" else MID
            buf, last, top = s["l" + tag], level.points - 1, level.rows - SUB
            start_faces(tag, EDGE_DIRS)
            for f, a in ((0, 0), (1, last)):
                put(
                    s["sx" + tag],
                    f,
                    pack(tag, [buf[a, SUB * z : SUB * z + SUB, :] for z in range(level.planes)]),
                )
            start_faces(tag, X_DIRS)
            for side, row in ((0, 0), (1, top)):
                put(
                    s["sz" + tag],
                    side,
                    pack(tag, [buf[a, row : row + SUB, :] for a in range(level.points)]),
                )
            start_faces(tag, Z_DIRS)
            before_inner()
            each(tag, 1, last, inner_update(tag, on))
            before_faces()
            face_update(tag, on, True)

        def steps(tag, count, residual, between):
            coefs = (FINE if tag == "f" else MID).steps(count)
            for index, (c1, c2) in enumerate(coefs):
                on = update(tag, "next", c1, c2, index == count - 2, residual)
                residual = "r"
                faces(tag, "d")
                interior(tag, "d", inner_update(tag, on))
                between[index]()
                face_update(tag, on)

        ones = [has_lo.astype(jnp.float32), 1.0, has_hi.astype(jnp.float32)]
        copies = [1.0 + ones[0], 1.0, 1.0 + ones[2]]
        def spread_row(row):
            return jnp.broadcast_to(row, (SUB, LANES))

        def patch(dx):
            at = lambda dz: s["dhalo"].at[DIRS.index((dx, dz))]
            mid = s["dsrc"] if dx == 0 else at(0)
            rows = [at(-1)[1:2, :], mid[0:1, :], mid[1:2, :], at(1)[0:1, :]]
            rows = [spread_row(row) for row in rows]
            if dx != 0:
                rows = [jnp.where(has_lo if dx < 0 else has_hi, row, 0.0) for row in rows]
            return rows

        def kinds_of(q):
            return [q[0] + q[1], q[1], q[1] + q[2], q[2], q[2] + q[3]]

        def kind_of(z, p):
            return {0: 0, p - 1: 2, 2 * p - 2: 4}.get(z, 1 if z < p else 3)

        def nodal(k, p):
            lo = k + jnp.where(lane > 0, pltpu.roll(k, 1, 1), 0.0)
            hi = k + jnp.where(lane < LANES - 1, pltpu.roll(k, LANES - 1, 1), 0.0)
            return jnp.where(sub == 0, lo, jnp.where(sub == p - 1, hi, k))

        def set_inverse(tag, level, a, xc, rows):
            row_k, _ = CONSTS.at["kzb" + tag]
            row_c, _ = CONSTS.at["cnt" + tag]
            kzb = s["cst"][row_k + rows.start : row_k + rows.stop, :]
            cnt = s["cst"][row_c + rows.start : row_c + rows.stop, :]
            diag = (float(level.kdiag[a]) + kzb) * s["cls" + tag][xc, rows, :]
            s["inv" + tag][a, rows, :] = 1.0 / (diag + copies[xc] * cnt)

        def diagonals_inside(levels):
            first, second = spread_row(s["dsrc"][0:1, :]), spread_row(s["dsrc"][1:2, :])
            kinds = [first, first, first + second, second, second]
            for tag, level in levels:
                p = level.points
                full = [nodal(k, p) for k in kinds]
                for z in range(level.planes):
                    rows = slice(SUB * z, SUB * z + SUB)
                    s["dz" + tag][rows, :] = kinds[kind_of(z, p)]
                    s["cls" + tag][1, rows, :] = full[kind_of(z, p)]
                for a in range(1, p - 1):
                    set_inverse(tag, level, a, 1, slice(SUB, level.rows - SUB))

        def side_diffusivity():
            q = [patch(-1), patch(0), patch(1)]
            for side in range(2):
                s["side"][side] = q[0][1 + side]
                s["side"][2 + side] = q[2][1 + side]
                s["side"][4 + side] = q[1][3 * side]

        def diagonals_faces(levels):
            q = [patch(-1), patch(0), patch(1)]
            xs = [[u + v for u, v in zip(q[0], q[1])], q[1], [u + v for u, v in zip(q[1], q[2])]]
            for xc in range(3):
                kinds = kinds_of(xs[xc])
                for tag, level in levels:
                    p = level.points
                    full = [
                        None if xc == 1 and i in (1, 2, 3) else nodal(k, p)
                        for i, k in enumerate(kinds)
                    ]
                    for z in range(level.planes):
                        value = full[kind_of(z, p)]
                        if value is not None:
                            s["cls" + tag][xc, SUB * z : SUB * z + SUB, :] = value
            for tag, level in levels:
                p, n = level.points, level.rows
                set_inverse(tag, level, 0, 0, slice(0, n))
                set_inverse(tag, level, p - 1, 2, slice(0, n))
                for a in range(1, p - 1):
                    set_inverse(tag, level, a, 1, slice(0, SUB))
                    set_inverse(tag, level, a, 1, slice(n - SUB, n))

        def restrict_fine():
            def line(a):
                res = s["locf"][a] - s["lf"][a]
                parts = [res[SUB * i : SUB * i + SUB] for i in range(FINE.planes)]
                for i, t in enumerate(mix(R73Z.T, parts)):
                    s["tmpf"][a, SUB * i : SUB * i + SUB, :] = t

            loop(0, PF, line)

            def plane(z):
                rows = plane_rows(z)
                v = s["tmpf"][:, rows, :]
                t = jnp.stack(mix(R73, [v[a] for a in range(PF)]))
                acc = const("r73", 0) * t
                for shift in range(1, SUB):
                    acc = acc + const("r73", shift) * pltpu.roll(t, shift, 1)
                s["locm"][:, rows, :] = acc
                s["lm"][:, rows, :] = acc

            each("m", 0, MID.planes, plane)

        def prolong_fine():
            def plane(z):
                rows = plane_rows(z)
                v = s["xm"][:, rows, :]
                acc = const("j73", 0) * v
                for shift in range(1, SUB):
                    acc = acc + const("j73", shift) * pltpu.roll(v, shift, 1)
                for a, t in enumerate(mix(J73, [acc[i] for i in range(PM)])):
                    s["tmpf"][a, rows, :] = t

            each("m", 0, MID.planes, plane)

            def line(a):
                v = s["tmpf"][a]
                parts = [v[SUB * i : SUB * i + SUB] for i in range(MID.planes)]
                for i, t in enumerate(mix(J73Z, parts)):
                    s["xf"][a, SUB * i : SUB * i + SUB, :] += t

            loop(0, PF, line)

        def restrict_mid():
            for a in range(PM):
                res = s["locm"][a] - s["lm"][a]
                parts = [res[SUB * i : SUB * i + SUB] for i in range(MID.planes)]
                for i, t in enumerate(mix(R31Z.T, parts)):
                    s["tmpm"][a, SUB * i : SUB * i + SUB, :] = t
            spare = jnp.zeros((SUB, LANES), jnp.float32)
            for z in range(3):
                v = s["tmpm"][:, SUB * z : SUB * z + SUB, :]
                for a, t in enumerate(mix(R31, [v[i] for i in range(PM)])):
                    acc = const("r31", 0) * t
                    for shift in (1, 5, 6, 7):
                        acc = acc + const("r31", shift) * pltpu.roll(t, shift, 0)
                    up = pltpu.roll(pltpu.roll(acc, 1, 1), SUB - 1, 0)
                    node_row = acc + jnp.where(lane > 0, up, 0.0)
                    s["ga"][dev, 3 * a + z : 3 * a + z + 1, :] = node_row[0:1, :]
                    spare = spare + jnp.where(lane == z * nx + dev + a, up[0:1, 0:1], 0.0)
            s["ga"][dev, 6:7, :] = spare[0:1, :]
            s["ga"][dev, 7:8, :] = jnp.zeros((1, LANES), jnp.float32)

        def sum_x_low():
            flat = s["ga"]
            g = jnp.zeros((low_rows, LANES), jnp.float32)
            pad = lambda rows, before: jnp.pad(
                rows, ((before, low_rows - before - rows.shape[0]), (0, 0))
            )
            mine = s["gb"].at[
                pl.ds(pl.multiple_of(low_rows + node * low_rows, low_rows), low_rows)
            ]
            mine[...] = g
            for z in range(3):
                mine[z * nx : z * nx + n_dev, :] = flat[:, z, :]
                mine[z * nx + 1 : z * nx + nx, :] += flat[:, 3 + z, :]
            mine[3 * nx : 3 * nx + 1, :] = jnp.sum(flat[:, 6, :], axis=0, keepdims=True)

        low_lane = lax.broadcasted_iota(jnp.int32, (nz, LANES), 1)
        LAST = LANES - 1

        def ahead(v):
            return jnp.where(low_lane > 0, pltpu.roll(v, 1, 1), 0.0)

        def to_end(x, v):
            return jnp.where(low_lane == x, pltpu.roll(v, x + 1, 1), 0.0)

        def low_weights():
            up_z = lambda v: pltpu.roll(v, 1, 0)
            elem = lambda x: s["db"][pl.ds(x, nz, stride=n_dev), :]
            zero = jnp.zeros((nz, LANES), jnp.float32)
            y_copies = jnp.where(low_lane > 0, 2.0, 1.0)
            end_wx = end_wy = end_wz = zero
            for x in range(nx):
                lo = elem(x - 1) if x > 0 else zero
                hi = elem(x) if x < n_dev else zero
                both = lo + hi
                wy = 0.5 * (both + up_z(both))
                wym = ahead(wy)
                wz = 0.5 * (both + ahead(both))
                wzm = up_z(wz)
                hz = hi + up_z(hi)
                wx = 0.5 * (hz + ahead(hz))
                wxm = s["c_wx"][x - 1] if x > 0 else zero
                s["c_wy"][x] = wy
                s["c_wym"][x] = wym
                s["c_wz"][x] = wz
                s["c_wzm"][x] = wzm
                s["c_wx"][x] = wx
                x_copies = 1.0 if x in (0, n_dev) else 2.0
                s["c_dg"][x] = wx + wxm + wy + wym + wz + wzm + 2.0 * SHIFT_MASS * x_copies * y_copies
                end_wx = end_wx + to_end(x, 0.5 * hz)
                end_wy = end_wy + to_end(x, wy)
                end_wz = end_wz + to_end(x, 0.5 * both)
            end_wxm, end_wzm = ahead(end_wx), up_z(end_wz)
            x_copies = jnp.where((low_lane == 0) | (low_lane == n_dev), 1.0, 2.0)
            x_copies = jnp.where(low_lane < nx, x_copies, 0.0)
            s["c_wx"][nx] = end_wx
            s["c_wxm"][...] = end_wxm
            s["c_wy"][nx] = end_wy
            s["c_wz"][nx] = end_wz
            s["c_wzm"][nx] = end_wzm
            s["c_dg"][nx] = (
                end_wx + end_wxm + end_wy + end_wz + end_wzm + 2.0 * SHIFT_MASS * x_copies
            )

        def low_rhs():
            buf = s["gb"]
            buf[0:low_rows, :] = buf[n_node * low_rows : (n_node + 1) * low_rows, :]
            own = lambda row: buf[pl.ds(low_rows + row, n_node, stride=low_rows), :]
            before = lambda row: buf[pl.ds(row, n_node, stride=low_rows), :]
            at = lax.broadcasted_iota(jnp.int32, (n_node, LANES), 1)
            spare, spare_before = own(3 * nx), before(3 * nx)

            def pick(rows, first):
                moved = rows if first == 0 else pltpu.roll(rows, LANES - first, 1)
                return jnp.where(at < nx, moved, 0.0)

            even, odd = pl.ds(0, n_node, stride=2), pl.ds(1, n_node, stride=2)
            res, main = s["c_cr"], s["c_main"]
            for x in range(nx):
                main[even, :] = own(x) + before(2 * nx + x)
                main[odd, :] = own(nx + x)
                res[x] = main[...]
            main[even, :] = pick(spare, 0) + pick(spare_before, 2 * nx)
            main[odd, :] = pick(spare, nx)
            res[nx] = main[...]

        def fold(v):
            parts = [v[i : i + SUB] for i in range(0, v.shape[0], SUB)]
            while len(parts) > 1:
                parts = [u + w for u, w in zip(parts[::2], parts[1::2])] + (
                    [parts[-1]] if len(parts) % 2 else []
                )
            return parts[0]

        def total(v):
            return jnp.sum(v, axis=(0, 1), keepdims=True)

        def set_direction(x, value):
            p = s["c_p"]
            p[x, SUB : SUB + nz, :] = value
            p[x, 0:SUB, :] = value[nz - SUB : nz]
            p[x, SUB + nz : 2 * SUB + nz, :] = value[0:SUB]

        def coarse_solve():
            p, q, res, sol = s["c_p"], s["c_cq"], s["c_cr"], s["c_cx"]
            here = pl.ds(SUB, nz)
            norm = jnp.zeros((SUB, LANES), jnp.float32)
            for x in range(nx + 1):
                v = res[x]
                set_direction(x, v)
                sol[x] = jnp.zeros_like(v)
                norm = norm + fold(v * v)

            def along_pipe(x):
                out = s["c_wz"][x] * p[x, SUB + 1 : SUB + 1 + nz, :]
                return out + s["c_wzm"][x] * p[x, SUB - 1 : SUB - 1 + nz, :]

            def iteration(_, now):
                dot = jnp.zeros((SUB, LANES), jnp.float32)
                end = p[nx, here, :]
                last = jnp.zeros((nz, LANES), jnp.float32)
                for x in range(nx):
                    v = p[x, here, :]
                    out = s["c_dg"][x] * v
                    if x > 0:
                        out = out - s["c_wx"][x - 1] * p[x - 1, here, :]
                    if x < nx - 1:
                        out = out - s["c_wx"][x] * p[x + 1, here, :]
                    above = jnp.where(
                        low_lane == LAST, pltpu.roll(end, LAST - x, 1), pltpu.roll(v, LAST, 1)
                    )
                    below = pltpu.roll(v, 1, 1)
                    out = out - s["c_wy"][x] * above - s["c_wym"][x] * below
                    out = out - along_pipe(x)
                    q[x] = out
                    dot = dot + fold(v * out)
                    last = jnp.where(low_lane == x, pltpu.roll(v, x + 1, 1), last)
                out = s["c_dg"][nx] * end - s["c_wx"][nx] * pltpu.roll(end, LAST, 1)
                out = out - s["c_wxm"][...] * pltpu.roll(end, 1, 1)
                out = out - s["c_wy"][nx] * last - along_pipe(nx)
                q[nx] = out
                dot = dot + fold(end * out)
                alpha = now / total(dot)
                norm = jnp.zeros((SUB, LANES), jnp.float32)
                for x in range(nx + 1):
                    sol[x] += alpha * p[x, here, :]
                    v = res[x] - alpha * q[x]
                    res[x] = v
                    norm = norm + fold(v * v)
                new = total(norm)
                beta = new / now
                for x in range(nx + 1):
                    set_direction(x, res[x] + beta * p[x, here, :])
                return new

            lax.fori_loop(0, COARSE_ITERS, iteration, total(norm))

        def add_low():
            p, n = PM, MID.planes
            h = float((MID.khat @ J31)[0, 0])
            spread = {}
            for i in range(4):
                for k in range(5):
                    if i in (0, 3) and k in (0, 4):
                        continue
                    x = jnp.clip(dev + i - 1, 0, n_dev)
                    z = lax.rem(2 * node + k - 1 + nz, nz)
                    low = spread_row(s["c_cx"][x, pl.ds(z, 1), :])
                    end = pltpu.roll(spread_row(s["c_cx"][nx, pl.ds(z, 1), :]), LAST - x, 1)
                    high = jnp.where(lane < LAST, pltpu.roll(low, LAST, 1), end)
                    spread[i, k] = const("j31", 0) * low + const("j31", 1) * high
            left = mix(J31Z, [spread[0, k] for k in (1, 2, 3)])
            right = mix(J31Z, [spread[3, k] for k in (1, 2, 3)])
            inner = [
                mix(J31, [spread[1, k], spread[2, k]]) for k in range(5)
            ]
            q = [patch(-1), patch(0), patch(1)]
            xs = [[u + v for u, v in zip(q[0], q[1])], q[1], [u + v for u, v in zip(q[1], q[2])]]
            along_x = [kinds_of(v) for v in q]
            lines = [mix(J31Z, [inner[k][a] for k in (1, 2, 3)]) for a in range(p)]
            for a in range(p):
                xc = 0 if a == 0 else 2 if a == p - 1 else 1
                w, u = xs[xc], lines[a]
                kinds = kinds_of(w)
                ends = (0, p - 1, n - 1)
                slope = [u[0] - inner[0][a], u[p - 1] - u[0], u[n - 1] - u[p - 1], inner[4][a] - u[n - 1]]
                flow = [v * t for v, t in zip(w, slope)]
                for z in range(n):
                    rows = slice(SUB * z, SUB * z + SUB)
                    kind = kind_of(z, p)
                    copies_z = 2.0 if z in ends else 1.0
                    out = kinds[kind] * along_y("m", u[z][None])[0]
                    out = out + (SHIFT_MASS * copies_z * copies[xc]) * u[z]
                    if z in ends:
                        k = ends.index(z)
                        out = out + h * (flow[k] - flow[k + 1])
                    if a == 0:
                        out = out + h * (
                            along_x[0][kind] * (u[z] - left[z])
                            + along_x[1][kind] * (u[z] - lines[p - 1][z])
                        )
                    if a == p - 1:
                        out = out + h * (
                            along_x[1][kind] * (u[z] - lines[0][z])
                            + along_x[2][kind] * (u[z] - right[z])
                        )
                    s["lm"][a, rows, :] += out
                    s["xm"][a, rows, :] += u[z]

        nothing = lambda: None
        load_diff.wait()
        s["da"][dev] = s["dsrc"][...]
        load_cst.wait()
        load_in.wait()
        wz = np.concatenate([FINE.w, FINE.w[1:]])

        def load_line(a):
            planes = []
            for e in range(2):
                for c in range(PF):
                    start = a * (PF * PF * 2) + 2 * c + e
                    planes.append(s["ein"][pl.ds(start, SUB, stride=2 * PF), :])
            merged = planes[: PF - 1] + [planes[PF - 1] + planes[PF]] + planes[PF + 1 :]
            scale = const("iwb") * wa_inverse(a)
            for z, v in enumerate(merged):
                t = scale * v * float(1.0 / wz[z])
                s["locf"][a, SUB * z : SUB * z + SUB, :] = t
                s["lf"][a, SUB * z : SUB * z + SUB, :] = t

        def wa_inverse(a):
            value = jnp.float32(1.0 / FINE.w[0])
            for i in range(1, PF // 2):
                value = jnp.where((a == i) | (a == PF - 1 - i), 1.0 / FINE.w[i], value)
            return value

        loop(0, PF, load_line)
        wait_barrier()
        start_some(halo_copy, range(8))

        def halo_done():
            start_a("d")
            wait_some(halo_copy, range(8))
            diagonals_faces([("f", FINE)])

        def diff_stage_b():
            diagonals_inside([("m", MID)])
            diagonals_faces([("m", MID)])
            wait_a("d")
            mine = slot("d", node)
            for e in range(2):
                mine[e * n_dev : (e + 1) * n_dev, :] = s["da"][:, e, :]
            start_b("d")

        raw_round("f", update("f", "zero"), lambda: diagonals_inside([("f", FINE)]), halo_done)
        side_diffusivity()
        steps("f", SMOOTH_FINE, "rhs", [diff_stage_b, lambda: forward_b("d")])
        apply("f", "x")
        restrict_fine()

        def weights():
            wait_b("d")
            low_weights()

        raw_round("m", update("m", "zero"), nothing, weights)
        steps("m", SMOOTH_MID, "rhs", [nothing, nothing])
        faces("m", "x")
        interior("m", "x")
        restrict_mid()
        start_a("g")
        add_faces("m", False)
        wait_a("g")
        sum_x_low()
        start_b("g")
        forward_b("g")
        wait_b("g")
        low_rhs()
        coarse_solve()
        add_low()
        first = update("m", "first")

        def first_mid(a):
            sum_y("m", a)
            first(a, slice(0, MID.rows))

        each("m", 0, PM, first_mid)
        steps("m", SMOOTH_MID, "r", [nothing, nothing])
        prolong_fine()
        first = update("f", "first")
        faces("f", "x")
        interior("f", "x", inner_update("f", first))
        face_update("f", first)
        steps("f", SMOOTH_FINE, "r", [nothing, nothing])

        chunk = PF * PF * 2

        def store_line(a):
            for e in range(2):
                for c in range(PF):
                    z = e * (PF - 1) + c
                    start = a * chunk + 2 * c + e
                    out_ref[pl.ds(start, SUB, stride=2 * PF), :] = s["xf"][
                        a, SUB * z : SUB * z + SUB, :
                    ]

        loop(0, PF, store_line)

    return kernel


def solution(mesh):
    n_node, n_dev = mesh.shape["node"], mesh.shape["dev"]
    shapes, low_rows = scratch_shapes(n_node, n_dev)
    kernel = make_kernel(n_node, n_dev, list(shapes), low_rows)
    rows = PF * PF * PF * 2

    def local(element_load, diffusivity):
        out = pl.pallas_call(
            kernel,
            out_shape=pltpu.VMEM((rows, LANES), jnp.float32),
            in_specs=[pl.BlockSpec(memory_space=pltpu.HBM)] * 3,
            out_specs=pl.BlockSpec(memory_space=pltpu.VMEM),
            scratch_shapes=list(shapes.values()),
            compiler_params=pltpu.CompilerParams(
                collective_id=0, has_side_effects=True, vmem_limit_bytes=48 * 1024 * 1024
            ),
        )(
            pltpu.with_memory_space_constraint(element_load.reshape(rows, LANES), pltpu.HBM),
            pltpu.with_memory_space_constraint(diffusivity.reshape(2, LANES), pltpu.HBM),
            pltpu.with_memory_space_constraint(jnp.asarray(CONSTS.array()), pltpu.HBM),
        )
        return out.reshape(element_load.shape)

    return jax.shard_map(
        local,
        mesh=mesh,
        in_specs=(P(None, None, None, "dev", "node", None), P("dev", "node", None)),
        out_specs=P(None, None, None, "dev", "node", None),
        check_vma=False,
    )
```

```python
import jax
import jax.numpy as jnp
import numpy as np
from jax import lax
from jax.experimental import pallas as pl
from jax.experimental.pallas import tpu as pltpu
from jax.sharding import PartitionSpec as P

PF = 8
PM = 4
PC = 2
SMOOTH_FINE = 3
SMOOTH_MID = 3
COARSE_ITERS = 5
SHIFT_MASS = 0.05
LANES = 128
SUB = 8
MESH = pl.DeviceIdType.MESH

def legendre_values(points, poly_order):
    columns = [points * 0.0 + 1.0, points]
    for degree in range(2, poly_order + 1):
        columns.append(
            ((2 * degree - 1) * points * columns[degree - 1] - (degree - 1) * columns[degree - 2])
            / degree
        )
    return np.stack(columns[: poly_order + 1], axis=1)


def largest_eigen(matrix):
    size_n = matrix.shape[0]
    vector = np.cos(2.7 * np.arange(size_n) + 0.3)
    for power_step in range(4000):
        vector = matrix @ vector
        vector = vector / np.sqrt(np.sum(vector * vector))
    return float(vector @ (matrix @ vector))


def gll_level(poly_order):
    point_count = poly_order + 1
    gll_nodes = np.cos(np.pi * np.arange(point_count) / poly_order)
    for newton_step in range(60):
        values = legendre_values(gll_nodes, poly_order)
        gll_nodes = gll_nodes - (gll_nodes * values[:, poly_order] - values[:, poly_order - 1]) / (
            point_count * values[:, poly_order]
        )
    gll_nodes = np.sort(gll_nodes)
    values = legendre_values(gll_nodes, poly_order)
    top_value = values[:, poly_order]
    weights = 2.0 / (poly_order * point_count * top_value**2)
    deriv_matrix = np.zeros((point_count, point_count))
    for row_index in range(point_count):
        for col_index in range(point_count):
            if row_index != col_index:
                deriv_matrix[row_index, col_index] = top_value[row_index] / (
                    top_value[col_index] * (gll_nodes[row_index] - gll_nodes[col_index])
                )
    deriv_matrix[0, 0] = -poly_order * point_count / 4.0
    deriv_matrix[poly_order, poly_order] = poly_order * point_count / 4.0
    stiffness = deriv_matrix.T @ (weights[:, None] * deriv_matrix)
    diag_ids = np.arange(point_count)
    stiff_diag = stiffness[diag_ids, diag_ids]
    diag_scale = 1.0 / np.sqrt(stiff_diag)
    eig_bound = largest_eigen(diag_scale[:, None] * stiffness * diag_scale[None, :])
    return (gll_nodes, weights, deriv_matrix, stiff_diag, eig_bound)


def interp_table(fine_nodes, coarse_nodes):
    interp_mat = np.ones((fine_nodes.shape[0], coarse_nodes.shape[0]))
    for col_index in range(coarse_nodes.shape[0]):
        for other_index in range(coarse_nodes.shape[0]):
            if other_index != col_index:
                interp_mat[:, col_index] *= (fine_nodes - coarse_nodes[other_index]) / (
                    coarse_nodes[col_index] - coarse_nodes[other_index]
                )
    return interp_mat


class Level:
    def __init__(self, points):
        nodes, w, deriv, stiff_diag, bound = gll_level(points - 1)
        self.points = points
        self.planes = 2 * points - 1
        self.rows = SUB * self.planes
        self.x_rows = SUB * (self.planes if points == SUB else -(-self.planes // 2))
        self.z_rows = SUB * (points if points == SUB else -(-points // 2))
        self.nodes = nodes
        self.w = w
        self.khat = (deriv.T @ (w[:, None] * deriv)) / w[:, None]
        self.kdiag = stiff_diag / w
        self.theta = 0.6 * bound
        self.delta = 0.5 * bound

    def steps(self, count):
        sig = self.theta / self.delta
        rho = 1.0 / sig
        out = []
        for _ in range(count - 1):
            rho_next = 1.0 / (2.0 * sig - rho)
            out.append((float(rho_next * rho), float(2.0 * rho_next / self.delta)))
            rho = rho_next
        return out


def roll_coefs(matrix):
    full = np.zeros((SUB, SUB))
    full[: matrix.shape[0], : matrix.shape[1]] = matrix
    i = np.arange(SUB)
    return [full[i, (i - s) % SUB] for s in range(SUB)]


def two_elements(matrix):
    n, m = matrix.shape
    out = np.zeros((2 * n - 1, 2 * m - 1))
    out[:n, :m] = matrix
    out[n - 1 :, m - 1 :] = matrix
    return out


def plane_sum(points):
    values = np.zeros((2 * points - 1,))
    values[:points] += 1
    values[points - 1 :] += 1
    return values


class Consts:
    def __init__(self):
        self.blocks = []
        self.at = {}
        self.row = 0

    def add(self, name, block):
        block = np.asarray(block, np.float64)
        if block.ndim == 1:
            block = np.broadcast_to(block[:, None], (block.shape[0], LANES))
        assert block.shape[0] % SUB == 0
        self.at[name] = (self.row, block.shape[0])
        self.blocks.append(block)
        self.row += block.shape[0]

    def array(self):
        return np.concatenate(self.blocks, 0).astype(np.float32)


FINE, MID, LOW = Level(PF), Level(PM), Level(PC)
J73 = interp_table(FINE.nodes, MID.nodes)
J31 = interp_table(MID.nodes, LOW.nodes)
R73 = (FINE.w[:, None] * J73 / MID.w[None, :]).T
R31 = (MID.w[:, None] * J31).T
R73Z = two_elements(FINE.w[:, None] * J73 / MID.w[None, :])
R73Z[PF - 1] = 0.0
R73Z[PF - 1, PM - 1] = FINE.w[0] / MID.w[0]
R31Z = two_elements(MID.w[:, None] * J31)
R31Z[PM - 1] = 0.0
R31Z[PM - 1, PC - 1] = MID.w[0]
J73Z = two_elements(J73)
J31Z = two_elements(J31)

CONSTS = Consts()
for tag, level in (("f", FINE), ("m", MID)):
    CONSTS.add("ky" + tag, np.concatenate(roll_coefs(level.khat)))
    kb = np.zeros(SUB)
    kb[: level.points] = level.kdiag
    kz = np.concatenate([level.kdiag, level.kdiag[1:]])
    CONSTS.add("kzb" + tag, (kz[:, None] + kb[None, :]).reshape(-1))
    ey = np.arange(LANES)
    my = np.ones((SUB, LANES))
    my[0] += ey > 0
    my[level.points - 1] += ey < LANES - 1
    mz = np.ones(level.planes)
    mz[[0, level.points - 1, -1]] = 2
    CONSTS.add("cnt" + tag, (SHIFT_MASS * mz[:, None, None] * my[None]).reshape(-1, LANES))
    CONSTS.add("mz" + tag, np.repeat(SHIFT_MASS * plane_sum(level.points), SUB))
CONSTS.add("r73", np.concatenate(roll_coefs(R73)))
CONSTS.add("j73", np.concatenate(roll_coefs(J73)))
CONSTS.add("r31", np.concatenate(roll_coefs(R31)))
CONSTS.add("j31", np.concatenate([np.pad(J31[:, p], (0, SUB - PM)) for p in range(PC)]))
CONSTS.add("iwb", 1.0 / FINE.w)

DIRS = ((-1, 0), (1, 0), (0, -1), (0, 1), (-1, -1), (-1, 1), (1, -1), (1, 1))
OPP = tuple(DIRS.index((-dx, -dz)) for dx, dz in DIRS)
COEF = 1e-13


def mix(matrix, parts):
    out = []
    for row in np.asarray(matrix):
        acc = None
        for c, v in zip(row, parts):
            if abs(c) > COEF:
                term = v if abs(c - 1.0) < COEF else float(c) * v
                acc = term if acc is None else acc + term
        out.append(acc)
    return out


def mix_even_odd(matrix, parts):
    n = len(parts)
    h = n // 2
    flipped = matrix[:h, ::-1][:, :h]
    even = mix(0.5 * (matrix[:h, :h] + flipped), [parts[i] + parts[n - 1 - i] for i in range(h)])
    odd = mix(0.5 * (matrix[:h, :h] - flipped), [parts[i] - parts[n - 1 - i] for i in range(h)])
    low = [e + o for e, o in zip(even, odd)]
    high = [e - o for e, o in zip(even, odd)]
    return low + high[::-1]


def scratch_shapes(n_node, n_dev):
    f32 = jnp.float32
    low_rows = -(-(3 * (n_dev + 1) + 1) // SUB) * SUB
    shapes = {}
    for tag, level in (("f", FINE), ("m", MID)):
        p, rows = level.points, level.rows
        for name in ("loc", "rhs", "inv", "x", "r", "d", "l"):
            shapes[name + tag] = pltpu.VMEM((p, rows, LANES), f32)
        shapes["cls" + tag] = pltpu.VMEM((3, rows, LANES), f32)
        shapes["dz" + tag] = pltpu.VMEM((rows, LANES), f32)
        shapes["rx" + tag] = pltpu.VMEM((2, 2, level.x_rows, LANES), f32)
        shapes["rz" + tag] = pltpu.VMEM((2, 2, level.z_rows, LANES), f32)
        shapes["sx" + tag] = pltpu.VMEM((2, level.x_rows, LANES), f32)
        shapes["sz" + tag] = pltpu.VMEM((2, level.z_rows, LANES), f32)
        shapes["rc" + tag] = pltpu.VMEM((2, 4, SUB, LANES), f32)
        shapes["ssem" + tag] = pltpu.SemaphoreType.DMA((8,))
        shapes["rsem" + tag] = pltpu.SemaphoreType.DMA((2, 8))
    shapes["tmpf"] = pltpu.VMEM((PF, MID.rows, LANES), f32)
    shapes["tmpm"] = pltpu.VMEM((PM, LOW.rows, LANES), f32)
    shapes["ein"] = pltpu.VMEM((PF * PF * PF * 2, LANES), f32)
    shapes["cst"] = pltpu.VMEM((CONSTS.row, LANES), f32)
    shapes["insem"] = pltpu.SemaphoreType.DMA((PF + 2,))
    shapes["side"] = pltpu.VMEM((6, SUB, LANES), f32)
    shapes["dsrc"] = pltpu.VMEM((SUB, LANES), f32)
    shapes["dhalo"] = pltpu.VMEM((8, SUB, LANES), f32)
    shapes["dssem"] = pltpu.SemaphoreType.DMA((8,))
    shapes["drsem"] = pltpu.SemaphoreType.DMA((8,))
    shapes["da"] = pltpu.VMEM((n_dev, SUB, LANES), f32)
    shapes["db"] = pltpu.VMEM((n_node * 2 * n_dev, LANES), f32)
    shapes["ga"] = pltpu.VMEM((n_dev, SUB, LANES), f32)
    shapes["gb"] = pltpu.VMEM(((n_node + 1) * low_rows, LANES), f32)
    half = n_node // 2
    for tag in "dg":
        shapes[tag + "a_s"] = pltpu.SemaphoreType.DMA((n_dev,))
        shapes[tag + "a_r"] = pltpu.SemaphoreType.DMA((n_dev,))
        shapes[tag + "b_s"] = pltpu.SemaphoreType.DMA((half,))
        shapes[tag + "b_r"] = pltpu.SemaphoreType.DMA((half,))
        shapes[tag + "c_s"] = pltpu.SemaphoreType.DMA((half,))
        shapes[tag + "c_r"] = pltpu.SemaphoreType.DMA((half,))
    nx, nz = n_dev + 1, 2 * n_node
    for name in ("wx", "wy", "wym", "wz", "wzm", "dg", "cx", "cr", "cq"):
        shapes["c_" + name] = pltpu.VMEM((nx + 1, nz, LANES), f32)
    shapes["c_wxm"] = pltpu.VMEM((nz, LANES), f32)
    shapes["c_main"] = pltpu.VMEM((nz, LANES), f32)
    shapes["c_p"] = pltpu.VMEM((nx + 1, nz + 2 * SUB, LANES), f32)
    return shapes, low_rows


def make_kernel(n_node, n_dev, names, low_rows):
    half = n_node // 2
    nx, nz = n_dev + 1, 2 * n_node

    def kernel(ein_hbm, diff_hbm, cst_hbm, out_ref, *scratch):
        s = dict(zip(names, scratch))
        node = lax.axis_index("node")
        dev = lax.axis_index("dev")
        sub = lax.broadcasted_iota(jnp.int32, (SUB, LANES), 0)
        lane = lax.broadcasted_iota(jnp.int32, (SUB, LANES), 1)
        has_lo, has_hi = dev > 0, dev < n_dev - 1

        s["dsrc"][...] = jnp.zeros_like(s["dsrc"])
        chunk = PF * PF * 2
        load_diff = pltpu.make_async_copy(
            diff_hbm, s["dsrc"].at[pl.ds(0, 2)], s["insem"].at[PF + 1]
        )
        load_cst = pltpu.make_async_copy(cst_hbm, s["cst"], s["insem"].at[PF])

        def load_in(a):
            rows = pl.ds(a * chunk, chunk)
            return pltpu.make_async_copy(ein_hbm.at[rows], s["ein"].at[rows], s["insem"].at[a])

        load_diff.start()
        for a in (0, PF - 1) + tuple(range(1, PF - 1)):
            load_in(a).start()
        load_cst.start()

        def const(name, index=None):
            row, size = CONSTS.at[name]
            if index is None:
                return s["cst"][row : row + size, :]
            return s["cst"][row + SUB * index : row + SUB * index + SUB, :]

        def neighbour(dx, dz):
            return (lax.rem(node + dz + n_node, n_node), lax.rem(dev + dx + n_dev, n_dev))

        sibling = (node + 1 - 2 * lax.rem(node, 2), dev)

        def same_core(k):
            return lax.rem(node + 2 * k, n_node)

        barrier = pltpu.get_barrier_semaphore()

        def greet(target):
            pl.semaphore_signal(barrier, inc=1, device_id=target, device_id_type=MESH)

        for dx, dz in DIRS:
            greet(neighbour(dx, dz))
        far = lambda k: lax.rem(dev + k, n_dev)

        def greet_far(k, _):
            greet((node, lax.rem(dev + k, n_dev)))
            return 0

        def greet_cores(k, _):
            greet((same_core(k), dev))
            return 0

        lax.fori_loop(1, n_dev, greet_far, 0)
        lax.fori_loop(1, half, greet_cores, 0)

        def wait_barrier():
            pl.semaphore_wait(barrier, n_dev - 1 + half - 1 + len(DIRS))

        def face_copy(tag, par, i):
            level = FINE if tag == "f" else MID
            dx, dz = DIRS[i]
            j = OPP[i]
            if dz == 0:
                src, dst = s["sx" + tag].at[i], s["rx" + tag].at[par, j]
            elif dx == 0:
                src, dst = s["sz" + tag].at[i - 2], s["rz" + tag].at[par, j - 2]
            else:
                a = 0 if dx < 0 else level.points - 1
                zrow = pl.ds(0 if dz < 0 else level.rows - SUB, SUB)
                src, dst = s["loc" + tag].at[a, zrow], s["rc" + tag].at[par, j - 4]
            return pltpu.make_async_remote_copy(
                src_ref=src,
                dst_ref=dst,
                send_sem=s["ssem" + tag].at[i],
                recv_sem=s["rsem" + tag].at[par, j],
                device_id=neighbour(dx, dz),
                device_id_type=MESH,
            )

        def halo_copy(i):
            return pltpu.make_async_remote_copy(
                src_ref=s["dsrc"],
                dst_ref=s["dhalo"].at[OPP[i]],
                send_sem=s["dssem"].at[i],
                recv_sem=s["drsem"].at[OPP[i]],
                device_id=neighbour(*DIRS[i]),
                device_id_type=MESH,
            )

        def start_some(make, which):
            for i in which:
                make(i).start()

        def wait_some(make, which):
            for i in which:
                make(i).wait_send()
            for i in which:
                make(i).wait_recv()

        X_DIRS, Z_DIRS, EDGE_DIRS = (0, 1), (2, 3), (4, 5, 6, 7)
        parity = {"f": 0, "m": 0}

        def start_faces(tag, which):
            start_some(lambda i: face_copy(tag, parity[tag], i), which)

        def pack(tag, parts):
            if tag == "f":
                return parts
            h = -(-len(parts) // 2)
            return [
                parts[i] + pltpu.roll(parts[i + h], PM, 0) if i + h < len(parts) else parts[i]
                for i in range(h)
            ]

        def unpack(tag, v, count):
            parts = [v[SUB * i : SUB * i + SUB] for i in range(v.shape[0] // SUB)]
            if tag == "f":
                return parts
            out = parts + [pltpu.roll(t, PM, 0) for t in parts]
            return [jnp.where(sub < PM, t, 0.0) for t in out[:count]]

        def put(ref, index, parts):
            for i, t in enumerate(parts):
                ref[index, SUB * i : SUB * i + SUB, :] = t

        def add_faces(tag):
            level = FINE if tag == "f" else MID
            par = parity[tag]
            parity[tag] = 1 - par
            wait_some(lambda i: face_copy(tag, par, i), X_DIRS + Z_DIRS)
            buf, rx, rz = (s[n + tag] for n in ("l", "rx", "rz"))
            last, top = level.points - 1, level.rows - SUB
            has = (has_lo, has_hi)
            for side, a in ((0, 0), (1, last)):
                for z, t in enumerate(unpack(tag, rx[par, side], level.planes)):
                    t = jnp.where(has[side], t, 0.0)
                    buf[a, SUB * z : SUB * z + SUB, :] += t
            for side, row in ((0, 0), (1, top)):
                for a, t in enumerate(unpack(tag, rz[par, side], level.points)):
                    buf[a, row : row + SUB, :] += t
            return par

        def sum_y(tag, a, first=0, count=None):
            level = FINE if tag == "f" else MID
            n = level.planes if count is None else count
            buf = s["l" + tag]
            rows_lo = pl.ds(SUB * first, n, stride=SUB)
            rows_hi = pl.ds(SUB * first + level.points - 1, n, stride=SUB)
            lo, hi = buf[a, rows_lo, :], buf[a, rows_hi, :]
            at = lax.broadcasted_iota(jnp.int32, (n, LANES), 1)
            buf[a, rows_lo, :] = lo + jnp.where(at > 0, pltpu.roll(hi, 1, 1), 0.0)
            buf[a, rows_hi, :] = hi + jnp.where(
                at < LANES - 1, pltpu.roll(lo, LANES - 1, 1), 0.0
            )

        def sum_y_planes(tag, row, which):
            p = (FINE if tag == "f" else MID).points
            sel = (which, slice(row, row + SUB))
            t = s["l" + tag][sel]
            across, along = t.ndim - 1, t.ndim - 2
            up = pltpu.roll(t, 1, across)
            down = pltpu.roll(t, LANES - 1, across)
            up = pltpu.roll(up, SUB - p + 1, along)
            down = pltpu.roll(down, p - 1, along)
            t = t + jnp.where((sub == 0) & (lane > 0), up, 0.0)
            t = t + jnp.where((sub == p - 1) & (lane < LANES - 1), down, 0.0)
            s["l" + tag][sel] = t

        def gather_a(tag, k):
            buf = s[tag + "a"]
            return pltpu.make_async_remote_copy(
                src_ref=buf.at[dev],
                dst_ref=buf.at[dev],
                send_sem=s[tag + "a_s"].at[k],
                recv_sem=s[tag + "a_r"].at[k],
                device_id=(node, far(k)),
                device_id_type=MESH,
            )

        block = {"d": 2 * n_dev, "g": low_rows}
        base = {"d": 0, "g": low_rows}

        def slot(tag, index):
            size = block[tag]
            return s[tag + "b"].at[pl.ds(pl.multiple_of(base[tag] + index * size, size), size)]

        def gather_b(tag, k):
            return pltpu.make_async_remote_copy(
                src_ref=slot(tag, node),
                dst_ref=slot(tag, node),
                send_sem=s[tag + "b_s"].at[k],
                recv_sem=s[tag + "b_r"].at[k],
                device_id=(same_core(k), dev),
                device_id_type=MESH,
            )

        def gather_c(tag, k):
            index = lax.rem(node - 2 * k + n_node, n_node)
            return pltpu.make_async_remote_copy(
                src_ref=slot(tag, index),
                dst_ref=slot(tag, index),
                send_sem=s[tag + "c_s"].at[k],
                recv_sem=s[tag + "c_r"].at[k],
                device_id=sibling,
                device_id_type=MESH,
            )

        def plane_rows(z):
            if isinstance(z, int):
                return slice(z * SUB, z * SUB + SUB)
            return pl.ds(pl.multiple_of(z * SUB, SUB), SUB)

        def each(tag, lower, upper, fn):
            if tag == "m":
                for k in range(lower, upper):
                    fn(k)
            else:
                loop(lower, upper, fn)

        def loop(lower, upper, fn):
            def step(k, _):
                fn(k)
                return 0

            lax.fori_loop(lower, upper, step, 0)

        def start_a(tag):
            loop(1, n_dev, lambda k: gather_a(tag, k).start())

        def wait_a(tag):
            loop(1, n_dev, lambda k: gather_a(tag, k).wait())

        def start_b(tag):
            loop(1, half, lambda k: gather_b(tag, k).start())
            gather_c(tag, 0).start()

        def forward_b(tag):
            def one(k):
                gather_b(tag, k).wait_recv()
                gather_c(tag, k).start()

            loop(1, half, one)

        def wait_b(tag):
            loop(1, half, lambda k: gather_b(tag, k).wait_send())
            loop(0, half, lambda k: gather_c(tag, k).wait())

        def along_y(tag, v):
            p = (FINE if tag == "f" else MID).points
            acc = const("ky" + tag, 0) * v
            for shift in range(1, SUB):
                if p == PF or shift < p or shift > SUB - p:
                    acc = acc + const("ky" + tag, shift) * pltpu.roll(v, shift, 1)
            return acc

        def along_z(tag, v):
            level = FINE if tag == "f" else MID
            n, p = level.planes, level.points
            parts = [v[SUB * i : SUB * i + SUB] for i in range(n)]
            low = mix_even_odd(level.khat, parts[:p])
            high = mix_even_odd(level.khat, parts[p - 1 :])
            first = s["dz" + tag][0:SUB, :]
            second = s["dz" + tag][level.rows - SUB : level.rows, :]
            out = [first * t for t in low[: p - 1]]
            out.append(first * low[p - 1] + second * high[0])
            out += [second * t for t in high[1:]]
            return out, low[0], high[-1]

        def faces(tag, name):
            level = FINE if tag == "f" else MID
            n, p, top = level.planes, level.points, level.rows - SUB
            src, dst, dz = s[name + tag], s["l" + tag], s["dz" + tag]
            mass_row, _ = CONSTS.at["mz" + tag]
            has = (has_lo.astype(jnp.float32), has_hi.astype(jnp.float32))
            ends = (0, p - 1)
            even_row = 0.5 * (level.khat[0:1] + level.khat[0:1, ::-1])[:, : p // 2]
            odd_row = 0.5 * (level.khat[0:1] - level.khat[0:1, ::-1])[:, : p // 2]
            x_edge, z_edge, x_out = {}, {}, []
            chunk = 5 if tag == "f" else n
            for z0 in range(0, n, chunk):
                rows = slice(SUB * z0, SUB * (z0 + chunk))
                v = [src[a, rows, :] for a in range(p)]
                even = mix(even_row, [v[i] + v[p - 1 - i] for i in range(p // 2)])[0]
                odd = mix(odd_row, [v[i] - v[p - 1 - i] for i in range(p // 2)])[0]
                for f, xt in ((0, even + odd), (1, even - odd)):
                    if z0 == 0:
                        x_edge[f, 0] = xt[0:SUB]
                    if z0 + chunk == n:
                        x_edge[f, 1] = xt[-SUB:]
                    u = v[ends[f]]
                    yt = along_y(tag, u.reshape(chunk, SUB, LANES)).reshape(chunk * SUB, LANES)
                    mass = s["cst"][mass_row + SUB * z0 : mass_row + SUB * (z0 + chunk), :]
                    dst[ends[f], rows, :] = dz[rows, :] * (xt + yt) + mass * u
            for f, a in enumerate(ends):
                out, z_edge[f, 0], z_edge[f, 1] = along_z(tag, src[a])
                out = [t + dst[a, SUB * z : SUB * z + SUB, :] for z, t in enumerate(out)]
                put(dst, a, out)
                out[0] = out[0] + s["side"][4] * x_edge[f, 0]
                out[-1] = out[-1] + s["side"][5] * x_edge[f, 1]
                x_out.append(out)
                if tag == "f":
                    put(s["sx" + tag], f, out)
            if tag == "f":
                start_faces(tag, X_DIRS)
            for side, row in ((0, 0), (1, top)):
                rows = slice(row, row + SUB)
                v = src[:, rows, :]
                yt = along_y(tag, v)
                xt = mix_even_odd(level.khat, [v[a] for a in range(p)])
                plane0 = 0 if side == 0 else p - 1
                zt = mix(
                    level.khat[p - 1 : p] if side else level.khat[0:1],
                    [
                        src[1 : p - 1, SUB * (plane0 + c) : SUB * (plane0 + c) + SUB, :]
                        for c in range(p)
                    ],
                )[0]
                weight = dz[rows, :]
                out = [None] * p
                for a in range(1, p - 1):
                    out[a] = weight * (xt[a] + yt[a] + zt[a - 1]) + SHIFT_MASS * v[a]
                    dst[a, rows, :] = out[a]
                for f, a in enumerate(ends):
                    out[a] = (
                        dst[a, rows, :]
                        + s["side"][2 * f + side] * (z_edge[f, side] + yt[a])
                        + (SHIFT_MASS * has[f]) * v[a]
                    )
                put(s["sz" + tag], side, pack(tag, out))
            start_faces(tag, Z_DIRS)
            if tag == "m":
                for f in range(2):
                    put(s["sx" + tag], f, pack(tag, x_out[f]))
                start_faces(tag, X_DIRS)

        def interior(tag, name, after=None):
            level = FINE if tag == "f" else MID
            n, p = level.planes, level.points
            src, dst = s[name + tag], s["l" + tag]

            def plane(z):
                rows = plane_rows(z)
                v = src[:, rows, :]
                acc = along_y(tag, v[1 : p - 1])
                along_x = mix_even_odd(level.khat, [v[a] for a in range(p)])
                weight = s["dz" + tag][rows, :]
                if isinstance(z, int):
                    mass = 2.0 * SHIFT_MASS if z == p - 1 else SHIFT_MASS
                else:
                    mass = jnp.where(z == p - 1, 2.0 * SHIFT_MASS, SHIFT_MASS)
                for a in range(1, p - 1):
                    dst[a, rows, :] = weight * (acc[a - 1] + along_x[a]) + mass * v[a]

            each(tag, 1, n - 1, plane)

            def line(a):
                out, _, _ = along_z(tag, src[a])
                for i in range(1, n - 1):
                    dst[a, SUB * i : SUB * i + SUB, :] += out[i]
                if after is not None:
                    after(a)

            each(tag, 1, p - 1, line)

        def apply(tag, name):
            level = FINE if tag == "f" else MID
            n, p = level.planes, level.points
            src, dst = s[name + tag], s["l" + tag]

            def plane(z):
                rows = plane_rows(z)
                v = src[:, rows, :]
                acc = along_y(tag, v)
                along_x = mix_even_odd(level.khat, [v[a] for a in range(p)])
                weight = s["dz" + tag][rows, :]
                mass = jnp.where(z == p - 1, 2.0 * SHIFT_MASS, SHIFT_MASS)
                for a in range(p):
                    dst[a, rows, :] = weight * (acc[a] + along_x[a]) + mass * v[a]

            loop(0, n, plane)

            def line(a):
                out, _, _ = along_z(tag, src[a])
                for i in range(n):
                    dst[a, SUB * i : SUB * i + SUB, :] += out[i]

            loop(0, p, line)

        def update(tag, kind, c1=0.0, c2=0.0, last=False, residual="r"):
            level = FINE if tag == "f" else MID
            c = float(1.0 / level.theta)
            l, rhs, inv, x, r, d = (s[k + tag] for k in ("l", "rhs", "inv", "x", "r", "d"))
            old = s[residual + tag]

            def on(*sel):
                if kind == "zero":
                    res = l[sel]
                    rhs[sel] = res
                    upd = c * inv[sel] * res
                    d[sel] = upd
                    x[sel] = upd
                elif kind == "first":
                    res = rhs[sel] - l[sel]
                    r[sel] = res
                    upd = c * inv[sel] * res
                    d[sel] = upd
                    x[sel] = x[sel] + upd
                else:
                    res = old[sel] - l[sel]
                    upd = c1 * d[sel] + c2 * inv[sel] * res
                    if not last:
                        r[sel] = res
                        d[sel] = upd
                    x[sel] = x[sel] + upd

            return on

        def inner_update(tag, on):
            level = FINE if tag == "f" else MID

            def one(a):
                sum_y(tag, a, 1, level.planes - 2)
                on(a, slice(SUB, level.rows - SUB))

            return one

        def face_update(tag, on):
            level = FINE if tag == "f" else MID
            add_faces(tag)
            for a in (0, level.points - 1):
                sum_y(tag, a)
                on(a, slice(0, level.rows))
            for row in (0, level.rows - SUB):
                sum_y_planes(tag, row, slice(1, level.points - 1))
                on(slice(1, level.points - 1), slice(row, row + SUB))

        def raw_start_x(tag):
            level = FINE if tag == "f" else MID
            buf = s["l" + tag]
            start_faces(tag, EDGE_DIRS)
            for f, a in ((0, 0), (1, level.points - 1)):
                parts = [buf[a, SUB * z : SUB * z + SUB, :] for z in range(level.planes)]
                put(s["sx" + tag], f, pack(tag, parts))
            start_faces(tag, X_DIRS)

        def raw_start_z(tag):
            level = FINE if tag == "f" else MID
            buf, top = s["l" + tag], level.rows - SUB
            for side, row in ((0, 0), (1, top)):
                parts = [buf[a, row : row + SUB, :] for a in range(level.points)]
                put(s["sz" + tag], side, pack(tag, parts))
            start_faces(tag, Z_DIRS)

        def raw_finish(tag, on, before_faces, before_edges):
            level = FINE if tag == "f" else MID
            buf, last, top = s["l" + tag], level.points - 1, level.rows - SUB
            each(tag, 1, last, inner_update(tag, on))
            before_faces()
            par = add_faces(tag)
            for a in (0, last):
                sum_y(tag, a, 1, level.planes - 2)
                on(a, slice(SUB, top))
            for row in (0, top):
                sum_y_planes(tag, row, slice(1, last))
                on(slice(1, last), slice(row, row + SUB))
            before_edges()
            wait_some(lambda i: face_copy(tag, par, i), EDGE_DIRS)
            for k, (a, row) in enumerate(((0, 0), (0, top), (last, 0), (last, top))):
                rows = slice(row, row + SUB)
                buf[a, rows, :] += jnp.where(has_lo if a == 0 else has_hi, s["rc" + tag][par, k], 0.0)
                sum_y_planes(tag, row, a)
                on(a, rows)

        def steps(tag, count, residual, between):
            coefs = (FINE if tag == "f" else MID).steps(count)
            for index, (c1, c2) in enumerate(coefs):
                on = update(tag, "next", c1, c2, index == count - 2, residual)
                residual = "r"
                faces(tag, "d")
                interior(tag, "d", inner_update(tag, on))
                between[index]()
                face_update(tag, on)

        ones = [has_lo.astype(jnp.float32), 1.0, has_hi.astype(jnp.float32)]
        copies = [1.0 + ones[0], 1.0, 1.0 + ones[2]]
        def spread_row(row):
            return jnp.broadcast_to(row, (SUB, LANES))

        def patch_row(dx, k):
            dz, row = ((-1, 1), (0, 0), (0, 1), (1, 0))[k]
            ref = s["dsrc"] if (dx, dz) == (0, 0) else s["dhalo"].at[DIRS.index((dx, dz))]
            value = spread_row(ref[row : row + 1, :])
            if dx != 0:
                value = jnp.where(has_lo if dx < 0 else has_hi, value, 0.0)
            return value

        def patch(dx):
            return [patch_row(dx, k) for k in range(4)]

        def kinds_of(q):
            return [q[0] + q[1], q[1], q[1] + q[2], q[2], q[2] + q[3]]

        def kind_of(z, p):
            return {0: 0, p - 1: 2, 2 * p - 2: 4}.get(z, 1 if z < p else 3)

        def nodal(k, p):
            lo = k + jnp.where(lane > 0, pltpu.roll(k, 1, 1), 0.0)
            hi = k + jnp.where(lane < LANES - 1, pltpu.roll(k, LANES - 1, 1), 0.0)
            return jnp.where(sub == 0, lo, jnp.where(sub == p - 1, hi, k))

        def set_inverse(tag, level, a, xc, rows):
            row_k, _ = CONSTS.at["kzb" + tag]
            row_c, _ = CONSTS.at["cnt" + tag]
            kzb = s["cst"][row_k + rows.start : row_k + rows.stop, :]
            cnt = s["cst"][row_c + rows.start : row_c + rows.stop, :]
            diag = (float(level.kdiag[a]) + kzb) * s["cls" + tag][xc, rows, :]
            s["inv" + tag][a, rows, :] = 1.0 / (diag + copies[xc] * cnt)

        def set_class(tag, level, xc, kind, value):
            full = nodal(value, level.points)
            for z in range(level.planes):
                if kind_of(z, level.points) == kind:
                    s["cls" + tag][xc, SUB * z : SUB * z + SUB, :] = full

        def diagonals_inside(tag, level):
            first, second = patch_row(0, 1), patch_row(0, 2)
            kinds = [first, first, first + second, second, second]
            for z in range(level.planes):
                s["dz" + tag][SUB * z : SUB * z + SUB, :] = kinds[kind_of(z, level.points)]
            for kind in (1, 2, 3):
                set_class(tag, level, 1, kind, kinds[kind])
            for a in range(1, level.points - 1):
                set_inverse(tag, level, a, 1, slice(SUB, level.rows - SUB))

        def diagonals_x(tag, level):
            for xc, dx, a in ((0, -1, 0), (2, 1, level.points - 1)):
                first = patch_row(0, 1) + patch_row(dx, 1)
                second = patch_row(0, 2) + patch_row(dx, 2)
                for kind, value in ((1, first), (2, first + second), (3, second)):
                    set_class(tag, level, xc, kind, value)
                set_inverse(tag, level, a, xc, slice(SUB, level.rows - SUB))

        def diagonals_z(tag, level):
            set_class(tag, level, 1, 0, patch_row(0, 0) + patch_row(0, 1))
            set_class(tag, level, 1, 4, patch_row(0, 2) + patch_row(0, 3))
            for a in range(1, level.points - 1):
                set_inverse(tag, level, a, 1, slice(0, SUB))
                set_inverse(tag, level, a, 1, slice(level.rows - SUB, level.rows))

        def diagonals_edges(tag, level):
            for xc, dx, a in ((0, -1, 0), (2, 1, level.points - 1)):
                q = [u + v for u, v in zip(patch(0), patch(dx))]
                set_class(tag, level, xc, 0, q[0] + q[1])
                set_class(tag, level, xc, 4, q[2] + q[3])
                set_inverse(tag, level, a, xc, slice(0, SUB))
                set_inverse(tag, level, a, xc, slice(level.rows - SUB, level.rows))

        def side_diffusivity():
            q = [patch(-1), patch(0), patch(1)]
            for side in range(2):
                s["side"][side] = q[0][1 + side]
                s["side"][2 + side] = q[2][1 + side]
                s["side"][4 + side] = q[1][3 * side]

        def restrict_fine():
            def line(a):
                res = s["locf"][a] - s["lf"][a]
                parts = [res[SUB * i : SUB * i + SUB] for i in range(FINE.planes)]
                for i, t in enumerate(mix(R73Z.T, parts)):
                    s["tmpf"][a, SUB * i : SUB * i + SUB, :] = t

            loop(0, PF, line)

            def plane(z):
                rows = plane_rows(z)
                v = s["tmpf"][:, rows, :]
                t = jnp.stack(mix(R73, [v[a] for a in range(PF)]))
                acc = const("r73", 0) * t
                for shift in range(1, SUB):
                    acc = acc + const("r73", shift) * pltpu.roll(t, shift, 1)
                s["locm"][:, rows, :] = acc
                s["lm"][:, rows, :] = acc

            each("m", 0, MID.planes, plane)

        def prolong_fine():
            def plane(z):
                rows = plane_rows(z)
                v = s["xm"][:, rows, :]
                acc = const("j73", 0) * v
                for shift in range(1, SUB):
                    acc = acc + const("j73", shift) * pltpu.roll(v, shift, 1)
                for a, t in enumerate(mix(J73, [acc[i] for i in range(PM)])):
                    s["tmpf"][a, rows, :] = t

            each("m", 0, MID.planes, plane)

            def line(a):
                v = s["tmpf"][a]
                parts = [v[SUB * i : SUB * i + SUB] for i in range(MID.planes)]
                for i, t in enumerate(mix(J73Z, parts)):
                    s["xf"][a, SUB * i : SUB * i + SUB, :] += t

            loop(0, PF, line)

        def restrict_mid():
            for a in range(PM):
                res = s["locm"][a] - s["lm"][a]
                parts = [res[SUB * i : SUB * i + SUB] for i in range(MID.planes)]
                for i, t in enumerate(mix(R31Z.T, parts)):
                    s["tmpm"][a, SUB * i : SUB * i + SUB, :] = t
            spare = jnp.zeros((SUB, LANES), jnp.float32)
            for z in range(3):
                v = s["tmpm"][:, SUB * z : SUB * z + SUB, :]
                for a, t in enumerate(mix(R31, [v[i] for i in range(PM)])):
                    acc = const("r31", 0) * t
                    for shift in (1, 5, 6, 7):
                        acc = acc + const("r31", shift) * pltpu.roll(t, shift, 0)
                    up = pltpu.roll(pltpu.roll(acc, 1, 1), SUB - 1, 0)
                    node_row = acc + jnp.where(lane > 0, up, 0.0)
                    s["ga"][dev, 3 * a + z : 3 * a + z + 1, :] = node_row[0:1, :]
                    spare = spare + jnp.where(lane == z * nx + dev + a, up[0:1, 0:1], 0.0)
            s["ga"][dev, 6:7, :] = spare[0:1, :]
            s["ga"][dev, 7:8, :] = jnp.zeros((1, LANES), jnp.float32)

        def sum_x_low():
            flat = s["ga"]
            g = jnp.zeros((low_rows, LANES), jnp.float32)
            pad = lambda rows, before: jnp.pad(
                rows, ((before, low_rows - before - rows.shape[0]), (0, 0))
            )
            mine = s["gb"].at[
                pl.ds(pl.multiple_of(low_rows + node * low_rows, low_rows), low_rows)
            ]
            mine[...] = g
            for z in range(3):
                mine[z * nx : z * nx + n_dev, :] = flat[:, z, :]
                mine[z * nx + 1 : z * nx + nx, :] += flat[:, 3 + z, :]
            mine[3 * nx : 3 * nx + 1, :] = jnp.sum(flat[:, 6, :], axis=0, keepdims=True)

        low_lane = lax.broadcasted_iota(jnp.int32, (nz, LANES), 1)
        LAST = LANES - 1

        def ahead(v):
            return jnp.where(low_lane > 0, pltpu.roll(v, 1, 1), 0.0)

        def to_end(x, v):
            return jnp.where(low_lane == x, pltpu.roll(v, x + 1, 1), 0.0)

        def low_weights():
            up_z = lambda v: pltpu.roll(v, 1, 0)
            elem = lambda x: s["db"][pl.ds(x, nz, stride=n_dev), :]
            zero = jnp.zeros((nz, LANES), jnp.float32)
            y_copies = jnp.where(low_lane > 0, 2.0, 1.0)
            end_wx = end_wy = end_wz = zero
            for x in range(nx):
                lo = elem(x - 1) if x > 0 else zero
                hi = elem(x) if x < n_dev else zero
                both = lo + hi
                wy = 0.5 * (both + up_z(both))
                wym = ahead(wy)
                wz = 0.5 * (both + ahead(both))
                wzm = up_z(wz)
                hz = hi + up_z(hi)
                wx = 0.5 * (hz + ahead(hz))
                wxm = s["c_wx"][x - 1] if x > 0 else zero
                s["c_wy"][x] = wy
                s["c_wym"][x] = wym
                s["c_wz"][x] = wz
                s["c_wzm"][x] = wzm
                s["c_wx"][x] = wx
                x_copies = 1.0 if x in (0, n_dev) else 2.0
                s["c_dg"][x] = wx + wxm + wy + wym + wz + wzm + 2.0 * SHIFT_MASS * x_copies * y_copies
                end_wx = end_wx + to_end(x, 0.5 * hz)
                end_wy = end_wy + to_end(x, wy)
                end_wz = end_wz + to_end(x, 0.5 * both)
            end_wxm, end_wzm = ahead(end_wx), up_z(end_wz)
            x_copies = jnp.where((low_lane == 0) | (low_lane == n_dev), 1.0, 2.0)
            x_copies = jnp.where(low_lane < nx, x_copies, 0.0)
            s["c_wx"][nx] = end_wx
            s["c_wxm"][...] = end_wxm
            s["c_wy"][nx] = end_wy
            s["c_wz"][nx] = end_wz
            s["c_wzm"][nx] = end_wzm
            s["c_dg"][nx] = (
                end_wx + end_wxm + end_wy + end_wz + end_wzm + 2.0 * SHIFT_MASS * x_copies
            )

        def low_rhs():
            buf = s["gb"]
            buf[0:low_rows, :] = buf[n_node * low_rows : (n_node + 1) * low_rows, :]
            own = lambda row: buf[pl.ds(low_rows + row, n_node, stride=low_rows), :]
            before = lambda row: buf[pl.ds(row, n_node, stride=low_rows), :]
            at = lax.broadcasted_iota(jnp.int32, (n_node, LANES), 1)
            spare, spare_before = own(3 * nx), before(3 * nx)

            def pick(rows, first):
                moved = rows if first == 0 else pltpu.roll(rows, LANES - first, 1)
                return jnp.where(at < nx, moved, 0.0)

            even, odd = pl.ds(0, n_node, stride=2), pl.ds(1, n_node, stride=2)
            res, main = s["c_cr"], s["c_main"]
            for x in range(nx):
                main[even, :] = own(x) + before(2 * nx + x)
                main[odd, :] = own(nx + x)
                res[x] = main[...]
            main[even, :] = pick(spare, 0) + pick(spare_before, 2 * nx)
            main[odd, :] = pick(spare, nx)
            res[nx] = main[...]

        def fold(v):
            parts = [v[i : i + SUB] for i in range(0, v.shape[0], SUB)]
            while len(parts) > 1:
                parts = [u + w for u, w in zip(parts[::2], parts[1::2])] + (
                    [parts[-1]] if len(parts) % 2 else []
                )
            return parts[0]

        def total(v):
            return jnp.sum(v, axis=(0, 1), keepdims=True)

        def set_direction(x, value):
            p = s["c_p"]
            p[x, SUB : SUB + nz, :] = value
            p[x, 0:SUB, :] = value[nz - SUB : nz]
            p[x, SUB + nz : 2 * SUB + nz, :] = value[0:SUB]

        def coarse_solve():
            p, q, res, sol = s["c_p"], s["c_cq"], s["c_cr"], s["c_cx"]
            here = pl.ds(SUB, nz)
            norm = jnp.zeros((SUB, LANES), jnp.float32)
            for x in range(nx + 1):
                v = res[x]
                set_direction(x, v)
                sol[x] = jnp.zeros_like(v)
                norm = norm + fold(v * v)

            def along_pipe(x):
                out = s["c_wz"][x] * p[x, SUB + 1 : SUB + 1 + nz, :]
                return out + s["c_wzm"][x] * p[x, SUB - 1 : SUB - 1 + nz, :]

            def step_length(now):
                dot = jnp.zeros((SUB, LANES), jnp.float32)
                end = p[nx, here, :]
                last = jnp.zeros((nz, LANES), jnp.float32)
                for x in range(nx):
                    v = p[x, here, :]
                    out = s["c_dg"][x] * v
                    if x > 0:
                        out = out - s["c_wx"][x - 1] * p[x - 1, here, :]
                    if x < nx - 1:
                        out = out - s["c_wx"][x] * p[x + 1, here, :]
                    above = jnp.where(
                        low_lane == LAST, pltpu.roll(end, LAST - x, 1), pltpu.roll(v, LAST, 1)
                    )
                    below = pltpu.roll(v, 1, 1)
                    out = out - s["c_wy"][x] * above - s["c_wym"][x] * below
                    out = out - along_pipe(x)
                    q[x] = out
                    dot = dot + fold(v * out)
                    last = jnp.where(low_lane == x, pltpu.roll(v, x + 1, 1), last)
                out = s["c_dg"][nx] * end - s["c_wx"][nx] * pltpu.roll(end, LAST, 1)
                out = out - s["c_wxm"][...] * pltpu.roll(end, 1, 1)
                out = out - s["c_wy"][nx] * last - along_pipe(nx)
                q[nx] = out
                dot = dot + fold(end * out)
                return now / total(dot)

            def iteration(_, now):
                alpha = step_length(now)
                norm = jnp.zeros((SUB, LANES), jnp.float32)
                for x in range(nx + 1):
                    sol[x] += alpha * p[x, here, :]
                    v = res[x] - alpha * q[x]
                    res[x] = v
                    norm = norm + fold(v * v)
                new = total(norm)
                beta = new / now
                for x in range(nx + 1):
                    set_direction(x, res[x] + beta * p[x, here, :])
                return new

            alpha = step_length(lax.fori_loop(0, COARSE_ITERS - 1, iteration, total(norm)))
            for x in range(nx + 1):
                sol[x] += alpha * p[x, here, :]

        def add_low():
            p, n = PM, MID.planes
            h = float((MID.khat @ J31)[0, 0])
            spread = {}
            for i in range(4):
                for k in range(5):
                    if i in (0, 3) and k in (0, 4):
                        continue
                    x = jnp.clip(dev + i - 1, 0, n_dev)
                    z = lax.rem(2 * node + k - 1 + nz, nz)
                    low = spread_row(s["c_cx"][x, pl.ds(z, 1), :])
                    end = pltpu.roll(spread_row(s["c_cx"][nx, pl.ds(z, 1), :]), LAST - x, 1)
                    high = jnp.where(lane < LAST, pltpu.roll(low, LAST, 1), end)
                    spread[i, k] = const("j31", 0) * low + const("j31", 1) * high
            left = mix(J31Z, [spread[0, k] for k in (1, 2, 3)])
            right = mix(J31Z, [spread[3, k] for k in (1, 2, 3)])
            inner = [
                mix(J31, [spread[1, k], spread[2, k]]) for k in range(5)
            ]
            q = [patch(-1), patch(0), patch(1)]
            xs = [[u + v for u, v in zip(q[0], q[1])], q[1], [u + v for u, v in zip(q[1], q[2])]]
            along_x = [kinds_of(v) for v in q]
            lines = [mix(J31Z, [inner[k][a] for k in (1, 2, 3)]) for a in range(p)]
            for a in range(p):
                xc = 0 if a == 0 else 2 if a == p - 1 else 1
                w, u = xs[xc], lines[a]
                kinds = kinds_of(w)
                ends = (0, p - 1, n - 1)
                slope = [u[0] - inner[0][a], u[p - 1] - u[0], u[n - 1] - u[p - 1], inner[4][a] - u[n - 1]]
                flow = [v * t for v, t in zip(w, slope)]
                for z in range(n):
                    rows = slice(SUB * z, SUB * z + SUB)
                    kind = kind_of(z, p)
                    copies_z = 2.0 if z in ends else 1.0
                    out = kinds[kind] * along_y("m", u[z][None])[0]
                    out = out + (SHIFT_MASS * copies_z * copies[xc]) * u[z]
                    if z in ends:
                        k = ends.index(z)
                        out = out + h * (flow[k] - flow[k + 1])
                    if a == 0:
                        out = out + h * (
                            along_x[0][kind] * (u[z] - left[z])
                            + along_x[1][kind] * (u[z] - lines[p - 1][z])
                        )
                    if a == p - 1:
                        out = out + h * (
                            along_x[1][kind] * (u[z] - lines[0][z])
                            + along_x[2][kind] * (u[z] - right[z])
                        )
                    s["lm"][a, rows, :] += out
                    s["xm"][a, rows, :] += u[z]

        nothing = lambda: None
        load_diff.wait()
        s["da"][dev] = s["dsrc"][...]
        wz = np.concatenate([FINE.w, FINE.w[1:]])

        def mirrored(index, values):
            out = jnp.float32(values[0])
            for i in range(1, PF // 2):
                out = jnp.where((index == i) | (index == PF - 1 - i), float(values[i]), out)
            return out

        across_y = mirrored(sub, 1.0 / FINE.w)

        def load_line(a):
            planes = []
            for e in range(2):
                for c in range(PF):
                    start = a * chunk + 2 * c + e
                    planes.append(s["ein"][pl.ds(start, SUB, stride=2 * PF), :])
            merged = planes[: PF - 1] + [planes[PF - 1] + planes[PF]] + planes[PF + 1 :]
            scale = across_y * mirrored(jnp.int32(a), 1.0 / FINE.w)
            for z, v in enumerate(merged):
                t = scale * v * float(1.0 / wz[z])
                s["locf"][a, SUB * z : SUB * z + SUB, :] = t
                s["lf"][a, SUB * z : SUB * z + SUB, :] = t

        for a in (0, PF - 1):
            load_in(a).wait()
            load_line(a)
        wait_barrier()
        start_some(halo_copy, range(8))
        raw_start_x("f")
        for a in range(1, PF - 1):
            load_in(a).wait()
        loop(1, PF - 1, load_line)
        raw_start_z("f")
        load_cst.wait()
        diagonals_inside("f", FINE)
        diagonals_inside("m", MID)

        def halo_sides():
            start_a("d")
            wait_some(halo_copy, X_DIRS)
            diagonals_x("f", FINE)
            wait_some(halo_copy, Z_DIRS)
            diagonals_z("f", FINE)

        def halo_edges():
            wait_some(halo_copy, EDGE_DIRS)
            diagonals_edges("f", FINE)

        def diff_stage_b():
            wait_a("d")
            mine = slot("d", node)
            for e in range(2):
                mine[e * n_dev : (e + 1) * n_dev, :] = s["da"][:, e, :]
            start_b("d")

        raw_finish("f", update("f", "zero"), halo_sides, halo_edges)
        side_diffusivity()
        steps("f", SMOOTH_FINE, "rhs", [diff_stage_b, lambda: forward_b("d")])
        apply("f", "x")
        restrict_fine()

        raw_start_x("m")
        raw_start_z("m")

        def order3_faces():
            diagonals_x("m", MID)
            diagonals_z("m", MID)
            diagonals_edges("m", MID)
            wait_b("d")

        raw_finish("m", update("m", "zero"), order3_faces, nothing)
        steps("m", SMOOTH_MID, "rhs", [low_weights, nothing])
        faces("m", "x")
        interior("m", "x")
        restrict_mid()
        start_a("g")
        add_faces("m")
        wait_a("g")
        sum_x_low()
        start_b("g")
        forward_b("g")
        wait_b("g")
        low_rhs()
        coarse_solve()
        add_low()
        first = update("m", "first")

        def first_mid(a):
            sum_y("m", a)
            first(a, slice(0, MID.rows))

        each("m", 0, PM, first_mid)
        steps("m", SMOOTH_MID, "r", [nothing, nothing])
        prolong_fine()
        first = update("f", "first")
        faces("f", "x")
        interior("f", "x", inner_update("f", first))
        face_update("f", first)
        steps("f", SMOOTH_FINE, "r", [nothing, nothing])

        def store_line(a):
            for e in range(2):
                for c in range(PF):
                    z = e * (PF - 1) + c
                    start = a * chunk + 2 * c + e
                    out_ref[pl.ds(start, SUB, stride=2 * PF), :] = s["xf"][
                        a, SUB * z : SUB * z + SUB, :
                    ]

        loop(0, PF, store_line)

    return kernel


def solution(mesh):
    n_node, n_dev = mesh.shape["node"], mesh.shape["dev"]
    shapes, low_rows = scratch_shapes(n_node, n_dev)
    kernel = make_kernel(n_node, n_dev, list(shapes), low_rows)
    rows = PF * PF * PF * 2

    def local(element_load, diffusivity):
        out = pl.pallas_call(
            kernel,
            out_shape=pltpu.VMEM((rows, LANES), jnp.float32),
            in_specs=[pl.BlockSpec(memory_space=pltpu.HBM)] * 3,
            out_specs=pl.BlockSpec(memory_space=pltpu.VMEM),
            scratch_shapes=list(shapes.values()),
            compiler_params=pltpu.CompilerParams(
                collective_id=0, has_side_effects=True, vmem_limit_bytes=48 * 1024 * 1024
            ),
        )(
            pltpu.with_memory_space_constraint(element_load.reshape(rows, LANES), pltpu.HBM),
            pltpu.with_memory_space_constraint(diffusivity.reshape(2, LANES), pltpu.HBM),
            pltpu.with_memory_space_constraint(jnp.asarray(CONSTS.array()), pltpu.HBM),
        )
        return out.reshape(element_load.shape)

    return jax.shard_map(
        local,
        mesh=mesh,
        in_specs=(P(None, None, None, "dev", "node", None), P("dev", "node", None)),
        out_specs=P(None, None, None, "dev", "node", None),
        check_vma=False,
    )
```

```python
import jax
import jax.numpy as jnp
import numpy as np
from jax import lax
from jax.experimental import pallas as pl
from jax.experimental.pallas import tpu as pltpu
from jax.sharding import PartitionSpec as P

PF = 8
PM = 4
PC = 2
SMOOTH_FINE = 3
SMOOTH_MID = 3
COARSE_ITERS = 5
SHIFT_MASS = 0.05
LANES = 128
SUB = 8
MESH = pl.DeviceIdType.MESH

def legendre_values(points, poly_order):
    columns = [points * 0.0 + 1.0, points]
    for degree in range(2, poly_order + 1):
        columns.append(
            ((2 * degree - 1) * points * columns[degree - 1] - (degree - 1) * columns[degree - 2])
            / degree
        )
    return np.stack(columns[: poly_order + 1], axis=1)


def largest_eigen(matrix):
    size_n = matrix.shape[0]
    vector = np.cos(2.7 * np.arange(size_n) + 0.3)
    for power_step in range(4000):
        vector = matrix @ vector
        vector = vector / np.sqrt(np.sum(vector * vector))
    return float(vector @ (matrix @ vector))


def gll_level(poly_order):
    point_count = poly_order + 1
    gll_nodes = np.cos(np.pi * np.arange(point_count) / poly_order)
    for newton_step in range(60):
        values = legendre_values(gll_nodes, poly_order)
        gll_nodes = gll_nodes - (gll_nodes * values[:, poly_order] - values[:, poly_order - 1]) / (
            point_count * values[:, poly_order]
        )
    gll_nodes = np.sort(gll_nodes)
    values = legendre_values(gll_nodes, poly_order)
    top_value = values[:, poly_order]
    weights = 2.0 / (poly_order * point_count * top_value**2)
    deriv_matrix = np.zeros((point_count, point_count))
    for row_index in range(point_count):
        for col_index in range(point_count):
            if row_index != col_index:
                deriv_matrix[row_index, col_index] = top_value[row_index] / (
                    top_value[col_index] * (gll_nodes[row_index] - gll_nodes[col_index])
                )
    deriv_matrix[0, 0] = -poly_order * point_count / 4.0
    deriv_matrix[poly_order, poly_order] = poly_order * point_count / 4.0
    stiffness = deriv_matrix.T @ (weights[:, None] * deriv_matrix)
    diag_ids = np.arange(point_count)
    stiff_diag = stiffness[diag_ids, diag_ids]
    diag_scale = 1.0 / np.sqrt(stiff_diag)
    eig_bound = largest_eigen(diag_scale[:, None] * stiffness * diag_scale[None, :])
    return (gll_nodes, weights, deriv_matrix, stiff_diag, eig_bound)


def interp_table(fine_nodes, coarse_nodes):
    interp_mat = np.ones((fine_nodes.shape[0], coarse_nodes.shape[0]))
    for col_index in range(coarse_nodes.shape[0]):
        for other_index in range(coarse_nodes.shape[0]):
            if other_index != col_index:
                interp_mat[:, col_index] *= (fine_nodes - coarse_nodes[other_index]) / (
                    coarse_nodes[col_index] - coarse_nodes[other_index]
                )
    return interp_mat


class Level:
    def __init__(self, points):
        nodes, w, deriv, stiff_diag, bound = gll_level(points - 1)
        self.points = points
        self.planes = 2 * points - 1
        self.rows = SUB * self.planes
        self.x_rows = SUB * (self.planes if points == SUB else -(-self.planes // 2))
        self.z_rows = SUB * (points if points == SUB else -(-points // 2))
        self.nodes = nodes
        self.w = w
        self.khat = (deriv.T @ (w[:, None] * deriv)) / w[:, None]
        self.kdiag = stiff_diag / w
        self.theta = 0.6 * bound
        self.delta = 0.5 * bound

    def steps(self, count):
        sig = self.theta / self.delta
        rho = 1.0 / sig
        out = []
        for _ in range(count - 1):
            rho_next = 1.0 / (2.0 * sig - rho)
            out.append((float(rho_next * rho), float(2.0 * rho_next / self.delta)))
            rho = rho_next
        return out


def roll_coefs(matrix):
    full = np.zeros((SUB, SUB))
    full[: matrix.shape[0], : matrix.shape[1]] = matrix
    i = np.arange(SUB)
    return [full[i, (i - s) % SUB] for s in range(SUB)]


def two_elements(matrix):
    n, m = matrix.shape
    out = np.zeros((2 * n - 1, 2 * m - 1))
    out[:n, :m] = matrix
    out[n - 1 :, m - 1 :] = matrix
    return out


def plane_sum(points):
    values = np.zeros((2 * points - 1,))
    values[:points] += 1
    values[points - 1 :] += 1
    return values


class Consts:
    def __init__(self):
        self.blocks = []
        self.at = {}
        self.row = 0

    def add(self, name, block):
        block = np.asarray(block, np.float64)
        if block.ndim == 1:
            block = np.broadcast_to(block[:, None], (block.shape[0], LANES))
        assert block.shape[0] % SUB == 0
        self.at[name] = (self.row, block.shape[0])
        self.blocks.append(block)
        self.row += block.shape[0]

    def array(self):
        return np.concatenate(self.blocks, 0).astype(np.float32)


FINE, MID, LOW = Level(PF), Level(PM), Level(PC)
J73 = interp_table(FINE.nodes, MID.nodes)
J31 = interp_table(MID.nodes, LOW.nodes)
R73 = (FINE.w[:, None] * J73 / MID.w[None, :]).T
R31 = (MID.w[:, None] * J31).T
R73Z = two_elements(FINE.w[:, None] * J73 / MID.w[None, :])
R73Z[PF - 1] = 0.0
R73Z[PF - 1, PM - 1] = FINE.w[0] / MID.w[0]
R31Z = two_elements(MID.w[:, None] * J31)
R31Z[PM - 1] = 0.0
R31Z[PM - 1, PC - 1] = MID.w[0]
J73Z = two_elements(J73)
J31Z = two_elements(J31)

CONSTS = Consts()
for tag, level in (("f", FINE), ("m", MID)):
    CONSTS.add("ky" + tag, np.concatenate(roll_coefs(level.khat)))
    kb = np.zeros(SUB)
    kb[: level.points] = level.kdiag
    kz = np.concatenate([level.kdiag, level.kdiag[1:]])
    CONSTS.add("kzb" + tag, (kz[:, None] + kb[None, :]).reshape(-1))
    ey = np.arange(LANES)
    my = np.ones((SUB, LANES))
    my[0] += ey > 0
    my[level.points - 1] += ey < LANES - 1
    mz = np.ones(level.planes)
    mz[[0, level.points - 1, -1]] = 2
    CONSTS.add("cnt" + tag, (SHIFT_MASS * mz[:, None, None] * my[None]).reshape(-1, LANES))
    CONSTS.add("mz" + tag, np.repeat(SHIFT_MASS * plane_sum(level.points), SUB))
MID_COPIES = np.ones(MID.planes)
MID_COPIES[[0, PM - 1, -1]] = 2
CONSTS.add("mzfull", np.repeat(SHIFT_MASS * MID_COPIES, SUB))
CONSTS.add("r73", np.concatenate(roll_coefs(R73)))
CONSTS.add("j73", np.concatenate(roll_coefs(J73)))
CONSTS.add("r31", np.concatenate(roll_coefs(R31)))
CONSTS.add("j31", np.concatenate([np.pad(J31[:, p], (0, SUB - PM)) for p in range(PC)]))
CONSTS.add("iwb", 1.0 / FINE.w)

DIRS = ((-1, 0), (1, 0), (0, -1), (0, 1), (-1, -1), (-1, 1), (1, -1), (1, 1))
OPP = tuple(DIRS.index((-dx, -dz)) for dx, dz in DIRS)
COEF = 1e-13


def mix(matrix, parts):
    out = []
    for row in np.asarray(matrix):
        acc = None
        for c, v in zip(row, parts):
            if abs(c) > COEF:
                term = v if abs(c - 1.0) < COEF else float(c) * v
                acc = term if acc is None else acc + term
        out.append(acc)
    return out


def mix_even_odd(matrix, parts):
    n = len(parts)
    h = n // 2
    flipped = matrix[:h, ::-1][:, :h]
    even = mix(0.5 * (matrix[:h, :h] + flipped), [parts[i] + parts[n - 1 - i] for i in range(h)])
    odd = mix(0.5 * (matrix[:h, :h] - flipped), [parts[i] - parts[n - 1 - i] for i in range(h)])
    low = [e + o for e, o in zip(even, odd)]
    high = [e - o for e, o in zip(even, odd)]
    return low + high[::-1]


def scratch_shapes(n_node, n_dev):
    f32 = jnp.float32
    low_rows = -(-(3 * (n_dev + 1) + 1) // SUB) * SUB
    shapes = {}
    for tag, level in (("f", FINE), ("m", MID)):
        p, rows = level.points, level.rows
        for name in ("loc", "rhs", "inv", "x", "r", "d", "l"):
            shapes[name + tag] = pltpu.VMEM((p, rows, LANES), f32)
        shapes["cls" + tag] = pltpu.VMEM((3, rows, LANES), f32)
        shapes["dz" + tag] = pltpu.VMEM((rows, LANES), f32)
        shapes["rx" + tag] = pltpu.VMEM((2, 2, level.x_rows, LANES), f32)
        shapes["rz" + tag] = pltpu.VMEM((2, 2, level.z_rows, LANES), f32)
        shapes["sx" + tag] = pltpu.VMEM((2, level.x_rows, LANES), f32)
        shapes["sz" + tag] = pltpu.VMEM((2, level.z_rows, LANES), f32)
        shapes["rc" + tag] = pltpu.VMEM((2, 4, SUB, LANES), f32)
        shapes["ssem" + tag] = pltpu.SemaphoreType.DMA((8,))
        shapes["rsem" + tag] = pltpu.SemaphoreType.DMA((2, 8))
    shapes["tmpf"] = pltpu.VMEM((PF, MID.rows, LANES), f32)
    shapes["tmpm"] = pltpu.VMEM((PM, LOW.rows, LANES), f32)
    shapes["ein"] = pltpu.VMEM((PF * PF * PF * 2, LANES), f32)
    shapes["cst"] = pltpu.VMEM((CONSTS.row, LANES), f32)
    shapes["insem"] = pltpu.SemaphoreType.DMA((PF + 2,))
    shapes["ghost_x"] = pltpu.VMEM((2, 3, MID.planes, SUB, LANES), f32)
    shapes["ghost_z"] = pltpu.VMEM((2, 3, PM, SUB, LANES), f32)
    shapes["side"] = pltpu.VMEM((6, SUB, LANES), f32)
    shapes["dsrc"] = pltpu.VMEM((SUB, LANES), f32)
    shapes["dhalo"] = pltpu.VMEM((8, SUB, LANES), f32)
    shapes["dssem"] = pltpu.SemaphoreType.DMA((8,))
    shapes["drsem"] = pltpu.SemaphoreType.DMA((8,))
    shapes["da"] = pltpu.VMEM((n_dev, SUB, LANES), f32)
    shapes["db"] = pltpu.VMEM((n_node * 2 * n_dev, LANES), f32)
    shapes["ga"] = pltpu.VMEM((n_dev, SUB, LANES), f32)
    shapes["gb"] = pltpu.VMEM(((n_node + 1) * low_rows, LANES), f32)
    half = n_node // 2
    for tag in "dg":
        shapes[tag + "a_s"] = pltpu.SemaphoreType.DMA((n_dev,))
        shapes[tag + "a_r"] = pltpu.SemaphoreType.DMA((n_dev,))
        shapes[tag + "b_s"] = pltpu.SemaphoreType.DMA((half,))
        shapes[tag + "b_r"] = pltpu.SemaphoreType.DMA((half,))
        shapes[tag + "c_s"] = pltpu.SemaphoreType.DMA((half,))
        shapes[tag + "c_r"] = pltpu.SemaphoreType.DMA((half,))
    nx, nz = n_dev + 1, 2 * n_node
    for name in ("wx", "wy", "wym", "wz", "wzm", "dg", "cx", "cr", "cq"):
        shapes["c_" + name] = pltpu.VMEM((nx + 1, nz, LANES), f32)
    shapes["c_wxm"] = pltpu.VMEM((nz, LANES), f32)
    shapes["c_main"] = pltpu.VMEM((nz, LANES), f32)
    shapes["c_p"] = pltpu.VMEM((nx + 1, nz + 2 * SUB, LANES), f32)
    return shapes, low_rows


def make_kernel(n_node, n_dev, names, low_rows):
    half = n_node // 2
    nx, nz = n_dev + 1, 2 * n_node

    def kernel(ein_hbm, diff_hbm, cst_hbm, out_ref, *scratch):
        s = dict(zip(names, scratch))
        node = lax.axis_index("node")
        dev = lax.axis_index("dev")
        sub = lax.broadcasted_iota(jnp.int32, (SUB, LANES), 0)
        lane = lax.broadcasted_iota(jnp.int32, (SUB, LANES), 1)
        has_lo, has_hi = dev > 0, dev < n_dev - 1

        s["dsrc"][...] = jnp.zeros_like(s["dsrc"])
        chunk = PF * PF * 2
        load_diff = pltpu.make_async_copy(
            diff_hbm, s["dsrc"].at[pl.ds(0, 2)], s["insem"].at[PF + 1]
        )
        load_cst = pltpu.make_async_copy(cst_hbm, s["cst"], s["insem"].at[PF])

        def load_in(a):
            rows = pl.ds(a * chunk, chunk)
            return pltpu.make_async_copy(ein_hbm.at[rows], s["ein"].at[rows], s["insem"].at[a])

        load_diff.start()
        for a in (0, PF - 1) + tuple(range(1, PF - 1)):
            load_in(a).start()
        load_cst.start()

        def const(name, index=None):
            row, size = CONSTS.at[name]
            if index is None:
                return s["cst"][row : row + size, :]
            return s["cst"][row + SUB * index : row + SUB * index + SUB, :]

        def neighbour(dx, dz):
            return (lax.rem(node + dz + n_node, n_node), lax.rem(dev + dx + n_dev, n_dev))

        sibling = (node + 1 - 2 * lax.rem(node, 2), dev)

        def same_core(k):
            return lax.rem(node + 2 * k, n_node)

        barrier = pltpu.get_barrier_semaphore()

        def greet(target):
            pl.semaphore_signal(barrier, inc=1, device_id=target, device_id_type=MESH)

        for dx, dz in DIRS:
            greet(neighbour(dx, dz))
        far = lambda k: lax.rem(dev + k, n_dev)

        def greet_far(k, _):
            greet((node, lax.rem(dev + k, n_dev)))
            return 0

        def greet_cores(k, _):
            greet((same_core(k), dev))
            return 0

        lax.fori_loop(1, n_dev, greet_far, 0)
        lax.fori_loop(1, half, greet_cores, 0)

        def wait_barrier():
            pl.semaphore_wait(barrier, n_dev - 1 + half - 1 + len(DIRS))

        def face_copy(tag, par, i):
            level = FINE if tag == "f" else MID
            dx, dz = DIRS[i]
            j = OPP[i]
            if dz == 0:
                src, dst = s["sx" + tag].at[i], s["rx" + tag].at[par, j]
            elif dx == 0:
                src, dst = s["sz" + tag].at[i - 2], s["rz" + tag].at[par, j - 2]
            else:
                a = 0 if dx < 0 else level.points - 1
                zrow = pl.ds(0 if dz < 0 else level.rows - SUB, SUB)
                src, dst = s["loc" + tag].at[a, zrow], s["rc" + tag].at[par, j - 4]
            return pltpu.make_async_remote_copy(
                src_ref=src,
                dst_ref=dst,
                send_sem=s["ssem" + tag].at[i],
                recv_sem=s["rsem" + tag].at[par, j],
                device_id=neighbour(dx, dz),
                device_id_type=MESH,
            )

        def halo_copy(i):
            return pltpu.make_async_remote_copy(
                src_ref=s["dsrc"],
                dst_ref=s["dhalo"].at[OPP[i]],
                send_sem=s["dssem"].at[i],
                recv_sem=s["drsem"].at[OPP[i]],
                device_id=neighbour(*DIRS[i]),
                device_id_type=MESH,
            )

        def start_some(make, which):
            for i in which:
                make(i).start()

        def wait_some(make, which):
            for i in which:
                make(i).wait_send()
            for i in which:
                make(i).wait_recv()

        X_DIRS, Z_DIRS, EDGE_DIRS = (0, 1), (2, 3), (4, 5, 6, 7)
        parity = {"f": 0, "m": 0}

        def start_faces(tag, which):
            start_some(lambda i: face_copy(tag, parity[tag], i), which)

        def pack(tag, parts):
            if tag == "f":
                return parts
            h = -(-len(parts) // 2)
            return [
                parts[i] + pltpu.roll(parts[i + h], PM, 0) if i + h < len(parts) else parts[i]
                for i in range(h)
            ]

        def unpack(tag, v, count):
            parts = [v[SUB * i : SUB * i + SUB] for i in range(v.shape[0] // SUB)]
            if tag == "f":
                return parts
            out = parts + [pltpu.roll(t, PM, 0) for t in parts]
            return [jnp.where(sub < PM, t, 0.0) for t in out[:count]]

        def put(ref, index, parts):
            for i, t in enumerate(parts):
                ref[index, SUB * i : SUB * i + SUB, :] = t

        def add_faces(tag):
            level = FINE if tag == "f" else MID
            par = parity[tag]
            parity[tag] = 1 - par
            wait_some(lambda i: face_copy(tag, par, i), X_DIRS + Z_DIRS)
            buf, rx, rz = (s[n + tag] for n in ("l", "rx", "rz"))
            last, top = level.points - 1, level.rows - SUB
            has = (has_lo, has_hi)
            for side, a in ((0, 0), (1, last)):
                for z, t in enumerate(unpack(tag, rx[par, side], level.planes)):
                    t = jnp.where(has[side], t, 0.0)
                    buf[a, SUB * z : SUB * z + SUB, :] += t
            for side, row in ((0, 0), (1, top)):
                for a, t in enumerate(unpack(tag, rz[par, side], level.points)):
                    buf[a, row : row + SUB, :] += t
            return par

        def sum_y(tag, a, first=0, count=None):
            level = FINE if tag == "f" else MID
            n = level.planes if count is None else count
            buf = s["l" + tag]
            rows_lo = pl.ds(SUB * first, n, stride=SUB)
            rows_hi = pl.ds(SUB * first + level.points - 1, n, stride=SUB)
            lo, hi = buf[a, rows_lo, :], buf[a, rows_hi, :]
            at = lax.broadcasted_iota(jnp.int32, (n, LANES), 1)
            buf[a, rows_lo, :] = lo + jnp.where(at > 0, pltpu.roll(hi, 1, 1), 0.0)
            buf[a, rows_hi, :] = hi + jnp.where(
                at < LANES - 1, pltpu.roll(lo, LANES - 1, 1), 0.0
            )

        def sum_y_planes(tag, row, which):
            p = (FINE if tag == "f" else MID).points
            sel = (which, slice(row, row + SUB))
            t = s["l" + tag][sel]
            across, along = t.ndim - 1, t.ndim - 2
            up = pltpu.roll(t, 1, across)
            down = pltpu.roll(t, LANES - 1, across)
            up = pltpu.roll(up, SUB - p + 1, along)
            down = pltpu.roll(down, p - 1, along)
            t = t + jnp.where((sub == 0) & (lane > 0), up, 0.0)
            t = t + jnp.where((sub == p - 1) & (lane < LANES - 1), down, 0.0)
            s["l" + tag][sel] = t

        def gather_a(tag, k):
            buf = s[tag + "a"]
            return pltpu.make_async_remote_copy(
                src_ref=buf.at[dev],
                dst_ref=buf.at[dev],
                send_sem=s[tag + "a_s"].at[k],
                recv_sem=s[tag + "a_r"].at[k],
                device_id=(node, far(k)),
                device_id_type=MESH,
            )

        block = {"d": 2 * n_dev, "g": low_rows}
        base = {"d": 0, "g": low_rows}

        def slot(tag, index):
            size = block[tag]
            return s[tag + "b"].at[pl.ds(pl.multiple_of(base[tag] + index * size, size), size)]

        def gather_b(tag, k):
            return pltpu.make_async_remote_copy(
                src_ref=slot(tag, node),
                dst_ref=slot(tag, node),
                send_sem=s[tag + "b_s"].at[k],
                recv_sem=s[tag + "b_r"].at[k],
                device_id=(same_core(k), dev),
                device_id_type=MESH,
            )

        def gather_c(tag, k):
            index = lax.rem(node - 2 * k + n_node, n_node)
            return pltpu.make_async_remote_copy(
                src_ref=slot(tag, index),
                dst_ref=slot(tag, index),
                send_sem=s[tag + "c_s"].at[k],
                recv_sem=s[tag + "c_r"].at[k],
                device_id=sibling,
                device_id_type=MESH,
            )

        def plane_rows(z):
            if isinstance(z, int):
                return slice(z * SUB, z * SUB + SUB)
            return pl.ds(pl.multiple_of(z * SUB, SUB), SUB)

        def each(tag, lower, upper, fn):
            if tag == "m":
                for k in range(lower, upper):
                    fn(k)
            else:
                loop(lower, upper, fn)

        def loop(lower, upper, fn):
            def step(k, _):
                fn(k)
                return 0

            lax.fori_loop(lower, upper, step, 0)

        def start_a(tag):
            loop(1, n_dev, lambda k: gather_a(tag, k).start())

        def wait_a(tag):
            loop(1, n_dev, lambda k: gather_a(tag, k).wait())

        def start_b(tag):
            loop(1, half, lambda k: gather_b(tag, k).start())
            gather_c(tag, 0).start()

        def forward_b(tag):
            def one(k):
                gather_b(tag, k).wait_recv()
                gather_c(tag, k).start()

            loop(1, half, one)

        def wait_b(tag):
            loop(1, half, lambda k: gather_b(tag, k).wait_send())
            loop(0, half, lambda k: gather_c(tag, k).wait())

        def along_y(tag, v):
            p = (FINE if tag == "f" else MID).points
            acc = const("ky" + tag, 0) * v
            for shift in range(1, SUB):
                if p == PF or shift < p or shift > SUB - p:
                    acc = acc + const("ky" + tag, shift) * pltpu.roll(v, shift, 1)
            return acc

        def along_z(tag, v):
            level = FINE if tag == "f" else MID
            n, p = level.planes, level.points
            parts = [v[SUB * i : SUB * i + SUB] for i in range(n)]
            low = mix_even_odd(level.khat, parts[:p])
            high = mix_even_odd(level.khat, parts[p - 1 :])
            first = s["dz" + tag][0:SUB, :]
            second = s["dz" + tag][level.rows - SUB : level.rows, :]
            out = [first * t for t in low[: p - 1]]
            out.append(first * low[p - 1] + second * high[0])
            out += [second * t for t in high[1:]]
            return out, low[0], high[-1]

        def faces(tag, name):
            level = FINE if tag == "f" else MID
            n, p, top = level.planes, level.points, level.rows - SUB
            src, dst, dz = s[name + tag], s["l" + tag], s["dz" + tag]
            mass_row, _ = CONSTS.at["mz" + tag]
            has = (has_lo.astype(jnp.float32), has_hi.astype(jnp.float32))
            ends = (0, p - 1)
            even_row = 0.5 * (level.khat[0:1] + level.khat[0:1, ::-1])[:, : p // 2]
            odd_row = 0.5 * (level.khat[0:1] - level.khat[0:1, ::-1])[:, : p // 2]
            x_edge, z_edge, x_out = {}, {}, []
            chunk = 5 if tag == "f" else n
            for z0 in range(0, n, chunk):
                rows = slice(SUB * z0, SUB * (z0 + chunk))
                v = [src[a, rows, :] for a in range(p)]
                even = mix(even_row, [v[i] + v[p - 1 - i] for i in range(p // 2)])[0]
                odd = mix(odd_row, [v[i] - v[p - 1 - i] for i in range(p // 2)])[0]
                for f, xt in ((0, even + odd), (1, even - odd)):
                    if z0 == 0:
                        x_edge[f, 0] = xt[0:SUB]
                    if z0 + chunk == n:
                        x_edge[f, 1] = xt[-SUB:]
                    u = v[ends[f]]
                    yt = along_y(tag, u.reshape(chunk, SUB, LANES)).reshape(chunk * SUB, LANES)
                    mass = s["cst"][mass_row + SUB * z0 : mass_row + SUB * (z0 + chunk), :]
                    dst[ends[f], rows, :] = dz[rows, :] * (xt + yt) + mass * u
            for f, a in enumerate(ends):
                out, z_edge[f, 0], z_edge[f, 1] = along_z(tag, src[a])
                out = [t + dst[a, SUB * z : SUB * z + SUB, :] for z, t in enumerate(out)]
                put(dst, a, out)
                out[0] = out[0] + s["side"][4] * x_edge[f, 0]
                out[-1] = out[-1] + s["side"][5] * x_edge[f, 1]
                x_out.append(out)
                if tag == "f":
                    put(s["sx" + tag], f, out)
            if tag == "f":
                start_faces(tag, X_DIRS)
            for side, row in ((0, 0), (1, top)):
                rows = slice(row, row + SUB)
                v = src[:, rows, :]
                yt = along_y(tag, v)
                xt = mix_even_odd(level.khat, [v[a] for a in range(p)])
                plane0 = 0 if side == 0 else p - 1
                zt = mix(
                    level.khat[p - 1 : p] if side else level.khat[0:1],
                    [
                        src[1 : p - 1, SUB * (plane0 + c) : SUB * (plane0 + c) + SUB, :]
                        for c in range(p)
                    ],
                )[0]
                weight = dz[rows, :]
                out = [None] * p
                for a in range(1, p - 1):
                    out[a] = weight * (xt[a] + yt[a] + zt[a - 1]) + SHIFT_MASS * v[a]
                    dst[a, rows, :] = out[a]
                for f, a in enumerate(ends):
                    out[a] = (
                        dst[a, rows, :]
                        + s["side"][2 * f + side] * (z_edge[f, side] + yt[a])
                        + (SHIFT_MASS * has[f]) * v[a]
                    )
                put(s["sz" + tag], side, pack(tag, out))
            start_faces(tag, Z_DIRS)
            if tag == "m":
                for f in range(2):
                    put(s["sx" + tag], f, pack(tag, x_out[f]))
                start_faces(tag, X_DIRS)

        def interior(tag, name, after=None):
            level = FINE if tag == "f" else MID
            n, p = level.planes, level.points
            src, dst = s[name + tag], s["l" + tag]

            def plane(z):
                rows = plane_rows(z)
                v = src[:, rows, :]
                acc = along_y(tag, v[1 : p - 1])
                along_x = mix_even_odd(level.khat, [v[a] for a in range(p)])
                weight = s["dz" + tag][rows, :]
                if isinstance(z, int):
                    mass = 2.0 * SHIFT_MASS if z == p - 1 else SHIFT_MASS
                else:
                    mass = jnp.where(z == p - 1, 2.0 * SHIFT_MASS, SHIFT_MASS)
                for a in range(1, p - 1):
                    dst[a, rows, :] = weight * (acc[a - 1] + along_x[a]) + mass * v[a]

            each(tag, 1, n - 1, plane)

            def line(a):
                out, _, _ = along_z(tag, src[a])
                for i in range(1, n - 1):
                    dst[a, SUB * i : SUB * i + SUB, :] += out[i]
                if after is not None:
                    after(a)

            each(tag, 1, p - 1, line)

        def apply(tag, name):
            level = FINE if tag == "f" else MID
            n, p = level.planes, level.points
            src, dst = s[name + tag], s["l" + tag]

            def plane(z):
                rows = plane_rows(z)
                v = src[:, rows, :]
                acc = along_y(tag, v)
                along_x = mix_even_odd(level.khat, [v[a] for a in range(p)])
                weight = s["dz" + tag][rows, :]
                mass = jnp.where(z == p - 1, 2.0 * SHIFT_MASS, SHIFT_MASS)
                for a in range(p):
                    dst[a, rows, :] = weight * (acc[a] + along_x[a]) + mass * v[a]

            loop(0, n, plane)

            def line(a):
                out, _, _ = along_z(tag, src[a])
                for i in range(n):
                    dst[a, SUB * i : SUB * i + SUB, :] += out[i]

            loop(0, p, line)

        def update(tag, kind, c1=0.0, c2=0.0, last=False, residual="r"):
            level = FINE if tag == "f" else MID
            c = float(1.0 / level.theta)
            l, rhs, inv, x, r, d = (s[k + tag] for k in ("l", "rhs", "inv", "x", "r", "d"))
            old = s[residual + tag]

            def on(*sel):
                if kind == "zero":
                    res = l[sel]
                    rhs[sel] = res
                    upd = c * inv[sel] * res
                    d[sel] = upd
                    x[sel] = upd
                elif kind == "first":
                    res = rhs[sel] - l[sel]
                    r[sel] = res
                    upd = c * inv[sel] * res
                    d[sel] = upd
                    x[sel] = x[sel] + upd
                else:
                    res = old[sel] - l[sel]
                    upd = c1 * d[sel] + c2 * inv[sel] * res
                    if not last:
                        r[sel] = res
                        d[sel] = upd
                    x[sel] = x[sel] + upd

            return on

        def inner_update(tag, on):
            level = FINE if tag == "f" else MID

            def one(a):
                sum_y(tag, a, 1, level.planes - 2)
                on(a, slice(SUB, level.rows - SUB))

            return one

        def face_update(tag, on):
            level = FINE if tag == "f" else MID
            add_faces(tag)
            for a in (0, level.points - 1):
                sum_y(tag, a)
                on(a, slice(0, level.rows))
            for row in (0, level.rows - SUB):
                sum_y_planes(tag, row, slice(1, level.points - 1))
                on(slice(1, level.points - 1), slice(row, row + SUB))

        def raw_start_x(tag):
            level = FINE if tag == "f" else MID
            buf = s["l" + tag]
            start_faces(tag, EDGE_DIRS)
            for f, a in ((0, 0), (1, level.points - 1)):
                parts = [buf[a, SUB * z : SUB * z + SUB, :] for z in range(level.planes)]
                put(s["sx" + tag], f, pack(tag, parts))
            start_faces(tag, X_DIRS)

        def raw_start_z(tag):
            level = FINE if tag == "f" else MID
            buf, top = s["l" + tag], level.rows - SUB
            for side, row in ((0, 0), (1, top)):
                parts = [buf[a, row : row + SUB, :] for a in range(level.points)]
                put(s["sz" + tag], side, pack(tag, parts))
            start_faces(tag, Z_DIRS)

        def raw_finish(tag, on, before_faces, before_edges):
            level = FINE if tag == "f" else MID
            buf, last, top = s["l" + tag], level.points - 1, level.rows - SUB
            each(tag, 1, last, inner_update(tag, on))
            before_faces()
            par = add_faces(tag)
            for a in (0, last):
                sum_y(tag, a, 1, level.planes - 2)
                on(a, slice(SUB, top))
            for row in (0, top):
                sum_y_planes(tag, row, slice(1, last))
                on(slice(1, last), slice(row, row + SUB))
            before_edges()
            wait_some(lambda i: face_copy(tag, par, i), EDGE_DIRS)
            for k, (a, row) in enumerate(((0, 0), (0, top), (last, 0), (last, top))):
                rows = slice(row, row + SUB)
                buf[a, rows, :] += jnp.where(has_lo if a == 0 else has_hi, s["rc" + tag][par, k], 0.0)
                sum_y_planes(tag, row, a)
                on(a, rows)

        def steps(tag, count, residual, between, done=0):
            coefs = (FINE if tag == "f" else MID).steps(count)
            for index, (c1, c2) in enumerate(coefs):
                if index < done:
                    continue
                on = update(tag, "next", c1, c2, index == count - 2, residual)
                residual = "r"
                faces(tag, "d")
                interior(tag, "d", inner_update(tag, on))
                between[index]()
                face_update(tag, on)

        ones = [has_lo.astype(jnp.float32), 1.0, has_hi.astype(jnp.float32)]
        copies = [1.0 + ones[0], 1.0, 1.0 + ones[2]]
        def spread_row(row):
            return jnp.broadcast_to(row, (SUB, LANES))

        def patch_row(dx, k):
            dz, row = ((-1, 1), (0, 0), (0, 1), (1, 0))[k]
            ref = s["dsrc"] if (dx, dz) == (0, 0) else s["dhalo"].at[DIRS.index((dx, dz))]
            value = spread_row(ref[row : row + 1, :])
            if dx != 0:
                value = jnp.where(has_lo if dx < 0 else has_hi, value, 0.0)
            return value

        def patch(dx):
            return [patch_row(dx, k) for k in range(4)]

        def kinds_of(q):
            return [q[0] + q[1], q[1], q[1] + q[2], q[2], q[2] + q[3]]

        def kind_of(z, p):
            return {0: 0, p - 1: 2, 2 * p - 2: 4}.get(z, 1 if z < p else 3)

        def nodal(k, p):
            lo = k + jnp.where(lane > 0, pltpu.roll(k, 1, 1), 0.0)
            hi = k + jnp.where(lane < LANES - 1, pltpu.roll(k, LANES - 1, 1), 0.0)
            return jnp.where(sub == 0, lo, jnp.where(sub == p - 1, hi, k))

        def set_inverse(tag, level, a, xc, rows):
            row_k, _ = CONSTS.at["kzb" + tag]
            row_c, _ = CONSTS.at["cnt" + tag]
            kzb = s["cst"][row_k + rows.start : row_k + rows.stop, :]
            cnt = s["cst"][row_c + rows.start : row_c + rows.stop, :]
            diag = (float(level.kdiag[a]) + kzb) * s["cls" + tag][xc, rows, :]
            s["inv" + tag][a, rows, :] = 1.0 / (diag + copies[xc] * cnt)

        def set_class(tag, level, xc, kind, value):
            full = nodal(value, level.points)
            for z in range(level.planes):
                if kind_of(z, level.points) == kind:
                    s["cls" + tag][xc, SUB * z : SUB * z + SUB, :] = full

        def diagonals_inside(tag, level):
            first, second = patch_row(0, 1), patch_row(0, 2)
            kinds = [first, first, first + second, second, second]
            for z in range(level.planes):
                s["dz" + tag][SUB * z : SUB * z + SUB, :] = kinds[kind_of(z, level.points)]
            for kind in (1, 2, 3):
                set_class(tag, level, 1, kind, kinds[kind])
            for a in range(1, level.points - 1):
                set_inverse(tag, level, a, 1, slice(SUB, level.rows - SUB))

        def diagonals_x(tag, level):
            for xc, dx, a in ((0, -1, 0), (2, 1, level.points - 1)):
                first = patch_row(0, 1) + patch_row(dx, 1)
                second = patch_row(0, 2) + patch_row(dx, 2)
                for kind, value in ((1, first), (2, first + second), (3, second)):
                    set_class(tag, level, xc, kind, value)
                set_inverse(tag, level, a, xc, slice(SUB, level.rows - SUB))

        def diagonals_z(tag, level):
            set_class(tag, level, 1, 0, patch_row(0, 0) + patch_row(0, 1))
            set_class(tag, level, 1, 4, patch_row(0, 2) + patch_row(0, 3))
            for a in range(1, level.points - 1):
                set_inverse(tag, level, a, 1, slice(0, SUB))
                set_inverse(tag, level, a, 1, slice(level.rows - SUB, level.rows))

        def diagonals_edges(tag, level):
            for xc, dx, a in ((0, -1, 0), (2, 1, level.points - 1)):
                q = [u + v for u, v in zip(patch(0), patch(dx))]
                set_class(tag, level, xc, 0, q[0] + q[1])
                set_class(tag, level, xc, 4, q[2] + q[3])
                set_inverse(tag, level, a, xc, slice(0, SUB))
                set_inverse(tag, level, a, xc, slice(level.rows - SUB, level.rows))

        def side_diffusivity():
            q = [patch(-1), patch(0), patch(1)]
            for side in range(2):
                s["side"][side] = q[0][1 + side]
                s["side"][2 + side] = q[2][1 + side]
                s["side"][4 + side] = q[1][3 * side]

        def restrict_fine():
            def line(a):
                res = s["locf"][a] - s["lf"][a]
                parts = [res[SUB * i : SUB * i + SUB] for i in range(FINE.planes)]
                for i, t in enumerate(mix(R73Z.T, parts)):
                    s["tmpf"][a, SUB * i : SUB * i + SUB, :] = t

            loop(0, PF, line)

            def plane(z):
                rows = plane_rows(z)
                v = s["tmpf"][:, rows, :]
                t = jnp.stack(mix(R73, [v[a] for a in range(PF)]))
                acc = const("r73", 0) * t
                for shift in range(1, SUB):
                    acc = acc + const("r73", shift) * pltpu.roll(t, shift, 1)
                s["locm"][:, rows, :] = acc
                s["lm"][:, rows, :] = acc

            each("m", 0, MID.planes, plane)

        def prolong_fine():
            def plane(z):
                rows = plane_rows(z)
                v = s["xm"][:, rows, :]
                acc = const("j73", 0) * v
                for shift in range(1, SUB):
                    acc = acc + const("j73", shift) * pltpu.roll(v, shift, 1)
                for a, t in enumerate(mix(J73, [acc[i] for i in range(PM)])):
                    s["tmpf"][a, rows, :] = t

            each("m", 0, MID.planes, plane)

            def line(a):
                v = s["tmpf"][a]
                parts = [v[SUB * i : SUB * i + SUB] for i in range(MID.planes)]
                for i, t in enumerate(mix(J73Z, parts)):
                    s["xf"][a, SUB * i : SUB * i + SUB, :] += t

            loop(0, PF, line)

        def restrict_mid():
            for a in range(PM):
                res = s["locm"][a] - s["lm"][a]
                parts = [res[SUB * i : SUB * i + SUB] for i in range(MID.planes)]
                for i, t in enumerate(mix(R31Z.T, parts)):
                    s["tmpm"][a, SUB * i : SUB * i + SUB, :] = t
            spare = jnp.zeros((SUB, LANES), jnp.float32)
            for z in range(3):
                v = s["tmpm"][:, SUB * z : SUB * z + SUB, :]
                for a, t in enumerate(mix(R31, [v[i] for i in range(PM)])):
                    acc = const("r31", 0) * t
                    for shift in (1, 5, 6, 7):
                        acc = acc + const("r31", shift) * pltpu.roll(t, shift, 0)
                    up = pltpu.roll(pltpu.roll(acc, 1, 1), SUB - 1, 0)
                    node_row = acc + jnp.where(lane > 0, up, 0.0)
                    s["ga"][dev, 3 * a + z : 3 * a + z + 1, :] = node_row[0:1, :]
                    spare = spare + jnp.where(lane == z * nx + dev + a, up[0:1, 0:1], 0.0)
            s["ga"][dev, 6:7, :] = spare[0:1, :]
            s["ga"][dev, 7:8, :] = jnp.zeros((1, LANES), jnp.float32)

        def sum_x_low():
            flat = s["ga"]
            g = jnp.zeros((low_rows, LANES), jnp.float32)
            pad = lambda rows, before: jnp.pad(
                rows, ((before, low_rows - before - rows.shape[0]), (0, 0))
            )
            mine = s["gb"].at[
                pl.ds(pl.multiple_of(low_rows + node * low_rows, low_rows), low_rows)
            ]
            mine[...] = g
            for z in range(3):
                mine[z * nx : z * nx + n_dev, :] = flat[:, z, :]
                mine[z * nx + 1 : z * nx + nx, :] += flat[:, 3 + z, :]
            mine[3 * nx : 3 * nx + 1, :] = jnp.sum(flat[:, 6, :], axis=0, keepdims=True)

        low_lane = lax.broadcasted_iota(jnp.int32, (nz, LANES), 1)
        LAST = LANES - 1

        def ahead(v):
            return jnp.where(low_lane > 0, pltpu.roll(v, 1, 1), 0.0)

        def to_end(x, v):
            return jnp.where(low_lane == x, pltpu.roll(v, x + 1, 1), 0.0)

        def low_weights():
            up_z = lambda v: pltpu.roll(v, 1, 0)
            elem = lambda x: s["db"][pl.ds(x, nz, stride=n_dev), :]
            zero = jnp.zeros((nz, LANES), jnp.float32)
            y_copies = jnp.where(low_lane > 0, 2.0, 1.0)
            end_wx = end_wy = end_wz = zero
            for x in range(nx):
                lo = elem(x - 1) if x > 0 else zero
                hi = elem(x) if x < n_dev else zero
                both = lo + hi
                wy = 0.5 * (both + up_z(both))
                wym = ahead(wy)
                wz = 0.5 * (both + ahead(both))
                wzm = up_z(wz)
                hz = hi + up_z(hi)
                wx = 0.5 * (hz + ahead(hz))
                wxm = s["c_wx"][x - 1] if x > 0 else zero
                s["c_wy"][x] = wy
                s["c_wym"][x] = wym
                s["c_wz"][x] = wz
                s["c_wzm"][x] = wzm
                s["c_wx"][x] = wx
                x_copies = 1.0 if x in (0, n_dev) else 2.0
                s["c_dg"][x] = wx + wxm + wy + wym + wz + wzm + 2.0 * SHIFT_MASS * x_copies * y_copies
                end_wx = end_wx + to_end(x, 0.5 * hz)
                end_wy = end_wy + to_end(x, wy)
                end_wz = end_wz + to_end(x, 0.5 * both)
            end_wxm, end_wzm = ahead(end_wx), up_z(end_wz)
            x_copies = jnp.where((low_lane == 0) | (low_lane == n_dev), 1.0, 2.0)
            x_copies = jnp.where(low_lane < nx, x_copies, 0.0)
            s["c_wx"][nx] = end_wx
            s["c_wxm"][...] = end_wxm
            s["c_wy"][nx] = end_wy
            s["c_wz"][nx] = end_wz
            s["c_wzm"][nx] = end_wzm
            s["c_dg"][nx] = (
                end_wx + end_wxm + end_wy + end_wz + end_wzm + 2.0 * SHIFT_MASS * x_copies
            )

        def low_rhs():
            buf = s["gb"]
            buf[0:low_rows, :] = buf[n_node * low_rows : (n_node + 1) * low_rows, :]
            own = lambda row: buf[pl.ds(low_rows + row, n_node, stride=low_rows), :]
            before = lambda row: buf[pl.ds(row, n_node, stride=low_rows), :]
            at = lax.broadcasted_iota(jnp.int32, (n_node, LANES), 1)
            spare, spare_before = own(3 * nx), before(3 * nx)

            def pick(rows, first):
                moved = rows if first == 0 else pltpu.roll(rows, LANES - first, 1)
                return jnp.where(at < nx, moved, 0.0)

            even, odd = pl.ds(0, n_node, stride=2), pl.ds(1, n_node, stride=2)
            res, main = s["c_cr"], s["c_main"]
            for x in range(nx):
                main[even, :] = own(x) + before(2 * nx + x)
                main[odd, :] = own(nx + x)
                res[x] = main[...]
            main[even, :] = pick(spare, 0) + pick(spare_before, 2 * nx)
            main[odd, :] = pick(spare, nx)
            res[nx] = main[...]

        def fold(v):
            parts = [v[i : i + SUB] for i in range(0, v.shape[0], SUB)]
            while len(parts) > 1:
                parts = [u + w for u, w in zip(parts[::2], parts[1::2])] + (
                    [parts[-1]] if len(parts) % 2 else []
                )
            return parts[0]

        def total(v):
            return jnp.sum(v, axis=(0, 1), keepdims=True)

        def set_direction(x, value):
            p = s["c_p"]
            p[x, SUB : SUB + nz, :] = value
            p[x, 0:SUB, :] = value[nz - SUB : nz]
            p[x, SUB + nz : 2 * SUB + nz, :] = value[0:SUB]

        def coarse_solve():
            p, q, res, sol = s["c_p"], s["c_cq"], s["c_cr"], s["c_cx"]
            here = pl.ds(SUB, nz)
            norm = jnp.zeros((SUB, LANES), jnp.float32)
            for x in range(nx + 1):
                v = res[x]
                set_direction(x, v)
                sol[x] = jnp.zeros_like(v)
                norm = norm + fold(v * v)

            def along_pipe(x):
                out = s["c_wz"][x] * p[x, SUB + 1 : SUB + 1 + nz, :]
                return out + s["c_wzm"][x] * p[x, SUB - 1 : SUB - 1 + nz, :]

            def step_length(now):
                dot = jnp.zeros((SUB, LANES), jnp.float32)
                end = p[nx, here, :]
                last = jnp.zeros((nz, LANES), jnp.float32)
                for x in range(nx):
                    v = p[x, here, :]
                    out = s["c_dg"][x] * v
                    if x > 0:
                        out = out - s["c_wx"][x - 1] * p[x - 1, here, :]
                    if x < nx - 1:
                        out = out - s["c_wx"][x] * p[x + 1, here, :]
                    above = jnp.where(
                        low_lane == LAST, pltpu.roll(end, LAST - x, 1), pltpu.roll(v, LAST, 1)
                    )
                    below = pltpu.roll(v, 1, 1)
                    out = out - s["c_wy"][x] * above - s["c_wym"][x] * below
                    out = out - along_pipe(x)
                    q[x] = out
                    dot = dot + fold(v * out)
                    last = jnp.where(low_lane == x, pltpu.roll(v, x + 1, 1), last)
                out = s["c_dg"][nx] * end - s["c_wx"][nx] * pltpu.roll(end, LAST, 1)
                out = out - s["c_wxm"][...] * pltpu.roll(end, 1, 1)
                out = out - s["c_wy"][nx] * last - along_pipe(nx)
                q[nx] = out
                dot = dot + fold(end * out)
                return now / total(dot)

            def iteration(_, now):
                alpha = step_length(now)
                norm = jnp.zeros((SUB, LANES), jnp.float32)
                for x in range(nx + 1):
                    sol[x] += alpha * p[x, here, :]
                    v = res[x] - alpha * q[x]
                    res[x] = v
                    norm = norm + fold(v * v)
                new = total(norm)
                beta = new / now
                for x in range(nx + 1):
                    set_direction(x, res[x] + beta * p[x, here, :])
                return new

            alpha = step_length(lax.fori_loop(0, COARSE_ITERS - 1, iteration, total(norm)))
            for x in range(nx + 1):
                sol[x] += alpha * p[x, here, :]

        n3, edge_slope = MID.planes, float((MID.khat @ J31)[0, 0])

        def stacked(parts):
            return jnp.stack(list(parts))

        def exists(o):
            return (dev + o >= 0) & (dev + o < n_dev)

        def diff_at(o, k):
            x = jnp.clip(dev + o, 0, n_dev - 1)
            z = lax.rem(2 * node + k + nz, nz)
            row = spread_row(s["db"][pl.ds(z * n_dev + x, 1), :])
            return row if o == 0 else jnp.where(exists(o), row, 0.0)

        def over_planes(q):
            kinds = kinds_of(q)
            return stacked(kinds[kind_of(z, PM)] for z in range(n3))

        def column(o):
            return [diff_at(o, k) for k in (-1, 0, 1, 2)]

        def add_rows(p, q):
            return [u + v for u, v in zip(p, q)]

        def copies_at(o, a):
            if a == 0:
                return 1.0 + exists(o - 1).astype(jnp.float32)
            if a == PM - 1:
                return 1.0 + exists(o + 1).astype(jnp.float32)
            return 1.0

        def around(o, a):
            q = column(o)
            if a == 0:
                q = add_rows(q, column(o - 1))
            if a == PM - 1:
                q = add_rows(q, column(o + 1))
            return q

        def spread_low(i, k):
            x = jnp.clip(dev + i, 0, n_dev)
            z = lax.rem(2 * node + k + nz, nz)
            low = spread_row(s["c_cx"][x, pl.ds(z, 1), :])
            end = pltpu.roll(spread_row(s["c_cx"][nx, pl.ds(z, 1), :]), LAST - x, 1)
            high = jnp.where(lane < LAST, pltpu.roll(low, LAST, 1), end)
            return const("j31", 0) * low + const("j31", 1) * high

        def once(fn):
            seen = {}

            def get(*key):
                if key not in seen:
                    seen[key] = fn(*key)
                return seen[key]

            return get

        def y_summed(v):
            across, along = v.ndim - 1, v.ndim - 2
            up = pltpu.roll(pltpu.roll(v, 1, across), SUB - PM + 1, along)
            down = pltpu.roll(pltpu.roll(v, LANES - 1, across), PM - 1, along)
            v = v + jnp.where((sub == 0) & (lane > 0), up, 0.0)
            return v + jnp.where((sub == PM - 1) & (lane < LANES - 1), down, 0.0)

        def low_tools():
            node_at = once(spread_low)
            line_at = once(lambda i: stacked(mix(J31Z, [node_at(i, k) for k in (0, 1, 2)])))
            mass = const("mzfull").reshape(n3, SUB, LANES)
            h = edge_slope

            def along_line(o, a):
                pick = lambda f: mix(J31[a : a + 1], [f(o), f(o + 1)])[0]
                u = pick(line_at)
                before, after = pick(lambda i: node_at(i, -1)), pick(lambda i: node_at(i, 3))
                w = around(o, a)
                out = over_planes(w) * along_y("m", u) + copies_at(o, a) * mass * u
                f0, f1 = w[0] * (u[0] - before), w[1] * (u[PM - 1] - u[0])
                f2, f3 = w[2] * (u[n3 - 1] - u[PM - 1]), w[3] * (after - u[n3 - 1])
                zero = jnp.zeros((SUB, LANES), jnp.float32)
                flow = [zero] * n3
                flow[0], flow[PM - 1], flow[n3 - 1] = f0 - f1, f1 - f2, f2 - f3
                out = out + h * stacked(flow)
                if a in (0, PM - 1):
                    inner = line_at(o + 1) if a == 0 else line_at(o)
                    outer_o = o - 1 if a == 0 else o + 1
                    outer = line_at(o - 1) if a == 0 else line_at(o + 2)
                    out = out + h * (
                        over_planes(column(o)) * (u - inner)
                        + over_planes(column(outer_o)) * (u - outer)
                    )
                return u, out

            def beyond_z(side, c):
                k = -1 if side == 0 else 2
                far = c == (0 if side == 0 else PM - 1)
                other = k - 1 if side == 0 else k + 1
                at_x = once(lambda i: mix(J31[c : c + 1], [node_at(i, k), node_at(i, k + 1)])[0])
                across = lambda kk: stacked(mix(J31, [node_at(0, kk), node_at(1, kk)]))
                weights = once(lambda o: diff_at(o, k) + diff_at(o, other) if far else diff_at(o, k))
                u = stacked(mix(J31, [at_x(0), at_x(1)]))
                sums = lambda f: stacked(
                    [f(0) + f(-1), f(0), f(0), f(0) + f(1)]
                )
                total_w = sums(weights)
                copies3 = [copies_at(0, a) * (2.0 if far else 1.0) * SHIFT_MASS for a in range(PM)]
                out = total_w * along_y("m", u) + stacked(copies3[a] * u[a] for a in range(PM))
                zero = jnp.zeros((SUB, LANES), jnp.float32)
                flow = [zero] * PM
                flow[0] = weights(-1) * (u[0] - at_x(-1)) + weights(0) * (u[0] - u[PM - 1])
                flow[PM - 1] = weights(0) * (u[PM - 1] - u[0]) + weights(1) * (u[PM - 1] - at_x(2))
                out = out + h * stacked(flow)
                if far:
                    inner, outer = (across(k + 1), across(k - 1)) if side == 0 else (
                        across(k),
                        across(k + 2),
                    )
                    out = out + h * (
                        sums(lambda o: diff_at(o, k)) * (u - inner)
                        + sums(lambda o: diff_at(o, other)) * (u - outer)
                    )
                return out

            return along_line, beyond_z

        beyond_x = ((-1, (0, 1, 2), MID.khat[PM - 1]), (1, (1, 2, 3), MID.khat[0]))
        beyond_c = (((0, 1, 2), MID.khat[PM - 1]), ((1, 2, 3), MID.khat[0]))

        def ghost_diagonals():
            theta = MID.theta
            my = 1.0 + jnp.where(((sub == 0) & (lane > 0)) | ((sub == PM - 1) & (lane < LAST)), 1.0, 0.0)
            kb = mirrored_rows(MID.kdiag)
            kz = [float(v) for v in np.concatenate([MID.kdiag, MID.kdiag[1:]])]
            for side, (o, points, row) in enumerate(beyond_x):
                for index, a in enumerate(points):
                    kinds = [nodal(k, PM) for k in kinds_of(around(o, a))]
                    for z in range(n3):
                        diag = (float(MID.kdiag[a]) + kz[z] + kb) * kinds[kind_of(z, PM)]
                        diag = diag + (float(MID_COPIES[z]) * SHIFT_MASS * copies_at(o, a)) * my
                        s["ghost_x"][side, index, z] = float(row[a] / theta) / diag
            for side, (planes, row) in enumerate(beyond_c):
                k = -1 if side == 0 else 2
                other = k - 1 if side == 0 else k + 1
                for index, c in enumerate(planes):
                    far = c in (0, PM - 1)
                    weights = lambda o: diff_at(o, k) + diff_at(o, other) if far else diff_at(o, k)
                    for a in range(PM):
                        w = weights(0)
                        if a in (0, PM - 1):
                            w = w + weights(-1 if a == 0 else 1)
                        diag = (float(MID.kdiag[a] + MID.kdiag[c]) + kb) * nodal(w, PM)
                        scale = (2.0 if far else 1.0) * SHIFT_MASS * copies_at(0, a)
                        s["ghost_z"][side, index, a] = float(row[c] / theta) / (diag + scale * my)

        def mirrored_rows(values):
            out = jnp.zeros((SUB, LANES), jnp.float32)
            for i, v in enumerate(values):
                out = jnp.where(sub == i, float(v), out)
            return out

        def send_known_part():
            c = float(1.0 / MID.theta)
            for a in range(PM):
                sum_y("m", a)
                res = s["rhsm"][a] - s["lm"][a]
                s["rm"][a] = res
                s["dm"][a] = c * s["invm"][a] * res
            plane = lambda z: s["dm"][:, SUB * z : SUB * z + SUB, :]
            for side, (points, row) in enumerate(((range(1, PM), 0), (range(PM - 1), PM - 1))):
                rows = [s["dm"][a] for a in points]
                t = mix(MID.khat[row : row + 1, list(points)], rows)[0]
                put(s["sxm"], side, pack("m", [t[SUB * z : SUB * z + SUB] for z in range(n3)]))
                first = 0 if side == 0 else PM - 1
                t = mix(MID.khat[row : row + 1, list(points)], [plane(first + c) for c in points])[0]
                put(s["szm"], side, pack("m", [t[a] for a in range(PM)]))
            start_faces("m", X_DIRS + Z_DIRS)

        def after_coarse(c1, c2):
            c = float(1.0 / MID.theta)
            along_line, beyond_z = low_tools()
            shape = (n3, SUB, LANES)
            flat = (MID.rows, LANES)
            par = parity["m"]
            parity["m"] = 1 - par
            for a in range(PM):
                u, rho = along_line(0, a)
                res = s["rm"][a] - y_summed(rho).reshape(flat)
                upd = c * s["invm"][a] * res
                s["rm"][a] = res
                s["dm"][a] = upd
                s["xm"][a] = s["xm"][a] + u.reshape(flat) + upd
            for side, (o, points, row) in enumerate(beyond_x):
                acc = None
                for index, a in enumerate(points):
                    _, rho = along_line(o, a)
                    t = s["ghost_x"][side, index] * y_summed(rho)
                    acc = t if acc is None else acc + t
                s["tmpf"][side] = acc.reshape(flat)
            for side, (planes, row) in enumerate(beyond_c):
                acc = None
                for index, cc in enumerate(planes):
                    t = s["ghost_z"][side, index] * y_summed(beyond_z(side, cc))
                    acc = t if acc is None else acc + t
                s["tmpf"][2 + side, 0 : PM * SUB, :] = acc.reshape(PM * SUB, LANES)
            wait_some(lambda i: face_copy("m", par, i), X_DIRS + Z_DIRS)
            d = [s["dm"][a].reshape(shape) for a in range(PM)]
            own_x = mix_even_odd(MID.khat, d)
            last = float(MID.khat[PM - 1, PM - 1])
            terms_x = []
            for side, a in ((0, 0), (1, PM - 1)):
                t = stacked(unpack("m", s["rxm"][par, side], n3)) - s["tmpf"][side].reshape(shape)
                terms_x.append(t + last * d[a])
            terms_z = []
            for side, z in ((0, 0), (1, n3 - 1)):
                t = stacked(unpack("m", s["rzm"][par, side], PM))
                t = t - s["tmpf"][2 + side, 0 : PM * SUB, :].reshape(PM, SUB, LANES)
                terms_z.append(t + last * stacked(v[z] for v in d))
            mass = const("mzfull").reshape(shape)
            here = over_planes(column(0))
            for a in range(PM):
                w = around(0, a)
                out = over_planes(w) * along_y("m", d[a]) + copies_at(0, a) * mass * d[a]
                out = out + here * own_x[a]
                if a == 0:
                    out = out + over_planes(column(-1)) * terms_x[0]
                if a == PM - 1:
                    out = out + over_planes(column(1)) * terms_x[1]
                low = mix_even_odd(MID.khat, [d[a][z] for z in range(PM)])
                high = mix_even_odd(MID.khat, [d[a][z] for z in range(PM - 1, n3)])
                along = [w[1] * v for v in low] + [w[2] * v for v in high[1:]]
                along[PM - 1] = along[PM - 1] + w[2] * high[0]
                along[0] = along[0] + w[0] * terms_z[0][a]
                along[n3 - 1] = along[n3 - 1] + w[3] * terms_z[1][a]
                out = y_summed(out + stacked(along)).reshape(flat)
                res = s["rm"][a] - out
                upd = c1 * s["dm"][a] + c2 * s["invm"][a] * res
                s["lm"][a] = res
                s["locm"][a] = upd
            for a in range(PM):
                s["rm"][a] = s["lm"][a]
                s["dm"][a] = s["locm"][a]
                s["xm"][a] = s["xm"][a] + s["locm"][a]

        nothing = lambda: None
        load_diff.wait()
        s["da"][dev] = s["dsrc"][...]
        wz = np.concatenate([FINE.w, FINE.w[1:]])

        def mirrored(index, values):
            out = jnp.float32(values[0])
            for i in range(1, PF // 2):
                out = jnp.where((index == i) | (index == PF - 1 - i), float(values[i]), out)
            return out

        across_y = mirrored(sub, 1.0 / FINE.w)

        def load_line(a):
            planes = []
            for e in range(2):
                for c in range(PF):
                    start = a * chunk + 2 * c + e
                    planes.append(s["ein"][pl.ds(start, SUB, stride=2 * PF), :])
            merged = planes[: PF - 1] + [planes[PF - 1] + planes[PF]] + planes[PF + 1 :]
            scale = across_y * mirrored(jnp.int32(a), 1.0 / FINE.w)
            for z, v in enumerate(merged):
                t = scale * v * float(1.0 / wz[z])
                s["locf"][a, SUB * z : SUB * z + SUB, :] = t
                s["lf"][a, SUB * z : SUB * z + SUB, :] = t

        for a in (0, PF - 1):
            load_in(a).wait()
            load_line(a)
        wait_barrier()
        start_some(halo_copy, range(8))
        raw_start_x("f")
        for a in range(1, PF - 1):
            load_in(a).wait()
        loop(1, PF - 1, load_line)
        raw_start_z("f")
        load_cst.wait()
        diagonals_inside("f", FINE)
        diagonals_inside("m", MID)

        def halo_sides():
            start_a("d")
            wait_some(halo_copy, X_DIRS)
            diagonals_x("f", FINE)
            wait_some(halo_copy, Z_DIRS)
            diagonals_z("f", FINE)

        def halo_edges():
            wait_some(halo_copy, EDGE_DIRS)
            diagonals_edges("f", FINE)

        def diff_stage_b():
            wait_a("d")
            mine = slot("d", node)
            for e in range(2):
                mine[e * n_dev : (e + 1) * n_dev, :] = s["da"][:, e, :]
            start_b("d")

        raw_finish("f", update("f", "zero"), halo_sides, halo_edges)
        side_diffusivity()
        steps("f", SMOOTH_FINE, "rhs", [diff_stage_b, lambda: forward_b("d")])
        apply("f", "x")
        restrict_fine()

        raw_start_x("m")
        raw_start_z("m")

        def order3_faces():
            diagonals_x("m", MID)
            diagonals_z("m", MID)
            diagonals_edges("m", MID)
            wait_b("d")

        raw_finish("m", update("m", "zero"), order3_faces, nothing)
        steps("m", SMOOTH_MID, "rhs", [low_weights, ghost_diagonals])
        faces("m", "x")
        interior("m", "x")
        restrict_mid()
        start_a("g")
        add_faces("m")
        send_known_part()
        wait_a("g")
        sum_x_low()
        start_b("g")
        forward_b("g")
        wait_b("g")
        low_rhs()
        coarse_solve()
        coefs = MID.steps(SMOOTH_MID)
        after_coarse(*coefs[0])
        steps("m", SMOOTH_MID, "r", [nothing, nothing], 1)
        prolong_fine()
        first = update("f", "first")
        faces("f", "x")
        interior("f", "x", inner_update("f", first))
        face_update("f", first)
        steps("f", SMOOTH_FINE, "r", [nothing, nothing])

        def store_line(a):
            for e in range(2):
                for c in range(PF):
                    z = e * (PF - 1) + c
                    start = a * chunk + 2 * c + e
                    out_ref[pl.ds(start, SUB, stride=2 * PF), :] = s["xf"][
                        a, SUB * z : SUB * z + SUB, :
                    ]

        loop(0, PF, store_line)

    return kernel


def solution(mesh):
    n_node, n_dev = mesh.shape["node"], mesh.shape["dev"]
    shapes, low_rows = scratch_shapes(n_node, n_dev)
    kernel = make_kernel(n_node, n_dev, list(shapes), low_rows)
    rows = PF * PF * PF * 2

    def local(element_load, diffusivity):
        out = pl.pallas_call(
            kernel,
            out_shape=pltpu.VMEM((rows, LANES), jnp.float32),
            in_specs=[pl.BlockSpec(memory_space=pltpu.HBM)] * 3,
            out_specs=pl.BlockSpec(memory_space=pltpu.VMEM),
            scratch_shapes=list(shapes.values()),
            compiler_params=pltpu.CompilerParams(
                collective_id=0, has_side_effects=True, vmem_limit_bytes=48 * 1024 * 1024
            ),
        )(
            pltpu.with_memory_space_constraint(element_load.reshape(rows, LANES), pltpu.HBM),
            pltpu.with_memory_space_constraint(diffusivity.reshape(2, LANES), pltpu.HBM),
            pltpu.with_memory_space_constraint(jnp.asarray(CONSTS.array()), pltpu.HBM),
        )
        return out.reshape(element_load.shape)

    return jax.shard_map(
        local,
        mesh=mesh,
        in_specs=(P(None, None, None, "dev", "node", None), P("dev", "node", None)),
        out_specs=P(None, None, None, "dev", "node", None),
        check_vma=False,
    )
```

```python
import jax
import jax.numpy as jnp
import numpy as np
from jax import lax
from jax.experimental import pallas as pl
from jax.experimental.pallas import tpu as pltpu
from jax.sharding import PartitionSpec as P

PF = 8
PM = 4
PC = 2
SMOOTH_FINE = 3
SMOOTH_MID = 3
COARSE_ITERS = 5
SHIFT_MASS = 0.05
LANES = 128
SUB = 8
MESH = pl.DeviceIdType.MESH

def legendre_values(points, poly_order):
    columns = [points * 0.0 + 1.0, points]
    for degree in range(2, poly_order + 1):
        columns.append(
            ((2 * degree - 1) * points * columns[degree - 1] - (degree - 1) * columns[degree - 2])
            / degree
        )
    return np.stack(columns[: poly_order + 1], axis=1)


def largest_eigen(matrix):
    size_n = matrix.shape[0]
    vector = np.cos(2.7 * np.arange(size_n) + 0.3)
    for power_step in range(4000):
        vector = matrix @ vector
        vector = vector / np.sqrt(np.sum(vector * vector))
    return float(vector @ (matrix @ vector))


def gll_level(poly_order):
    point_count = poly_order + 1
    gll_nodes = np.cos(np.pi * np.arange(point_count) / poly_order)
    for newton_step in range(60):
        values = legendre_values(gll_nodes, poly_order)
        gll_nodes = gll_nodes - (gll_nodes * values[:, poly_order] - values[:, poly_order - 1]) / (
            point_count * values[:, poly_order]
        )
    gll_nodes = np.sort(gll_nodes)
    values = legendre_values(gll_nodes, poly_order)
    top_value = values[:, poly_order]
    weights = 2.0 / (poly_order * point_count * top_value**2)
    deriv_matrix = np.zeros((point_count, point_count))
    for row_index in range(point_count):
        for col_index in range(point_count):
            if row_index != col_index:
                deriv_matrix[row_index, col_index] = top_value[row_index] / (
                    top_value[col_index] * (gll_nodes[row_index] - gll_nodes[col_index])
                )
    deriv_matrix[0, 0] = -poly_order * point_count / 4.0
    deriv_matrix[poly_order, poly_order] = poly_order * point_count / 4.0
    stiffness = deriv_matrix.T @ (weights[:, None] * deriv_matrix)
    diag_ids = np.arange(point_count)
    stiff_diag = stiffness[diag_ids, diag_ids]
    diag_scale = 1.0 / np.sqrt(stiff_diag)
    eig_bound = largest_eigen(diag_scale[:, None] * stiffness * diag_scale[None, :])
    return (gll_nodes, weights, deriv_matrix, stiff_diag, eig_bound)


def interp_table(fine_nodes, coarse_nodes):
    interp_mat = np.ones((fine_nodes.shape[0], coarse_nodes.shape[0]))
    for col_index in range(coarse_nodes.shape[0]):
        for other_index in range(coarse_nodes.shape[0]):
            if other_index != col_index:
                interp_mat[:, col_index] *= (fine_nodes - coarse_nodes[other_index]) / (
                    coarse_nodes[col_index] - coarse_nodes[other_index]
                )
    return interp_mat


class Level:
    def __init__(self, points):
        nodes, w, deriv, stiff_diag, bound = gll_level(points - 1)
        self.points = points
        self.planes = 2 * points - 1
        self.rows = SUB * self.planes
        self.x_rows = SUB * (self.planes if points == SUB else -(-self.planes // 2))
        self.z_rows = SUB * (points if points == SUB else -(-points // 2))
        self.nodes = nodes
        self.w = w
        self.khat = (deriv.T @ (w[:, None] * deriv)) / w[:, None]
        self.kdiag = stiff_diag / w
        self.theta = 0.6 * bound
        self.delta = 0.5 * bound

    def steps(self, count):
        sig = self.theta / self.delta
        rho = 1.0 / sig
        out = []
        for _ in range(count - 1):
            rho_next = 1.0 / (2.0 * sig - rho)
            out.append((float(rho_next * rho), float(2.0 * rho_next / self.delta)))
            rho = rho_next
        return out


def roll_coefs(matrix):
    full = np.zeros((SUB, SUB))
    full[: matrix.shape[0], : matrix.shape[1]] = matrix
    i = np.arange(SUB)
    return [full[i, (i - s) % SUB] for s in range(SUB)]


def two_elements(matrix):
    n, m = matrix.shape
    out = np.zeros((2 * n - 1, 2 * m - 1))
    out[:n, :m] = matrix
    out[n - 1 :, m - 1 :] = matrix
    return out


def plane_sum(points):
    values = np.zeros((2 * points - 1,))
    values[:points] += 1
    values[points - 1 :] += 1
    return values


class Consts:
    def __init__(self):
        self.blocks = []
        self.at = {}
        self.row = 0

    def add(self, name, block):
        block = np.asarray(block, np.float64)
        if block.ndim == 1:
            block = np.broadcast_to(block[:, None], (block.shape[0], LANES))
        assert block.shape[0] % SUB == 0
        self.at[name] = (self.row, block.shape[0])
        self.blocks.append(block)
        self.row += block.shape[0]

    def array(self):
        return np.concatenate(self.blocks, 0).astype(np.float32)


FINE, MID, LOW = Level(PF), Level(PM), Level(PC)
J73 = interp_table(FINE.nodes, MID.nodes)
J31 = interp_table(MID.nodes, LOW.nodes)
R73 = (FINE.w[:, None] * J73 / MID.w[None, :]).T
R31 = (MID.w[:, None] * J31).T
R73Z = two_elements(FINE.w[:, None] * J73 / MID.w[None, :])
R73Z[PF - 1] = 0.0
R73Z[PF - 1, PM - 1] = FINE.w[0] / MID.w[0]
R31Z = two_elements(MID.w[:, None] * J31)
R31Z[PM - 1] = 0.0
R31Z[PM - 1, PC - 1] = MID.w[0]
J73Z = two_elements(J73)
J31Z = two_elements(J31)

CONSTS = Consts()
for tag, level in (("f", FINE), ("m", MID)):
    CONSTS.add("ky" + tag, np.concatenate(roll_coefs(level.khat)))
    kb = np.zeros(SUB)
    kb[: level.points] = level.kdiag
    kz = np.concatenate([level.kdiag, level.kdiag[1:]])
    CONSTS.add("kzb" + tag, (kz[:, None] + kb[None, :]).reshape(-1))
    ey = np.arange(LANES)
    my = np.ones((SUB, LANES))
    my[0] += ey > 0
    my[level.points - 1] += ey < LANES - 1
    mz = np.ones(level.planes)
    mz[[0, level.points - 1, -1]] = 2
    CONSTS.add("cnt" + tag, (SHIFT_MASS * mz[:, None, None] * my[None]).reshape(-1, LANES))
    CONSTS.add("mz" + tag, np.repeat(SHIFT_MASS * plane_sum(level.points), SUB))
MID_COPIES = np.ones(MID.planes)
MID_COPIES[[0, PM - 1, -1]] = 2
CONSTS.add("mzfull", np.repeat(SHIFT_MASS * MID_COPIES, SUB))
CONSTS.add("r73", np.concatenate(roll_coefs(R73)))
CONSTS.add("j73", np.concatenate(roll_coefs(J73)))
CONSTS.add("r31", np.concatenate(roll_coefs(R31)))
CONSTS.add("j31", np.concatenate([np.pad(J31[:, p], (0, SUB - PM)) for p in range(PC)]))
CONSTS.add("iwb", 1.0 / FINE.w)

DIRS = ((-1, 0), (1, 0), (0, -1), (0, 1), (-1, -1), (-1, 1), (1, -1), (1, 1))
OPP = tuple(DIRS.index((-dx, -dz)) for dx, dz in DIRS)
COEF = 1e-13


def mix(matrix, parts):
    out = []
    for row in np.asarray(matrix):
        acc = None
        for c, v in zip(row, parts):
            if abs(c) > COEF:
                term = v if abs(c - 1.0) < COEF else float(c) * v
                acc = term if acc is None else acc + term
        out.append(acc)
    return out


def mix_even_odd(matrix, parts):
    n = len(parts)
    h = n // 2
    flipped = matrix[:h, ::-1][:, :h]
    even = mix(0.5 * (matrix[:h, :h] + flipped), [parts[i] + parts[n - 1 - i] for i in range(h)])
    odd = mix(0.5 * (matrix[:h, :h] - flipped), [parts[i] - parts[n - 1 - i] for i in range(h)])
    low = [e + o for e, o in zip(even, odd)]
    high = [e - o for e, o in zip(even, odd)]
    return low + high[::-1]


def scratch_shapes(n_node, n_dev):
    f32 = jnp.float32
    low_rows = -(-(3 * (n_dev + 1) + 1) // SUB) * SUB
    shapes = {}
    for tag, level in (("f", FINE), ("m", MID)):
        p, rows = level.points, level.rows
        for name in ("loc", "rhs", "inv", "x", "r", "d", "l"):
            shapes[name + tag] = pltpu.VMEM((p, rows, LANES), f32)
        shapes["cls" + tag] = pltpu.VMEM((3, rows, LANES), f32)
        shapes["dz" + tag] = pltpu.VMEM((rows, LANES), f32)
        shapes["rx" + tag] = pltpu.VMEM((2, 2, level.x_rows, LANES), f32)
        shapes["rz" + tag] = pltpu.VMEM((2, 2, level.z_rows, LANES), f32)
        shapes["sx" + tag] = pltpu.VMEM((2, level.x_rows, LANES), f32)
        shapes["sz" + tag] = pltpu.VMEM((2, level.z_rows, LANES), f32)
        shapes["rc" + tag] = pltpu.VMEM((2, 4, SUB, LANES), f32)
        shapes["ssem" + tag] = pltpu.SemaphoreType.DMA((8,))
        shapes["rsem" + tag] = pltpu.SemaphoreType.DMA((2, 8))
    shapes["tmpf"] = pltpu.VMEM((PF, MID.rows, LANES), f32)
    shapes["tmpm"] = pltpu.VMEM((PM, LOW.rows, LANES), f32)
    shapes["ein"] = pltpu.VMEM((PF * PF * PF * 2, LANES), f32)
    shapes["cst"] = pltpu.VMEM((CONSTS.row, LANES), f32)
    shapes["insem"] = pltpu.SemaphoreType.DMA((PF + 2,))
    shapes["ghost_x"] = pltpu.VMEM((2, 3, MID.planes, SUB, LANES), f32)
    shapes["ghost_z"] = pltpu.VMEM((2, 3, PM, SUB, LANES), f32)
    shapes["side"] = pltpu.VMEM((6, SUB, LANES), f32)
    shapes["dsrc"] = pltpu.VMEM((SUB, LANES), f32)
    shapes["dhalo"] = pltpu.VMEM((8, SUB, LANES), f32)
    shapes["dssem"] = pltpu.SemaphoreType.DMA((8,))
    shapes["drsem"] = pltpu.SemaphoreType.DMA((8,))
    shapes["da"] = pltpu.VMEM((n_dev, SUB, LANES), f32)
    shapes["db"] = pltpu.VMEM((n_node * 2 * n_dev, LANES), f32)
    shapes["ga"] = pltpu.VMEM((n_dev, SUB, LANES), f32)
    shapes["gb"] = pltpu.VMEM(((n_node + 1) * low_rows, LANES), f32)
    half = n_node // 2
    for tag in "dg":
        shapes[tag + "a_s"] = pltpu.SemaphoreType.DMA((n_dev,))
        shapes[tag + "a_r"] = pltpu.SemaphoreType.DMA((n_dev,))
        shapes[tag + "b_s"] = pltpu.SemaphoreType.DMA((half,))
        shapes[tag + "b_r"] = pltpu.SemaphoreType.DMA((half,))
        shapes[tag + "c_s"] = pltpu.SemaphoreType.DMA((half,))
        shapes[tag + "c_r"] = pltpu.SemaphoreType.DMA((half,))
    nx, nz = n_dev + 1, 2 * n_node
    for name in ("wx", "wy", "wym", "wz", "wzm", "dg", "cx", "cr", "cq"):
        shapes["c_" + name] = pltpu.VMEM((nx + 1, nz, LANES), f32)
    shapes["c_wxm"] = pltpu.VMEM((nz, LANES), f32)
    shapes["c_main"] = pltpu.VMEM((nz, LANES), f32)
    shapes["c_p"] = pltpu.VMEM((nx + 1, nz + 2 * SUB, LANES), f32)
    return shapes, low_rows


def make_kernel(n_node, n_dev, names, low_rows):
    half = n_node // 2
    nx, nz = n_dev + 1, 2 * n_node

    def kernel(ein_hbm, diff_hbm, cst_hbm, out_ref, *scratch):
        s = dict(zip(names, scratch))
        node = lax.axis_index("node")
        dev = lax.axis_index("dev")
        sub = lax.broadcasted_iota(jnp.int32, (SUB, LANES), 0)
        lane = lax.broadcasted_iota(jnp.int32, (SUB, LANES), 1)
        has_lo, has_hi = dev > 0, dev < n_dev - 1

        def const(name, index=None):
            row, size = CONSTS.at[name]
            if index is None:
                return s["cst"][row : row + size, :]
            return s["cst"][row + SUB * index : row + SUB * index + SUB, :]

        def neighbour(dx, dz):
            return (lax.rem(node + dz + n_node, n_node), lax.rem(dev + dx + n_dev, n_dev))

        sibling = (node + 1 - 2 * lax.rem(node, 2), dev)

        def same_core(k):
            return lax.rem(node + 2 * k, n_node)

        barrier = pltpu.get_barrier_semaphore()

        def greet(target):
            pl.semaphore_signal(barrier, inc=1, device_id=target, device_id_type=MESH)

        for dx, dz in DIRS:
            greet(neighbour(dx, dz))
        s["dsrc"][...] = jnp.zeros_like(s["dsrc"])
        chunk = PF * PF * 2
        load_diff = pltpu.make_async_copy(
            diff_hbm, s["dsrc"].at[pl.ds(0, 2)], s["insem"].at[PF + 1]
        )
        load_cst = pltpu.make_async_copy(cst_hbm, s["cst"], s["insem"].at[PF])

        def load_in(a):
            rows = pl.ds(a * chunk, chunk)
            return pltpu.make_async_copy(ein_hbm.at[rows], s["ein"].at[rows], s["insem"].at[a])

        load_diff.start()
        for a in (0, PF - 1) + tuple(range(1, PF - 1)):
            load_in(a).start()
        load_cst.start()

        far = lambda k: lax.rem(dev + k, n_dev)

        def greet_far(k, _):
            greet((node, lax.rem(dev + k, n_dev)))
            return 0

        def greet_cores(k, _):
            greet((same_core(k), dev))
            return 0

        lax.fori_loop(1, n_dev, greet_far, 0)
        lax.fori_loop(1, half, greet_cores, 0)

        def wait_barrier():
            pl.semaphore_wait(barrier, n_dev - 1 + half - 1 + len(DIRS))

        def face_copy(tag, par, i):
            level = FINE if tag == "f" else MID
            dx, dz = DIRS[i]
            j = OPP[i]
            if dz == 0:
                src, dst = s["sx" + tag].at[i], s["rx" + tag].at[par, j]
            elif dx == 0:
                src, dst = s["sz" + tag].at[i - 2], s["rz" + tag].at[par, j - 2]
            else:
                a = 0 if dx < 0 else level.points - 1
                zrow = pl.ds(0 if dz < 0 else level.rows - SUB, SUB)
                src, dst = s["loc" + tag].at[a, zrow], s["rc" + tag].at[par, j - 4]
            return pltpu.make_async_remote_copy(
                src_ref=src,
                dst_ref=dst,
                send_sem=s["ssem" + tag].at[i],
                recv_sem=s["rsem" + tag].at[par, j],
                device_id=neighbour(dx, dz),
                device_id_type=MESH,
            )

        def halo_copy(i):
            return pltpu.make_async_remote_copy(
                src_ref=s["dsrc"],
                dst_ref=s["dhalo"].at[OPP[i]],
                send_sem=s["dssem"].at[i],
                recv_sem=s["drsem"].at[OPP[i]],
                device_id=neighbour(*DIRS[i]),
                device_id_type=MESH,
            )

        def start_some(make, which):
            for i in which:
                make(i).start()

        def wait_some(make, which):
            for i in which:
                make(i).wait_send()
            for i in which:
                make(i).wait_recv()

        X_DIRS, Z_DIRS, EDGE_DIRS = (0, 1), (2, 3), (4, 5, 6, 7)
        parity = {"f": 0, "m": 0}

        def start_faces(tag, which):
            start_some(lambda i: face_copy(tag, parity[tag], i), which)

        def pack(tag, parts):
            if tag == "f":
                return parts
            h = -(-len(parts) // 2)
            return [
                parts[i] + pltpu.roll(parts[i + h], PM, 0) if i + h < len(parts) else parts[i]
                for i in range(h)
            ]

        def unpack(tag, v, count):
            parts = [v[SUB * i : SUB * i + SUB] for i in range(v.shape[0] // SUB)]
            if tag == "f":
                return parts
            out = parts + [pltpu.roll(t, PM, 0) for t in parts]
            return [jnp.where(sub < PM, t, 0.0) for t in out[:count]]

        def put(ref, index, parts):
            for i, t in enumerate(parts):
                ref[index, SUB * i : SUB * i + SUB, :] = t

        def add_faces(tag):
            level = FINE if tag == "f" else MID
            par = parity[tag]
            parity[tag] = 1 - par
            wait_some(lambda i: face_copy(tag, par, i), X_DIRS + Z_DIRS)
            buf, rx, rz = (s[n + tag] for n in ("l", "rx", "rz"))
            last, top = level.points - 1, level.rows - SUB
            has = (has_lo, has_hi)
            for side, a in ((0, 0), (1, last)):
                for z, t in enumerate(unpack(tag, rx[par, side], level.planes)):
                    t = jnp.where(has[side], t, 0.0)
                    buf[a, SUB * z : SUB * z + SUB, :] += t
            for side, row in ((0, 0), (1, top)):
                for a, t in enumerate(unpack(tag, rz[par, side], level.points)):
                    buf[a, row : row + SUB, :] += t
            return par

        def sum_y(tag, a, first=0, count=None):
            level = FINE if tag == "f" else MID
            n = level.planes if count is None else count
            buf = s["l" + tag]
            rows_lo = pl.ds(SUB * first, n, stride=SUB)
            rows_hi = pl.ds(SUB * first + level.points - 1, n, stride=SUB)
            lo, hi = buf[a, rows_lo, :], buf[a, rows_hi, :]
            at = lax.broadcasted_iota(jnp.int32, (n, LANES), 1)
            buf[a, rows_lo, :] = lo + jnp.where(at > 0, pltpu.roll(hi, 1, 1), 0.0)
            buf[a, rows_hi, :] = hi + jnp.where(
                at < LANES - 1, pltpu.roll(lo, LANES - 1, 1), 0.0
            )

        def sum_y_planes(tag, row, which):
            p = (FINE if tag == "f" else MID).points
            sel = (which, slice(row, row + SUB))
            t = s["l" + tag][sel]
            across, along = t.ndim - 1, t.ndim - 2
            up = pltpu.roll(t, 1, across)
            down = pltpu.roll(t, LANES - 1, across)
            up = pltpu.roll(up, SUB - p + 1, along)
            down = pltpu.roll(down, p - 1, along)
            t = t + jnp.where((sub == 0) & (lane > 0), up, 0.0)
            t = t + jnp.where((sub == p - 1) & (lane < LANES - 1), down, 0.0)
            s["l" + tag][sel] = t

        def gather_a(tag, k):
            buf = s[tag + "a"]
            return pltpu.make_async_remote_copy(
                src_ref=buf.at[dev],
                dst_ref=buf.at[dev],
                send_sem=s[tag + "a_s"].at[k],
                recv_sem=s[tag + "a_r"].at[k],
                device_id=(node, far(k)),
                device_id_type=MESH,
            )

        block = {"d": 2 * n_dev, "g": low_rows}
        base = {"d": 0, "g": low_rows}

        def slot(tag, index):
            size = block[tag]
            return s[tag + "b"].at[pl.ds(pl.multiple_of(base[tag] + index * size, size), size)]

        def gather_b(tag, k):
            return pltpu.make_async_remote_copy(
                src_ref=slot(tag, node),
                dst_ref=slot(tag, node),
                send_sem=s[tag + "b_s"].at[k],
                recv_sem=s[tag + "b_r"].at[k],
                device_id=(same_core(k), dev),
                device_id_type=MESH,
            )

        def gather_c(tag, k):
            index = lax.rem(node - 2 * k + n_node, n_node)
            return pltpu.make_async_remote_copy(
                src_ref=slot(tag, index),
                dst_ref=slot(tag, index),
                send_sem=s[tag + "c_s"].at[k],
                recv_sem=s[tag + "c_r"].at[k],
                device_id=sibling,
                device_id_type=MESH,
            )

        def plane_rows(z):
            if isinstance(z, int):
                return slice(z * SUB, z * SUB + SUB)
            return pl.ds(pl.multiple_of(z * SUB, SUB), SUB)

        def each(tag, lower, upper, fn):
            if tag == "m":
                for k in range(lower, upper):
                    fn(k)
            else:
                loop(lower, upper, fn)

        def loop(lower, upper, fn):
            def step(k, _):
                fn(k)
                return 0

            lax.fori_loop(lower, upper, step, 0)

        def start_a(tag):
            loop(1, n_dev, lambda k: gather_a(tag, k).start())

        def wait_a(tag):
            loop(1, n_dev, lambda k: gather_a(tag, k).wait())

        def start_b(tag):
            loop(1, half, lambda k: gather_b(tag, k).start())
            gather_c(tag, 0).start()

        def forward_b(tag):
            def one(k):
                gather_b(tag, k).wait_recv()
                gather_c(tag, k).start()

            loop(1, half, one)

        def wait_b(tag):
            loop(1, half, lambda k: gather_b(tag, k).wait_send())
            loop(0, half, lambda k: gather_c(tag, k).wait())

        def along_y(tag, v):
            p = (FINE if tag == "f" else MID).points
            acc = const("ky" + tag, 0) * v
            for shift in range(1, SUB):
                if p == PF or shift < p or shift > SUB - p:
                    acc = acc + const("ky" + tag, shift) * pltpu.roll(v, shift, 1)
            return acc

        def along_z(tag, v):
            level = FINE if tag == "f" else MID
            n, p = level.planes, level.points
            parts = [v[SUB * i : SUB * i + SUB] for i in range(n)]
            low = mix_even_odd(level.khat, parts[:p])
            high = mix_even_odd(level.khat, parts[p - 1 :])
            first = s["dz" + tag][0:SUB, :]
            second = s["dz" + tag][level.rows - SUB : level.rows, :]
            out = [first * t for t in low[: p - 1]]
            out.append(first * low[p - 1] + second * high[0])
            out += [second * t for t in high[1:]]
            return out

        def faces(tag, name):
            level = FINE if tag == "f" else MID
            n, p, top = level.planes, level.points, level.rows - SUB
            src, dst, dz = s[name + tag], s["l" + tag], s["dz" + tag]
            mass_row, _ = CONSTS.at["mz" + tag]
            has = (has_lo.astype(jnp.float32), has_hi.astype(jnp.float32))
            ends = (0, p - 1)
            even_row = 0.5 * (level.khat[0:1] + level.khat[0:1, ::-1])[:, : p // 2]
            odd_row = 0.5 * (level.khat[0:1] - level.khat[0:1, ::-1])[:, : p // 2]
            x_edge = {}
            for side, row in ((0, 0), (1, top)):
                rows = slice(row, row + SUB)
                v = src[:, rows, :]
                yt = along_y(tag, v)
                xt = mix_even_odd(level.khat, [v[a] for a in range(p)])
                plane0 = 0 if side == 0 else p - 1
                zt = mix(
                    level.khat[p - 1 : p] if side else level.khat[0:1],
                    [
                        src[:, SUB * (plane0 + c) : SUB * (plane0 + c) + SUB, :]
                        for c in range(p)
                    ],
                )[0]
                weight = dz[rows, :]
                out = [weight * (xt[a] + yt[a] + zt[a]) + SHIFT_MASS * v[a] for a in range(p)]
                for a in range(1, p - 1):
                    dst[a, rows, :] = out[a]
                for f, a in enumerate(ends):
                    x_edge[f, side] = xt[a]
                    out[a] = (
                        out[a]
                        + s["side"][2 * f + side] * (zt[a] + yt[a])
                        + (SHIFT_MASS * has[f]) * v[a]
                    )
                put(s["sz" + tag], side, pack(tag, out))
            start_faces(tag, Z_DIRS)
            chunk = 5 if tag == "f" else n
            for z0 in range(0, n, chunk):
                rows = slice(SUB * z0, SUB * (z0 + chunk))
                v = [src[a, rows, :] for a in range(p)]
                even = mix(even_row, [v[i] + v[p - 1 - i] for i in range(p // 2)])[0]
                odd = mix(odd_row, [v[i] - v[p - 1 - i] for i in range(p // 2)])[0]
                for f, xt in ((0, even + odd), (1, even - odd)):
                    u = v[ends[f]]
                    yt = along_y(tag, u.reshape(chunk, SUB, LANES)).reshape(chunk * SUB, LANES)
                    mass = s["cst"][mass_row + SUB * z0 : mass_row + SUB * (z0 + chunk), :]
                    dst[ends[f], rows, :] = dz[rows, :] * (xt + yt) + mass * u
            for f, a in enumerate(ends):
                out = along_z(tag, src[a])
                out = [t + dst[a, SUB * z : SUB * z + SUB, :] for z, t in enumerate(out)]
                put(dst, a, out)
                out[0] = out[0] + s["side"][4] * x_edge[f, 0]
                out[-1] = out[-1] + s["side"][5] * x_edge[f, 1]
                put(s["sx" + tag], f, pack(tag, out))
            start_faces(tag, X_DIRS)

        def interior(tag, name, after=None):
            level = FINE if tag == "f" else MID
            n, p = level.planes, level.points
            src, dst = s[name + tag], s["l" + tag]

            def plane(z):
                rows = plane_rows(z)
                v = src[:, rows, :]
                acc = along_y(tag, v[1 : p - 1])
                along_x = mix_even_odd(level.khat, [v[a] for a in range(p)])
                weight = s["dz" + tag][rows, :]
                if isinstance(z, int):
                    mass = 2.0 * SHIFT_MASS if z == p - 1 else SHIFT_MASS
                else:
                    mass = jnp.where(z == p - 1, 2.0 * SHIFT_MASS, SHIFT_MASS)
                for a in range(1, p - 1):
                    dst[a, rows, :] = weight * (acc[a - 1] + along_x[a]) + mass * v[a]

            each(tag, 1, n - 1, plane)

            def line(a):
                out = along_z(tag, src[a])
                for i in range(1, n - 1):
                    dst[a, SUB * i : SUB * i + SUB, :] += out[i]
                if after is not None:
                    after(a)

            each(tag, 1, p - 1, line)

        def apply(tag, name):
            level = FINE if tag == "f" else MID
            n, p = level.planes, level.points
            src, dst = s[name + tag], s["l" + tag]

            def plane(z):
                rows = plane_rows(z)
                v = src[:, rows, :]
                acc = along_y(tag, v)
                along_x = mix_even_odd(level.khat, [v[a] for a in range(p)])
                weight = s["dz" + tag][rows, :]
                mass = jnp.where(z == p - 1, 2.0 * SHIFT_MASS, SHIFT_MASS)
                for a in range(p):
                    dst[a, rows, :] = weight * (acc[a] + along_x[a]) + mass * v[a]

            loop(0, n, plane)

            def line(a):
                out = along_z(tag, src[a])
                for i in range(n):
                    dst[a, SUB * i : SUB * i + SUB, :] += out[i]

            loop(0, p, line)

        def update(tag, kind, c1=0.0, c2=0.0, last=False, residual="r"):
            level = FINE if tag == "f" else MID
            c = float(1.0 / level.theta)
            l, rhs, inv, x, r, d = (s[k + tag] for k in ("l", "rhs", "inv", "x", "r", "d"))
            old = s[residual + tag]

            def on(*sel):
                if kind == "zero":
                    res = l[sel]
                    rhs[sel] = res
                    upd = c * inv[sel] * res
                    d[sel] = upd
                    x[sel] = upd
                elif kind == "first":
                    res = rhs[sel] - l[sel]
                    r[sel] = res
                    upd = c * inv[sel] * res
                    d[sel] = upd
                    x[sel] = x[sel] + upd
                else:
                    res = old[sel] - l[sel]
                    upd = c1 * d[sel] + c2 * inv[sel] * res
                    if not last:
                        r[sel] = res
                        d[sel] = upd
                    x[sel] = x[sel] + upd

            return on

        def inner_update(tag, on):
            level = FINE if tag == "f" else MID

            def one(a):
                sum_y(tag, a, 1, level.planes - 2)
                on(a, slice(SUB, level.rows - SUB))

            return one

        def face_update(tag, on):
            level = FINE if tag == "f" else MID
            add_faces(tag)
            for a in (0, level.points - 1):
                sum_y(tag, a)
                on(a, slice(0, level.rows))
            for row in (0, level.rows - SUB):
                sum_y_planes(tag, row, slice(1, level.points - 1))
                on(slice(1, level.points - 1), slice(row, row + SUB))

        def raw_start_x(tag):
            level = FINE if tag == "f" else MID
            buf = s["l" + tag]
            start_faces(tag, EDGE_DIRS)
            for f, a in ((0, 0), (1, level.points - 1)):
                parts = [buf[a, SUB * z : SUB * z + SUB, :] for z in range(level.planes)]
                put(s["sx" + tag], f, pack(tag, parts))
            start_faces(tag, X_DIRS)

        def raw_start_z(tag):
            level = FINE if tag == "f" else MID
            buf, top = s["l" + tag], level.rows - SUB
            for side, row in ((0, 0), (1, top)):
                parts = [buf[a, row : row + SUB, :] for a in range(level.points)]
                put(s["sz" + tag], side, pack(tag, parts))
            start_faces(tag, Z_DIRS)

        def raw_finish(tag, on, before_faces, before_edges):
            level = FINE if tag == "f" else MID
            buf, last, top = s["l" + tag], level.points - 1, level.rows - SUB
            each(tag, 1, last, inner_update(tag, on))
            before_faces()
            par = add_faces(tag)
            for a in (0, last):
                sum_y(tag, a, 1, level.planes - 2)
                on(a, slice(SUB, top))
            for row in (0, top):
                sum_y_planes(tag, row, slice(1, last))
                on(slice(1, last), slice(row, row + SUB))
            before_edges()
            wait_some(lambda i: face_copy(tag, par, i), EDGE_DIRS)
            for k, (a, row) in enumerate(((0, 0), (0, top), (last, 0), (last, top))):
                rows = slice(row, row + SUB)
                buf[a, rows, :] += jnp.where(has_lo if a == 0 else has_hi, s["rc" + tag][par, k], 0.0)
                sum_y_planes(tag, row, a)
                on(a, rows)

        def steps(tag, count, residual, between, done=0):
            coefs = (FINE if tag == "f" else MID).steps(count)
            for index, (c1, c2) in enumerate(coefs):
                if index < done:
                    continue
                on = update(tag, "next", c1, c2, index == count - 2, residual)
                residual = "r"
                faces(tag, "d")
                interior(tag, "d", inner_update(tag, on))
                between[index]()
                face_update(tag, on)

        ones = [has_lo.astype(jnp.float32), 1.0, has_hi.astype(jnp.float32)]
        copies = [1.0 + ones[0], 1.0, 1.0 + ones[2]]
        def spread_row(row):
            return jnp.broadcast_to(row, (SUB, LANES))

        def patch_row(dx, k):
            dz, row = ((-1, 1), (0, 0), (0, 1), (1, 0))[k]
            ref = s["dsrc"] if (dx, dz) == (0, 0) else s["dhalo"].at[DIRS.index((dx, dz))]
            value = spread_row(ref[row : row + 1, :])
            if dx != 0:
                value = jnp.where(has_lo if dx < 0 else has_hi, value, 0.0)
            return value

        def patch(dx):
            return [patch_row(dx, k) for k in range(4)]

        def kinds_of(q):
            return [q[0] + q[1], q[1], q[1] + q[2], q[2], q[2] + q[3]]

        def kind_of(z, p):
            return {0: 0, p - 1: 2, 2 * p - 2: 4}.get(z, 1 if z < p else 3)

        def nodal(k, p):
            lo = k + jnp.where(lane > 0, pltpu.roll(k, 1, 1), 0.0)
            hi = k + jnp.where(lane < LANES - 1, pltpu.roll(k, LANES - 1, 1), 0.0)
            return jnp.where(sub == 0, lo, jnp.where(sub == p - 1, hi, k))

        def set_inverse(tag, level, a, xc, rows):
            row_k, _ = CONSTS.at["kzb" + tag]
            row_c, _ = CONSTS.at["cnt" + tag]
            kzb = s["cst"][row_k + rows.start : row_k + rows.stop, :]
            cnt = s["cst"][row_c + rows.start : row_c + rows.stop, :]
            diag = (float(level.kdiag[a]) + kzb) * s["cls" + tag][xc, rows, :]
            s["inv" + tag][a, rows, :] = 1.0 / (diag + copies[xc] * cnt)

        def set_class(tag, level, xc, kind, value):
            full = nodal(value, level.points)
            for z in range(level.planes):
                if kind_of(z, level.points) == kind:
                    s["cls" + tag][xc, SUB * z : SUB * z + SUB, :] = full

        def diagonals_inside(tag, level):
            first, second = patch_row(0, 1), patch_row(0, 2)
            kinds = [first, first, first + second, second, second]
            for z in range(level.planes):
                s["dz" + tag][SUB * z : SUB * z + SUB, :] = kinds[kind_of(z, level.points)]
            for kind in (1, 2, 3):
                set_class(tag, level, 1, kind, kinds[kind])
            for a in range(1, level.points - 1):
                set_inverse(tag, level, a, 1, slice(SUB, level.rows - SUB))

        def diagonals_x(tag, level):
            for xc, dx, a in ((0, -1, 0), (2, 1, level.points - 1)):
                first = patch_row(0, 1) + patch_row(dx, 1)
                second = patch_row(0, 2) + patch_row(dx, 2)
                for kind, value in ((1, first), (2, first + second), (3, second)):
                    set_class(tag, level, xc, kind, value)
                set_inverse(tag, level, a, xc, slice(SUB, level.rows - SUB))

        def diagonals_z(tag, level):
            set_class(tag, level, 1, 0, patch_row(0, 0) + patch_row(0, 1))
            set_class(tag, level, 1, 4, patch_row(0, 2) + patch_row(0, 3))
            for a in range(1, level.points - 1):
                set_inverse(tag, level, a, 1, slice(0, SUB))
                set_inverse(tag, level, a, 1, slice(level.rows - SUB, level.rows))

        def diagonals_edges(tag, level):
            for xc, dx, a in ((0, -1, 0), (2, 1, level.points - 1)):
                q = [u + v for u, v in zip(patch(0), patch(dx))]
                set_class(tag, level, xc, 0, q[0] + q[1])
                set_class(tag, level, xc, 4, q[2] + q[3])
                set_inverse(tag, level, a, xc, slice(0, SUB))
                set_inverse(tag, level, a, xc, slice(level.rows - SUB, level.rows))

        def side_diffusivity():
            q = [patch(-1), patch(0), patch(1)]
            for side in range(2):
                s["side"][side] = q[0][1 + side]
                s["side"][2 + side] = q[2][1 + side]
                s["side"][4 + side] = q[1][3 * side]

        def restrict_fine():
            def line(a):
                res = s["locf"][a] - s["lf"][a]
                parts = [res[SUB * i : SUB * i + SUB] for i in range(FINE.planes)]
                for i, t in enumerate(mix(R73Z.T, parts)):
                    s["tmpf"][a, SUB * i : SUB * i + SUB, :] = t

            loop(0, PF, line)

            def plane(z):
                rows = plane_rows(z)
                v = s["tmpf"][:, rows, :]
                t = jnp.stack(mix(R73, [v[a] for a in range(PF)]))
                acc = const("r73", 0) * t
                for shift in range(1, SUB):
                    acc = acc + const("r73", shift) * pltpu.roll(t, shift, 1)
                s["locm"][:, rows, :] = acc
                s["lm"][:, rows, :] = acc

            each("m", 0, MID.planes, plane)

        def prolong_fine():
            def plane(z):
                rows = plane_rows(z)
                v = s["xm"][:, rows, :]
                acc = const("j73", 0) * v
                for shift in range(1, SUB):
                    acc = acc + const("j73", shift) * pltpu.roll(v, shift, 1)
                for a, t in enumerate(mix(J73, [acc[i] for i in range(PM)])):
                    s["tmpf"][a, rows, :] = t

            each("m", 0, MID.planes, plane)

            def line(a):
                v = s["tmpf"][a]
                parts = [v[SUB * i : SUB * i + SUB] for i in range(MID.planes)]
                for i, t in enumerate(mix(J73Z, parts)):
                    s["xf"][a, SUB * i : SUB * i + SUB, :] += t

            loop(0, PF, line)

        def restrict_mid():
            for a in range(PM):
                res = s["locm"][a] - s["lm"][a]
                parts = [res[SUB * i : SUB * i + SUB] for i in range(MID.planes)]
                for i, t in enumerate(mix(R31Z.T, parts)):
                    s["tmpm"][a, SUB * i : SUB * i + SUB, :] = t
            spare = jnp.zeros((SUB, LANES), jnp.float32)
            for z in range(3):
                v = s["tmpm"][:, SUB * z : SUB * z + SUB, :]
                for a, t in enumerate(mix(R31, [v[i] for i in range(PM)])):
                    acc = const("r31", 0) * t
                    for shift in (1, 5, 6, 7):
                        acc = acc + const("r31", shift) * pltpu.roll(t, shift, 0)
                    up = pltpu.roll(pltpu.roll(acc, 1, 1), SUB - 1, 0)
                    node_row = acc + jnp.where(lane > 0, up, 0.0)
                    s["ga"][dev, 3 * a + z : 3 * a + z + 1, :] = node_row[0:1, :]
                    spare = spare + jnp.where(lane == z * nx + dev + a, up[0:1, 0:1], 0.0)
            s["ga"][dev, 6:7, :] = spare[0:1, :]
            s["ga"][dev, 7:8, :] = jnp.zeros((1, LANES), jnp.float32)

        def sum_x_low():
            flat = s["ga"]
            g = jnp.zeros((low_rows, LANES), jnp.float32)
            pad = lambda rows, before: jnp.pad(
                rows, ((before, low_rows - before - rows.shape[0]), (0, 0))
            )
            mine = s["gb"].at[
                pl.ds(pl.multiple_of(low_rows + node * low_rows, low_rows), low_rows)
            ]
            mine[...] = g
            for z in range(3):
                mine[z * nx : z * nx + n_dev, :] = flat[:, z, :]
                mine[z * nx + 1 : z * nx + nx, :] += flat[:, 3 + z, :]
            mine[3 * nx : 3 * nx + 1, :] = jnp.sum(flat[:, 6, :], axis=0, keepdims=True)

        low_lane = lax.broadcasted_iota(jnp.int32, (nz, LANES), 1)
        LAST = LANES - 1

        def ahead(v):
            return jnp.where(low_lane > 0, pltpu.roll(v, 1, 1), 0.0)

        def to_end(x, v):
            return jnp.where(low_lane == x, pltpu.roll(v, x + 1, 1), 0.0)

        def low_weights():
            up_z = lambda v: pltpu.roll(v, 1, 0)
            elem = lambda x: s["db"][pl.ds(x, nz, stride=n_dev), :]
            zero = jnp.zeros((nz, LANES), jnp.float32)
            y_copies = jnp.where(low_lane > 0, 2.0, 1.0)
            end_wx = end_wy = end_wz = zero
            for x in range(nx):
                lo = elem(x - 1) if x > 0 else zero
                hi = elem(x) if x < n_dev else zero
                both = lo + hi
                wy = 0.5 * (both + up_z(both))
                wym = ahead(wy)
                wz = 0.5 * (both + ahead(both))
                wzm = up_z(wz)
                hz = hi + up_z(hi)
                wx = 0.5 * (hz + ahead(hz))
                wxm = s["c_wx"][x - 1] if x > 0 else zero
                s["c_wy"][x] = wy
                s["c_wym"][x] = wym
                s["c_wz"][x] = wz
                s["c_wzm"][x] = wzm
                s["c_wx"][x] = wx
                x_copies = 1.0 if x in (0, n_dev) else 2.0
                s["c_dg"][x] = wx + wxm + wy + wym + wz + wzm + 2.0 * SHIFT_MASS * x_copies * y_copies
                end_wx = end_wx + to_end(x, 0.5 * hz)
                end_wy = end_wy + to_end(x, wy)
                end_wz = end_wz + to_end(x, 0.5 * both)
            end_wxm, end_wzm = ahead(end_wx), up_z(end_wz)
            x_copies = jnp.where((low_lane == 0) | (low_lane == n_dev), 1.0, 2.0)
            x_copies = jnp.where(low_lane < nx, x_copies, 0.0)
            s["c_wx"][nx] = end_wx
            s["c_wxm"][...] = end_wxm
            s["c_wy"][nx] = end_wy
            s["c_wz"][nx] = end_wz
            s["c_wzm"][nx] = end_wzm
            s["c_dg"][nx] = (
                end_wx + end_wxm + end_wy + end_wz + end_wzm + 2.0 * SHIFT_MASS * x_copies
            )

        def low_rhs():
            buf = s["gb"]
            buf[0:low_rows, :] = buf[n_node * low_rows : (n_node + 1) * low_rows, :]
            own = lambda row: buf[pl.ds(low_rows + row, n_node, stride=low_rows), :]
            before = lambda row: buf[pl.ds(row, n_node, stride=low_rows), :]
            at = lax.broadcasted_iota(jnp.int32, (n_node, LANES), 1)
            spare, spare_before = own(3 * nx), before(3 * nx)

            def pick(rows, first):
                moved = rows if first == 0 else pltpu.roll(rows, LANES - first, 1)
                return jnp.where(at < nx, moved, 0.0)

            even, odd = pl.ds(0, n_node, stride=2), pl.ds(1, n_node, stride=2)
            res, main = s["c_cr"], s["c_main"]
            for x in range(nx):
                main[even, :] = own(x) + before(2 * nx + x)
                main[odd, :] = own(nx + x)
                res[x] = main[...]
            main[even, :] = pick(spare, 0) + pick(spare_before, 2 * nx)
            main[odd, :] = pick(spare, nx)
            res[nx] = main[...]

        def fold(v):
            parts = [v[i : i + SUB] for i in range(0, v.shape[0], SUB)]
            while len(parts) > 1:
                parts = [u + w for u, w in zip(parts[::2], parts[1::2])] + (
                    [parts[-1]] if len(parts) % 2 else []
                )
            return parts[0]

        def total(v):
            return jnp.sum(v, axis=(0, 1), keepdims=True)

        def set_direction(x, value):
            p = s["c_p"]
            p[x, SUB : SUB + nz, :] = value
            p[x, 0:SUB, :] = value[nz - SUB : nz]
            p[x, SUB + nz : 2 * SUB + nz, :] = value[0:SUB]

        def coarse_solve():
            p, q, res, sol = s["c_p"], s["c_cq"], s["c_cr"], s["c_cx"]
            here = pl.ds(SUB, nz)
            norm = jnp.zeros((SUB, LANES), jnp.float32)
            for x in range(nx + 1):
                v = res[x]
                set_direction(x, v)
                sol[x] = jnp.zeros_like(v)
                norm = norm + fold(v * v)

            def along_pipe(x):
                out = s["c_wz"][x] * p[x, SUB + 1 : SUB + 1 + nz, :]
                return out + s["c_wzm"][x] * p[x, SUB - 1 : SUB - 1 + nz, :]

            def step_length(now):
                dot = jnp.zeros((SUB, LANES), jnp.float32)
                end = p[nx, here, :]
                last = jnp.zeros((nz, LANES), jnp.float32)
                for x in range(nx):
                    v = p[x, here, :]
                    out = s["c_dg"][x] * v
                    if x > 0:
                        out = out - s["c_wx"][x - 1] * p[x - 1, here, :]
                    if x < nx - 1:
                        out = out - s["c_wx"][x] * p[x + 1, here, :]
                    above = jnp.where(
                        low_lane == LAST, pltpu.roll(end, LAST - x, 1), pltpu.roll(v, LAST, 1)
                    )
                    below = pltpu.roll(v, 1, 1)
                    out = out - s["c_wy"][x] * above - s["c_wym"][x] * below
                    out = out - along_pipe(x)
                    q[x] = out
                    dot = dot + fold(v * out)
                    last = jnp.where(low_lane == x, pltpu.roll(v, x + 1, 1), last)
                out = s["c_dg"][nx] * end - s["c_wx"][nx] * pltpu.roll(end, LAST, 1)
                out = out - s["c_wxm"][...] * pltpu.roll(end, 1, 1)
                out = out - s["c_wy"][nx] * last - along_pipe(nx)
                q[nx] = out
                dot = dot + fold(end * out)
                return now / total(dot)

            def iteration(_, now):
                alpha = step_length(now)
                norm = jnp.zeros((SUB, LANES), jnp.float32)
                for x in range(nx + 1):
                    sol[x] += alpha * p[x, here, :]
                    v = res[x] - alpha * q[x]
                    res[x] = v
                    norm = norm + fold(v * v)
                new = total(norm)
                beta = new / now
                for x in range(nx + 1):
                    set_direction(x, res[x] + beta * p[x, here, :])
                return new

            alpha = step_length(lax.fori_loop(0, COARSE_ITERS - 1, iteration, total(norm)))
            for x in range(nx + 1):
                sol[x] += alpha * p[x, here, :]

        n3, edge_slope = MID.planes, float((MID.khat @ J31)[0, 0])

        def stacked(parts):
            return jnp.stack(list(parts))

        def exists(o):
            return (dev + o >= 0) & (dev + o < n_dev)

        def diff_at(o, k):
            x = jnp.clip(dev + o, 0, n_dev - 1)
            z = lax.rem(2 * node + k + nz, nz)
            row = spread_row(s["db"][pl.ds(z * n_dev + x, 1), :])
            return row if o == 0 else jnp.where(exists(o), row, 0.0)

        def over_planes(q):
            kinds = kinds_of(q)
            return stacked(kinds[kind_of(z, PM)] for z in range(n3))

        def column(o):
            return [diff_at(o, k) for k in (-1, 0, 1, 2)]

        def add_rows(p, q):
            return [u + v for u, v in zip(p, q)]

        def copies_at(o, a):
            if a == 0:
                return 1.0 + exists(o - 1).astype(jnp.float32)
            if a == PM - 1:
                return 1.0 + exists(o + 1).astype(jnp.float32)
            return 1.0

        def around(o, a):
            q = column(o)
            if a == 0:
                q = add_rows(q, column(o - 1))
            if a == PM - 1:
                q = add_rows(q, column(o + 1))
            return q

        def spread_low(i, k):
            x = jnp.clip(dev + i, 0, n_dev)
            z = lax.rem(2 * node + k + nz, nz)
            low = spread_row(s["c_cx"][x, pl.ds(z, 1), :])
            end = pltpu.roll(spread_row(s["c_cx"][nx, pl.ds(z, 1), :]), LAST - x, 1)
            high = jnp.where(lane < LAST, pltpu.roll(low, LAST, 1), end)
            return const("j31", 0) * low + const("j31", 1) * high

        def once(fn):
            seen = {}

            def get(*key):
                if key not in seen:
                    seen[key] = fn(*key)
                return seen[key]

            return get

        def y_summed(v):
            across, along = v.ndim - 1, v.ndim - 2
            up = pltpu.roll(pltpu.roll(v, 1, across), SUB - PM + 1, along)
            down = pltpu.roll(pltpu.roll(v, LANES - 1, across), PM - 1, along)
            v = v + jnp.where((sub == 0) & (lane > 0), up, 0.0)
            return v + jnp.where((sub == PM - 1) & (lane < LANES - 1), down, 0.0)

        def low_tools():
            node_at = once(spread_low)
            line_at = once(lambda i: stacked(mix(J31Z, [node_at(i, k) for k in (0, 1, 2)])))
            mass = const("mzfull").reshape(n3, SUB, LANES)
            h = edge_slope

            def along_line(o, a):
                pick = lambda f: mix(J31[a : a + 1], [f(o), f(o + 1)])[0]
                u = pick(line_at)
                before, after = pick(lambda i: node_at(i, -1)), pick(lambda i: node_at(i, 3))
                w = around(o, a)
                out = over_planes(w) * along_y("m", u) + copies_at(o, a) * mass * u
                f0, f1 = w[0] * (u[0] - before), w[1] * (u[PM - 1] - u[0])
                f2, f3 = w[2] * (u[n3 - 1] - u[PM - 1]), w[3] * (after - u[n3 - 1])
                zero = jnp.zeros((SUB, LANES), jnp.float32)
                flow = [zero] * n3
                flow[0], flow[PM - 1], flow[n3 - 1] = f0 - f1, f1 - f2, f2 - f3
                out = out + h * stacked(flow)
                if a in (0, PM - 1):
                    inner = line_at(o + 1) if a == 0 else line_at(o)
                    outer_o = o - 1 if a == 0 else o + 1
                    outer = line_at(o - 1) if a == 0 else line_at(o + 2)
                    out = out + h * (
                        over_planes(column(o)) * (u - inner)
                        + over_planes(column(outer_o)) * (u - outer)
                    )
                return u, out

            def beyond_z(side, c):
                k = -1 if side == 0 else 2
                far = c == (0 if side == 0 else PM - 1)
                other = k - 1 if side == 0 else k + 1
                at_x = once(lambda i: mix(J31[c : c + 1], [node_at(i, k), node_at(i, k + 1)])[0])
                across = lambda kk: stacked(mix(J31, [node_at(0, kk), node_at(1, kk)]))
                weights = once(lambda o: diff_at(o, k) + diff_at(o, other) if far else diff_at(o, k))
                u = stacked(mix(J31, [at_x(0), at_x(1)]))
                sums = lambda f: stacked(
                    [f(0) + f(-1), f(0), f(0), f(0) + f(1)]
                )
                total_w = sums(weights)
                copies3 = [copies_at(0, a) * (2.0 if far else 1.0) * SHIFT_MASS for a in range(PM)]
                out = total_w * along_y("m", u) + stacked(copies3[a] * u[a] for a in range(PM))
                zero = jnp.zeros((SUB, LANES), jnp.float32)
                flow = [zero] * PM
                flow[0] = weights(-1) * (u[0] - at_x(-1)) + weights(0) * (u[0] - u[PM - 1])
                flow[PM - 1] = weights(0) * (u[PM - 1] - u[0]) + weights(1) * (u[PM - 1] - at_x(2))
                out = out + h * stacked(flow)
                if far:
                    inner, outer = (across(k + 1), across(k - 1)) if side == 0 else (
                        across(k),
                        across(k + 2),
                    )
                    out = out + h * (
                        sums(lambda o: diff_at(o, k)) * (u - inner)
                        + sums(lambda o: diff_at(o, other)) * (u - outer)
                    )
                return out

            return along_line, beyond_z

        beyond_x = ((-1, (0, 1, 2), MID.khat[PM - 1]), (1, (1, 2, 3), MID.khat[0]))
        beyond_c = (((0, 1, 2), MID.khat[PM - 1]), ((1, 2, 3), MID.khat[0]))

        def ghost_diagonals():
            theta = MID.theta
            my = 1.0 + jnp.where(((sub == 0) & (lane > 0)) | ((sub == PM - 1) & (lane < LAST)), 1.0, 0.0)
            kb = mirrored_rows(MID.kdiag)
            kz = [float(v) for v in np.concatenate([MID.kdiag, MID.kdiag[1:]])]
            for side, (o, points, row) in enumerate(beyond_x):
                for index, a in enumerate(points):
                    kinds = [nodal(k, PM) for k in kinds_of(around(o, a))]
                    for z in range(n3):
                        diag = (float(MID.kdiag[a]) + kz[z] + kb) * kinds[kind_of(z, PM)]
                        diag = diag + (float(MID_COPIES[z]) * SHIFT_MASS * copies_at(o, a)) * my
                        s["ghost_x"][side, index, z] = float(row[a] / theta) / diag
            for side, (planes, row) in enumerate(beyond_c):
                k = -1 if side == 0 else 2
                other = k - 1 if side == 0 else k + 1
                for index, c in enumerate(planes):
                    far = c in (0, PM - 1)
                    weights = lambda o: diff_at(o, k) + diff_at(o, other) if far else diff_at(o, k)
                    for a in range(PM):
                        w = weights(0)
                        if a in (0, PM - 1):
                            w = w + weights(-1 if a == 0 else 1)
                        diag = (float(MID.kdiag[a] + MID.kdiag[c]) + kb) * nodal(w, PM)
                        scale = (2.0 if far else 1.0) * SHIFT_MASS * copies_at(0, a)
                        s["ghost_z"][side, index, a] = float(row[c] / theta) / (diag + scale * my)

        def mirrored_rows(values):
            out = jnp.zeros((SUB, LANES), jnp.float32)
            for i, v in enumerate(values):
                out = jnp.where(sub == i, float(v), out)
            return out

        def send_known_part():
            c = float(1.0 / MID.theta)
            for a in range(PM):
                sum_y("m", a)
                res = s["rhsm"][a] - s["lm"][a]
                s["rm"][a] = res
                s["dm"][a] = c * s["invm"][a] * res
            plane = lambda z: s["dm"][:, SUB * z : SUB * z + SUB, :]
            for side, (points, row) in enumerate(((range(1, PM), 0), (range(PM - 1), PM - 1))):
                rows = [s["dm"][a] for a in points]
                t = mix(MID.khat[row : row + 1, list(points)], rows)[0]
                put(s["sxm"], side, pack("m", [t[SUB * z : SUB * z + SUB] for z in range(n3)]))
                first = 0 if side == 0 else PM - 1
                t = mix(MID.khat[row : row + 1, list(points)], [plane(first + c) for c in points])[0]
                put(s["szm"], side, pack("m", [t[a] for a in range(PM)]))
            start_faces("m", X_DIRS + Z_DIRS)

        def after_coarse(c1, c2):
            c = float(1.0 / MID.theta)
            along_line, beyond_z = low_tools()
            shape = (n3, SUB, LANES)
            flat = (MID.rows, LANES)
            par = parity["m"]
            parity["m"] = 1 - par
            for a in range(PM):
                u, rho = along_line(0, a)
                res = s["rm"][a] - y_summed(rho).reshape(flat)
                upd = c * s["invm"][a] * res
                s["rm"][a] = res
                s["dm"][a] = upd
                s["xm"][a] = s["xm"][a] + u.reshape(flat) + upd
            for side, (o, points, row) in enumerate(beyond_x):
                acc = None
                for index, a in enumerate(points):
                    _, rho = along_line(o, a)
                    t = s["ghost_x"][side, index] * y_summed(rho)
                    acc = t if acc is None else acc + t
                s["tmpf"][side] = acc.reshape(flat)
            for side, (planes, row) in enumerate(beyond_c):
                acc = None
                for index, cc in enumerate(planes):
                    t = s["ghost_z"][side, index] * y_summed(beyond_z(side, cc))
                    acc = t if acc is None else acc + t
                s["tmpf"][2 + side, 0 : PM * SUB, :] = acc.reshape(PM * SUB, LANES)
            wait_some(lambda i: face_copy("m", par, i), X_DIRS + Z_DIRS)
            d = [s["dm"][a].reshape(shape) for a in range(PM)]
            own_x = mix_even_odd(MID.khat, d)
            last = float(MID.khat[PM - 1, PM - 1])
            terms_x = []
            for side, a in ((0, 0), (1, PM - 1)):
                t = stacked(unpack("m", s["rxm"][par, side], n3)) - s["tmpf"][side].reshape(shape)
                terms_x.append(t + last * d[a])
            terms_z = []
            for side, z in ((0, 0), (1, n3 - 1)):
                t = stacked(unpack("m", s["rzm"][par, side], PM))
                t = t - s["tmpf"][2 + side, 0 : PM * SUB, :].reshape(PM, SUB, LANES)
                terms_z.append(t + last * stacked(v[z] for v in d))
            mass = const("mzfull").reshape(shape)
            here = over_planes(column(0))
            for a in range(PM):
                w = around(0, a)
                out = over_planes(w) * along_y("m", d[a]) + copies_at(0, a) * mass * d[a]
                out = out + here * own_x[a]
                if a == 0:
                    out = out + over_planes(column(-1)) * terms_x[0]
                if a == PM - 1:
                    out = out + over_planes(column(1)) * terms_x[1]
                low = mix_even_odd(MID.khat, [d[a][z] for z in range(PM)])
                high = mix_even_odd(MID.khat, [d[a][z] for z in range(PM - 1, n3)])
                along = [w[1] * v for v in low] + [w[2] * v for v in high[1:]]
                along[PM - 1] = along[PM - 1] + w[2] * high[0]
                along[0] = along[0] + w[0] * terms_z[0][a]
                along[n3 - 1] = along[n3 - 1] + w[3] * terms_z[1][a]
                out = y_summed(out + stacked(along)).reshape(flat)
                res = s["rm"][a] - out
                upd = c1 * s["dm"][a] + c2 * s["invm"][a] * res
                s["lm"][a] = res
                s["locm"][a] = upd
            for a in range(PM):
                s["rm"][a] = s["lm"][a]
                s["dm"][a] = s["locm"][a]
                s["xm"][a] = s["xm"][a] + s["locm"][a]

        nothing = lambda: None
        load_diff.wait()
        s["da"][dev] = s["dsrc"][...]
        wz = np.concatenate([FINE.w, FINE.w[1:]])

        def mirrored(index, values):
            out = jnp.float32(values[0])
            for i in range(1, PF // 2):
                out = jnp.where((index == i) | (index == PF - 1 - i), float(values[i]), out)
            return out

        across_y = mirrored(sub, 1.0 / FINE.w)

        def load_line(a):
            planes = []
            for e in range(2):
                for c in range(PF):
                    start = a * chunk + 2 * c + e
                    planes.append(s["ein"][pl.ds(start, SUB, stride=2 * PF), :])
            merged = planes[: PF - 1] + [planes[PF - 1] + planes[PF]] + planes[PF + 1 :]
            scale = across_y * mirrored(jnp.int32(a), 1.0 / FINE.w)
            for z, v in enumerate(merged):
                t = scale * v * float(1.0 / wz[z])
                s["locf"][a, SUB * z : SUB * z + SUB, :] = t
                s["lf"][a, SUB * z : SUB * z + SUB, :] = t

        for a in (0, PF - 1):
            load_in(a).wait()
            load_line(a)
        wait_barrier()
        start_some(halo_copy, range(8))
        raw_start_x("f")
        for a in range(1, PF - 1):
            load_in(a).wait()
        loop(1, PF - 1, load_line)
        raw_start_z("f")
        load_cst.wait()
        diagonals_inside("f", FINE)
        diagonals_inside("m", MID)

        def halo_sides():
            start_a("d")
            wait_some(halo_copy, X_DIRS)
            diagonals_x("f", FINE)
            wait_some(halo_copy, Z_DIRS)
            diagonals_z("f", FINE)

        def halo_edges():
            wait_some(halo_copy, EDGE_DIRS)
            diagonals_edges("f", FINE)

        def diff_stage_b():
            wait_a("d")
            mine = slot("d", node)
            for e in range(2):
                mine[e * n_dev : (e + 1) * n_dev, :] = s["da"][:, e, :]
            start_b("d")

        raw_finish("f", update("f", "zero"), halo_sides, halo_edges)
        side_diffusivity()
        steps("f", SMOOTH_FINE, "rhs", [diff_stage_b, lambda: forward_b("d")])
        apply("f", "x")
        restrict_fine()

        raw_start_x("m")
        raw_start_z("m")

        def order3_faces():
            diagonals_x("m", MID)
            diagonals_z("m", MID)
            diagonals_edges("m", MID)
            wait_b("d")

        raw_finish("m", update("m", "zero"), order3_faces, nothing)
        steps("m", SMOOTH_MID, "rhs", [low_weights, ghost_diagonals])
        faces("m", "x")
        interior("m", "x")
        restrict_mid()
        start_a("g")
        add_faces("m")
        send_known_part()
        wait_a("g")
        sum_x_low()
        start_b("g")
        forward_b("g")
        wait_b("g")
        low_rhs()
        coarse_solve()
        coefs = MID.steps(SMOOTH_MID)
        after_coarse(*coefs[0])
        steps("m", SMOOTH_MID, "r", [nothing, nothing], 1)
        prolong_fine()
        first = update("f", "first")
        faces("f", "x")
        interior("f", "x", inner_update("f", first))
        face_update("f", first)
        steps("f", SMOOTH_FINE, "r", [nothing, nothing])

        def store_line(a):
            for e in range(2):
                for c in range(PF):
                    z = e * (PF - 1) + c
                    start = a * chunk + 2 * c + e
                    out_ref[pl.ds(start, SUB, stride=2 * PF), :] = s["xf"][
                        a, SUB * z : SUB * z + SUB, :
                    ]

        loop(0, PF, store_line)

    return kernel


def solution(mesh):
    n_node, n_dev = mesh.shape["node"], mesh.shape["dev"]
    shapes, low_rows = scratch_shapes(n_node, n_dev)
    kernel = make_kernel(n_node, n_dev, list(shapes), low_rows)
    rows = PF * PF * PF * 2

    def local(element_load, diffusivity):
        out = pl.pallas_call(
            kernel,
            out_shape=pltpu.VMEM((rows, LANES), jnp.float32),
            in_specs=[pl.BlockSpec(memory_space=pltpu.HBM)] * 3,
            out_specs=pl.BlockSpec(memory_space=pltpu.VMEM),
            scratch_shapes=list(shapes.values()),
            compiler_params=pltpu.CompilerParams(
                collective_id=0, has_side_effects=True, vmem_limit_bytes=48 * 1024 * 1024
            ),
        )(
            pltpu.with_memory_space_constraint(element_load.reshape(rows, LANES), pltpu.HBM),
            pltpu.with_memory_space_constraint(diffusivity.reshape(2, LANES), pltpu.HBM),
            pltpu.with_memory_space_constraint(jnp.asarray(CONSTS.array()), pltpu.HBM),
        )
        return out.reshape(element_load.shape)

    return jax.shard_map(
        local,
        mesh=mesh,
        in_specs=(P(None, None, None, "dev", "node", None), P("dev", "node", None)),
        out_specs=P(None, None, None, "dev", "node", None),
        check_vma=False,
    )
```

```python
import jax
import jax.numpy as jnp
import numpy as np
from jax import lax
from jax.experimental import pallas as pl
from jax.experimental.pallas import tpu as pltpu
from jax.sharding import PartitionSpec as P

PF = 8
PM = 4
PC = 2
SMOOTH_FINE = 3
SMOOTH_MID = 3
COARSE_ITERS = 5
SHIFT_MASS = 0.05
LANES = 128
SUB = 8
MESH = pl.DeviceIdType.MESH

def legendre_values(points, poly_order):
    columns = [points * 0.0 + 1.0, points]
    for degree in range(2, poly_order + 1):
        columns.append(
            ((2 * degree - 1) * points * columns[degree - 1] - (degree - 1) * columns[degree - 2])
            / degree
        )
    return np.stack(columns[: poly_order + 1], axis=1)


def largest_eigen(matrix):
    size_n = matrix.shape[0]
    vector = np.cos(2.7 * np.arange(size_n) + 0.3)
    for power_step in range(4000):
        vector = matrix @ vector
        vector = vector / np.sqrt(np.sum(vector * vector))
    return float(vector @ (matrix @ vector))


def gll_level(poly_order):
    point_count = poly_order + 1
    gll_nodes = np.cos(np.pi * np.arange(point_count) / poly_order)
    for newton_step in range(60):
        values = legendre_values(gll_nodes, poly_order)
        gll_nodes = gll_nodes - (gll_nodes * values[:, poly_order] - values[:, poly_order - 1]) / (
            point_count * values[:, poly_order]
        )
    gll_nodes = np.sort(gll_nodes)
    values = legendre_values(gll_nodes, poly_order)
    top_value = values[:, poly_order]
    weights = 2.0 / (poly_order * point_count * top_value**2)
    deriv_matrix = np.zeros((point_count, point_count))
    for row_index in range(point_count):
        for col_index in range(point_count):
            if row_index != col_index:
                deriv_matrix[row_index, col_index] = top_value[row_index] / (
                    top_value[col_index] * (gll_nodes[row_index] - gll_nodes[col_index])
                )
    deriv_matrix[0, 0] = -poly_order * point_count / 4.0
    deriv_matrix[poly_order, poly_order] = poly_order * point_count / 4.0
    stiffness = deriv_matrix.T @ (weights[:, None] * deriv_matrix)
    diag_ids = np.arange(point_count)
    stiff_diag = stiffness[diag_ids, diag_ids]
    diag_scale = 1.0 / np.sqrt(stiff_diag)
    eig_bound = largest_eigen(diag_scale[:, None] * stiffness * diag_scale[None, :])
    return (gll_nodes, weights, deriv_matrix, stiff_diag, eig_bound)


def interp_table(fine_nodes, coarse_nodes):
    interp_mat = np.ones((fine_nodes.shape[0], coarse_nodes.shape[0]))
    for col_index in range(coarse_nodes.shape[0]):
        for other_index in range(coarse_nodes.shape[0]):
            if other_index != col_index:
                interp_mat[:, col_index] *= (fine_nodes - coarse_nodes[other_index]) / (
                    coarse_nodes[col_index] - coarse_nodes[other_index]
                )
    return interp_mat


class Level:
    def __init__(self, points):
        nodes, w, deriv, stiff_diag, bound = gll_level(points - 1)
        self.points = points
        self.planes = 2 * points - 1
        self.rows = SUB * self.planes
        self.x_rows = SUB * (self.planes if points == SUB else -(-self.planes // 2))
        self.z_rows = SUB * (points if points == SUB else -(-points // 2))
        self.nodes = nodes
        self.w = w
        self.khat = (deriv.T @ (w[:, None] * deriv)) / w[:, None]
        self.kdiag = stiff_diag / w
        self.theta = 0.6 * bound
        self.delta = 0.5 * bound

    def steps(self, count):
        sig = self.theta / self.delta
        rho = 1.0 / sig
        out = []
        for _ in range(count - 1):
            rho_next = 1.0 / (2.0 * sig - rho)
            out.append((float(rho_next * rho), float(2.0 * rho_next / self.delta)))
            rho = rho_next
        return out


def roll_coefs(matrix):
    full = np.zeros((SUB, SUB))
    full[: matrix.shape[0], : matrix.shape[1]] = matrix
    i = np.arange(SUB)
    return [full[i, (i - s) % SUB] for s in range(SUB)]


def two_elements(matrix):
    n, m = matrix.shape
    out = np.zeros((2 * n - 1, 2 * m - 1))
    out[:n, :m] = matrix
    out[n - 1 :, m - 1 :] = matrix
    return out


def plane_sum(points):
    values = np.zeros((2 * points - 1,))
    values[:points] += 1
    values[points - 1 :] += 1
    return values


class Consts:
    def __init__(self):
        self.blocks = []
        self.at = {}
        self.row = 0

    def add(self, name, block):
        block = np.asarray(block, np.float64)
        if block.ndim == 1:
            block = np.broadcast_to(block[:, None], (block.shape[0], LANES))
        assert block.shape[0] % SUB == 0
        self.at[name] = (self.row, block.shape[0])
        self.blocks.append(block)
        self.row += block.shape[0]

    def array(self):
        return np.concatenate(self.blocks, 0).astype(np.float32)


FINE, MID, LOW = Level(PF), Level(PM), Level(PC)
J73 = interp_table(FINE.nodes, MID.nodes)
J31 = interp_table(MID.nodes, LOW.nodes)
R73 = (FINE.w[:, None] * J73 / MID.w[None, :]).T
R31 = (MID.w[:, None] * J31).T
R73Z = two_elements(FINE.w[:, None] * J73 / MID.w[None, :])
R73Z[PF - 1] = 0.0
R73Z[PF - 1, PM - 1] = FINE.w[0] / MID.w[0]
R31Z = two_elements(MID.w[:, None] * J31)
R31Z[PM - 1] = 0.0
R31Z[PM - 1, PC - 1] = MID.w[0]
J73Z = two_elements(J73)
J31Z = two_elements(J31)

CONSTS = Consts()
for tag, level in (("f", FINE), ("m", MID)):
    CONSTS.add("ky" + tag, np.concatenate(roll_coefs(level.khat)))
    kb = np.zeros(SUB)
    kb[: level.points] = level.kdiag
    kz = np.concatenate([level.kdiag, level.kdiag[1:]])
    CONSTS.add("kzb" + tag, (kz[:, None] + kb[None, :]).reshape(-1))
    ey = np.arange(LANES)
    my = np.ones((SUB, LANES))
    my[0] += ey > 0
    my[level.points - 1] += ey < LANES - 1
    mz = np.ones(level.planes)
    mz[[0, level.points - 1, -1]] = 2
    CONSTS.add("cnt" + tag, (SHIFT_MASS * mz[:, None, None] * my[None]).reshape(-1, LANES))
    CONSTS.add("mz" + tag, np.repeat(SHIFT_MASS * plane_sum(level.points), SUB))
MID_COPIES = np.ones(MID.planes)
MID_COPIES[[0, PM - 1, -1]] = 2
CONSTS.add("mzfull", np.repeat(SHIFT_MASS * MID_COPIES, SUB))
CONSTS.add("r73", np.concatenate(roll_coefs(R73)))
CONSTS.add("j73", np.concatenate(roll_coefs(J73)))
CONSTS.add("r31", np.concatenate(roll_coefs(R31)))
CONSTS.add("j31", np.concatenate([np.pad(J31[:, p], (0, SUB - PM)) for p in range(PC)]))
CONSTS.add("iwb", 1.0 / FINE.w)

DIRS = ((-1, 0), (1, 0), (0, -1), (0, 1), (-1, -1), (-1, 1), (1, -1), (1, 1))
OPP = tuple(DIRS.index((-dx, -dz)) for dx, dz in DIRS)
COEF = 1e-13


def mix(matrix, parts):
    out = []
    for row in np.asarray(matrix):
        acc = None
        for c, v in zip(row, parts):
            if abs(c) > COEF:
                term = v if abs(c - 1.0) < COEF else float(c) * v
                acc = term if acc is None else acc + term
        out.append(acc)
    return out


def mix_even_odd(matrix, parts):
    n = len(parts)
    h = n // 2
    flipped = matrix[:h, ::-1][:, :h]
    even = mix(0.5 * (matrix[:h, :h] + flipped), [parts[i] + parts[n - 1 - i] for i in range(h)])
    odd = mix(0.5 * (matrix[:h, :h] - flipped), [parts[i] - parts[n - 1 - i] for i in range(h)])
    low = [e + o for e, o in zip(even, odd)]
    high = [e - o for e, o in zip(even, odd)]
    return low + high[::-1]


def scratch_shapes(n_node, n_dev):
    f32 = jnp.float32
    low_rows = -(-(3 * (n_dev + 1) + 1) // SUB) * SUB
    shapes = {}
    for tag, level in (("f", FINE), ("m", MID)):
        p, rows = level.points, level.rows
        for name in ("loc", "rhs", "inv", "x", "r", "d", "l"):
            shapes[name + tag] = pltpu.VMEM((p, rows, LANES), f32)
        shapes["cls" + tag] = pltpu.VMEM((3, rows, LANES), f32)
        shapes["dz" + tag] = pltpu.VMEM((rows, LANES), f32)
        shapes["rx" + tag] = pltpu.VMEM((2, 2, level.x_rows, LANES), f32)
        shapes["rz" + tag] = pltpu.VMEM((2, 2, level.z_rows, LANES), f32)
        shapes["sx" + tag] = pltpu.VMEM((2, level.x_rows, LANES), f32)
        shapes["sz" + tag] = pltpu.VMEM((2, level.z_rows, LANES), f32)
        shapes["rc" + tag] = pltpu.VMEM((2, 4, SUB, LANES), f32)
        shapes["ssem" + tag] = pltpu.SemaphoreType.DMA((8,))
        shapes["rsem" + tag] = pltpu.SemaphoreType.DMA((2, 8))
    shapes["tmpf"] = pltpu.VMEM((PF, MID.rows, LANES), f32)
    shapes["tmpm"] = pltpu.VMEM((PM, LOW.rows, LANES), f32)
    shapes["ein"] = pltpu.VMEM((PF * PF * PF * 2, LANES), f32)
    shapes["cst"] = pltpu.VMEM((CONSTS.row, LANES), f32)
    shapes["insem"] = pltpu.SemaphoreType.DMA((PF + 2,))
    shapes["ghost_x"] = pltpu.VMEM((2, 3, MID.planes, SUB, LANES), f32)
    shapes["ghost_z"] = pltpu.VMEM((2, 3, PM, SUB, LANES), f32)
    shapes["side"] = pltpu.VMEM((6, SUB, LANES), f32)
    shapes["dsrc"] = pltpu.VMEM((SUB, LANES), f32)
    shapes["dhalo"] = pltpu.VMEM((8, SUB, LANES), f32)
    shapes["dssem"] = pltpu.SemaphoreType.DMA((8,))
    shapes["drsem"] = pltpu.SemaphoreType.DMA((8,))
    shapes["da"] = pltpu.VMEM((n_dev, SUB, LANES), f32)
    shapes["db"] = pltpu.VMEM((n_node * 2 * n_dev, LANES), f32)
    shapes["ga"] = pltpu.VMEM((n_dev, SUB, LANES), f32)
    shapes["gb"] = pltpu.VMEM(((n_node + 1) * low_rows, LANES), f32)
    half = n_node // 2
    for tag in "dg":
        shapes[tag + "a_s"] = pltpu.SemaphoreType.DMA((n_dev,))
        shapes[tag + "a_r"] = pltpu.SemaphoreType.DMA((n_dev,))
        shapes[tag + "b_s"] = pltpu.SemaphoreType.DMA((half,))
        shapes[tag + "b_r"] = pltpu.SemaphoreType.DMA((half,))
        shapes[tag + "c_s"] = pltpu.SemaphoreType.DMA((half,))
        shapes[tag + "c_r"] = pltpu.SemaphoreType.DMA((half,))
    nx, nz = n_dev + 1, 2 * n_node
    for name in ("wx", "wy", "wym", "wz", "wzm", "dg", "cx", "cr", "cq"):
        shapes["c_" + name] = pltpu.VMEM((nx + 1, nz, LANES), f32)
    shapes["c_wxm"] = pltpu.VMEM((nz, LANES), f32)
    shapes["c_main"] = pltpu.VMEM((nz, LANES), f32)
    shapes["c_p"] = pltpu.VMEM((nx + 1, nz + 2 * SUB, LANES), f32)
    return shapes, low_rows


def make_kernel(n_node, n_dev, names, low_rows):
    half = n_node // 2
    nx, nz = n_dev + 1, 2 * n_node

    def kernel(ein_hbm, diff_hbm, cst_hbm, out_ref, *scratch):
        s = dict(zip(names, scratch))
        node = lax.axis_index("node")
        dev = lax.axis_index("dev")
        sub = lax.broadcasted_iota(jnp.int32, (SUB, LANES), 0)
        lane = lax.broadcasted_iota(jnp.int32, (SUB, LANES), 1)
        has_lo, has_hi = dev > 0, dev < n_dev - 1

        def const(name, index=None):
            row, size = CONSTS.at[name]
            if index is None:
                return s["cst"][row : row + size, :]
            return s["cst"][row + SUB * index : row + SUB * index + SUB, :]

        def neighbour(dx, dz):
            return (lax.rem(node + dz + n_node, n_node), lax.rem(dev + dx + n_dev, n_dev))

        sibling = (node + 1 - 2 * lax.rem(node, 2), dev)

        def same_core(k):
            return lax.rem(node + 2 * k, n_node)

        barrier = pltpu.get_barrier_semaphore()

        def greet(target):
            pl.semaphore_signal(barrier, inc=1, device_id=target, device_id_type=MESH)

        for dx, dz in DIRS:
            greet(neighbour(dx, dz))
        s["dsrc"][...] = jnp.zeros_like(s["dsrc"])
        chunk = PF * PF * 2
        load_diff = pltpu.make_async_copy(
            diff_hbm, s["dsrc"].at[pl.ds(0, 2)], s["insem"].at[PF + 1]
        )
        load_cst = pltpu.make_async_copy(cst_hbm, s["cst"], s["insem"].at[PF])

        def load_in(a):
            rows = pl.ds(a * chunk, chunk)
            return pltpu.make_async_copy(ein_hbm.at[rows], s["ein"].at[rows], s["insem"].at[a])

        load_diff.start()
        for a in (0, PF - 1) + tuple(range(1, PF - 1)):
            load_in(a).start()
        load_cst.start()

        far = lambda k: lax.rem(dev + k, n_dev)

        def greet_far(k, _):
            greet((node, lax.rem(dev + k, n_dev)))
            return 0

        def greet_cores(k, _):
            greet((same_core(k), dev))
            return 0

        lax.fori_loop(1, n_dev, greet_far, 0)
        lax.fori_loop(1, half, greet_cores, 0)

        def wait_barrier():
            pl.semaphore_wait(barrier, n_dev - 1 + half - 1 + len(DIRS))

        def face_copy(tag, par, i):
            level = FINE if tag == "f" else MID
            dx, dz = DIRS[i]
            j = OPP[i]
            if dz == 0:
                src, dst = s["sx" + tag].at[i], s["rx" + tag].at[par, j]
            elif dx == 0:
                src, dst = s["sz" + tag].at[i - 2], s["rz" + tag].at[par, j - 2]
            else:
                a = 0 if dx < 0 else level.points - 1
                zrow = pl.ds(0 if dz < 0 else level.rows - SUB, SUB)
                src, dst = s["loc" + tag].at[a, zrow], s["rc" + tag].at[par, j - 4]
            return pltpu.make_async_remote_copy(
                src_ref=src,
                dst_ref=dst,
                send_sem=s["ssem" + tag].at[i],
                recv_sem=s["rsem" + tag].at[par, j],
                device_id=neighbour(dx, dz),
                device_id_type=MESH,
            )

        def halo_copy(i):
            return pltpu.make_async_remote_copy(
                src_ref=s["dsrc"],
                dst_ref=s["dhalo"].at[OPP[i]],
                send_sem=s["dssem"].at[i],
                recv_sem=s["drsem"].at[OPP[i]],
                device_id=neighbour(*DIRS[i]),
                device_id_type=MESH,
            )

        def start_some(make, which):
            for i in which:
                make(i).start()

        def wait_some(make, which):
            for i in which:
                make(i).wait_send()
            for i in which:
                make(i).wait_recv()

        X_DIRS, Z_DIRS, EDGE_DIRS = (0, 1), (2, 3), (4, 5, 6, 7)
        parity = {"f": 0, "m": 0}

        def start_faces(tag, which):
            start_some(lambda i: face_copy(tag, parity[tag], i), which)

        def pack(tag, parts):
            if tag == "f":
                return parts
            h = -(-len(parts) // 2)
            return [
                parts[i] + pltpu.roll(parts[i + h], PM, 0) if i + h < len(parts) else parts[i]
                for i in range(h)
            ]

        def unpack(tag, v, count):
            parts = [v[SUB * i : SUB * i + SUB] for i in range(v.shape[0] // SUB)]
            if tag == "f":
                return parts
            out = parts + [pltpu.roll(t, PM, 0) for t in parts]
            return [jnp.where(sub < PM, t, 0.0) for t in out[:count]]

        def put(ref, index, parts):
            for i, t in enumerate(parts):
                ref[index, SUB * i : SUB * i + SUB, :] = t

        def add_faces(tag):
            level = FINE if tag == "f" else MID
            par = parity[tag]
            parity[tag] = 1 - par
            wait_some(lambda i: face_copy(tag, par, i), X_DIRS + Z_DIRS)
            buf, rx, rz = (s[n + tag] for n in ("l", "rx", "rz"))
            last, top = level.points - 1, level.rows - SUB
            has = (has_lo, has_hi)
            for side, a in ((0, 0), (1, last)):
                for z, t in enumerate(unpack(tag, rx[par, side], level.planes)):
                    t = jnp.where(has[side], t, 0.0)
                    buf[a, SUB * z : SUB * z + SUB, :] += t
            for side, row in ((0, 0), (1, top)):
                for a, t in enumerate(unpack(tag, rz[par, side], level.points)):
                    buf[a, row : row + SUB, :] += t
            return par

        def sum_y(tag, a, first=0, count=None):
            level = FINE if tag == "f" else MID
            n = level.planes if count is None else count
            buf = s["l" + tag]
            rows_lo = pl.ds(SUB * first, n, stride=SUB)
            rows_hi = pl.ds(SUB * first + level.points - 1, n, stride=SUB)
            lo, hi = buf[a, rows_lo, :], buf[a, rows_hi, :]
            at = lax.broadcasted_iota(jnp.int32, (n, LANES), 1)
            buf[a, rows_lo, :] = lo + jnp.where(at > 0, pltpu.roll(hi, 1, 1), 0.0)
            buf[a, rows_hi, :] = hi + jnp.where(
                at < LANES - 1, pltpu.roll(lo, LANES - 1, 1), 0.0
            )

        def sum_y_planes(tag, row, which):
            p = (FINE if tag == "f" else MID).points
            sel = (which, slice(row, row + SUB))
            t = s["l" + tag][sel]
            across, along = t.ndim - 1, t.ndim - 2
            up = pltpu.roll(t, 1, across)
            down = pltpu.roll(t, LANES - 1, across)
            up = pltpu.roll(up, SUB - p + 1, along)
            down = pltpu.roll(down, p - 1, along)
            t = t + jnp.where((sub == 0) & (lane > 0), up, 0.0)
            t = t + jnp.where((sub == p - 1) & (lane < LANES - 1), down, 0.0)
            s["l" + tag][sel] = t

        def gather_a(tag, k):
            buf = s[tag + "a"]
            return pltpu.make_async_remote_copy(
                src_ref=buf.at[dev],
                dst_ref=buf.at[dev],
                send_sem=s[tag + "a_s"].at[k],
                recv_sem=s[tag + "a_r"].at[k],
                device_id=(node, far(k)),
                device_id_type=MESH,
            )

        block = {"d": 2 * n_dev, "g": low_rows}
        base = {"d": 0, "g": low_rows}

        def slot(tag, index):
            size = block[tag]
            return s[tag + "b"].at[pl.ds(pl.multiple_of(base[tag] + index * size, size), size)]

        def gather_b(tag, k):
            return pltpu.make_async_remote_copy(
                src_ref=slot(tag, node),
                dst_ref=slot(tag, node),
                send_sem=s[tag + "b_s"].at[k],
                recv_sem=s[tag + "b_r"].at[k],
                device_id=(same_core(k), dev),
                device_id_type=MESH,
            )

        def gather_c(tag, k):
            index = lax.rem(node - 2 * k + n_node, n_node)
            return pltpu.make_async_remote_copy(
                src_ref=slot(tag, index),
                dst_ref=slot(tag, index),
                send_sem=s[tag + "c_s"].at[k],
                recv_sem=s[tag + "c_r"].at[k],
                device_id=sibling,
                device_id_type=MESH,
            )

        def plane_rows(z):
            if isinstance(z, int):
                return slice(z * SUB, z * SUB + SUB)
            return pl.ds(pl.multiple_of(z * SUB, SUB), SUB)

        def each(tag, lower, upper, fn):
            if tag == "m":
                for k in range(lower, upper):
                    fn(k)
            else:
                loop(lower, upper, fn)

        def loop(lower, upper, fn):
            def step(k, _):
                fn(k)
                return 0

            lax.fori_loop(lower, upper, step, 0)

        def ring(k, size):
            return min(k % size, -k % size)

        side = 4 if half % 4 == 0 else half
        far_first_dev = sorted(range(1, n_dev), key=lambda k: -ring(k, n_dev))
        far_first_node = sorted(
            range(1, half), key=lambda k: -(ring(k % side, side) + ring(k // side, half // side))
        )

        def start_a(tag):
            for k in far_first_dev:
                gather_a(tag, k).start()

        def wait_a(tag):
            loop(1, n_dev, lambda k: gather_a(tag, k).wait())

        def start_b(tag):
            for k in far_first_node:
                gather_b(tag, k).start()
            gather_c(tag, 0).start()

        def forward_b(tag):
            def one(k):
                gather_b(tag, k).wait_recv()
                gather_c(tag, k).start()

            for k in far_first_node[::-1]:
                one(k)

        def wait_b(tag):
            loop(1, half, lambda k: gather_b(tag, k).wait_send())
            loop(0, half, lambda k: gather_c(tag, k).wait())

        def along_y(tag, v):
            p = (FINE if tag == "f" else MID).points
            acc = const("ky" + tag, 0) * v
            for shift in range(1, SUB):
                if p == PF or shift < p or shift > SUB - p:
                    acc = acc + const("ky" + tag, shift) * pltpu.roll(v, shift, 1)
            return acc

        def along_z(tag, v):
            level = FINE if tag == "f" else MID
            n, p = level.planes, level.points
            parts = [v[SUB * i : SUB * i + SUB] for i in range(n)]
            low = mix_even_odd(level.khat, parts[:p])
            high = mix_even_odd(level.khat, parts[p - 1 :])
            first = s["dz" + tag][0:SUB, :]
            second = s["dz" + tag][level.rows - SUB : level.rows, :]
            out = [first * t for t in low[: p - 1]]
            out.append(first * low[p - 1] + second * high[0])
            out += [second * t for t in high[1:]]
            return out

        def faces(tag, name):
            level = FINE if tag == "f" else MID
            n, p, top = level.planes, level.points, level.rows - SUB
            src, dst, dz = s[name + tag], s["l" + tag], s["dz" + tag]
            mass_row, _ = CONSTS.at["mz" + tag]
            has = (has_lo.astype(jnp.float32), has_hi.astype(jnp.float32))
            ends = (0, p - 1)
            even_row = 0.5 * (level.khat[0:1] + level.khat[0:1, ::-1])[:, : p // 2]
            odd_row = 0.5 * (level.khat[0:1] - level.khat[0:1, ::-1])[:, : p // 2]
            x_edge = {}
            for side, row in ((0, 0), (1, top)):
                rows = slice(row, row + SUB)
                v = src[:, rows, :]
                yt = along_y(tag, v)
                xt = mix_even_odd(level.khat, [v[a] for a in range(p)])
                plane0 = 0 if side == 0 else p - 1
                zt = mix(
                    level.khat[p - 1 : p] if side else level.khat[0:1],
                    [
                        src[:, SUB * (plane0 + c) : SUB * (plane0 + c) + SUB, :]
                        for c in range(p)
                    ],
                )[0]
                weight = dz[rows, :]
                out = [weight * (xt[a] + yt[a] + zt[a]) + SHIFT_MASS * v[a] for a in range(p)]
                for a in range(1, p - 1):
                    dst[a, rows, :] = out[a]
                for f, a in enumerate(ends):
                    x_edge[f, side] = xt[a]
                    out[a] = (
                        out[a]
                        + s["side"][2 * f + side] * (zt[a] + yt[a])
                        + (SHIFT_MASS * has[f]) * v[a]
                    )
                put(s["sz" + tag], side, pack(tag, out))
            start_faces(tag, Z_DIRS)
            chunk = 5 if tag == "f" else n
            for z0 in range(0, n, chunk):
                rows = slice(SUB * z0, SUB * (z0 + chunk))
                v = [src[a, rows, :] for a in range(p)]
                even = mix(even_row, [v[i] + v[p - 1 - i] for i in range(p // 2)])[0]
                odd = mix(odd_row, [v[i] - v[p - 1 - i] for i in range(p // 2)])[0]
                for f, xt in ((0, even + odd), (1, even - odd)):
                    u = v[ends[f]]
                    yt = along_y(tag, u.reshape(chunk, SUB, LANES)).reshape(chunk * SUB, LANES)
                    mass = s["cst"][mass_row + SUB * z0 : mass_row + SUB * (z0 + chunk), :]
                    dst[ends[f], rows, :] = dz[rows, :] * (xt + yt) + mass * u
            for f, a in enumerate(ends):
                out = along_z(tag, src[a])
                out = [t + dst[a, SUB * z : SUB * z + SUB, :] for z, t in enumerate(out)]
                put(dst, a, out)
                out[0] = out[0] + s["side"][4] * x_edge[f, 0]
                out[-1] = out[-1] + s["side"][5] * x_edge[f, 1]
                put(s["sx" + tag], f, pack(tag, out))
            start_faces(tag, X_DIRS)

        def interior(tag, name, after=None):
            level = FINE if tag == "f" else MID
            n, p = level.planes, level.points
            src, dst = s[name + tag], s["l" + tag]

            def plane(z):
                rows = plane_rows(z)
                v = src[:, rows, :]
                acc = along_y(tag, v[1 : p - 1])
                along_x = mix_even_odd(level.khat, [v[a] for a in range(p)])
                weight = s["dz" + tag][rows, :]
                if isinstance(z, int):
                    mass = 2.0 * SHIFT_MASS if z == p - 1 else SHIFT_MASS
                else:
                    mass = jnp.where(z == p - 1, 2.0 * SHIFT_MASS, SHIFT_MASS)
                for a in range(1, p - 1):
                    dst[a, rows, :] = weight * (acc[a - 1] + along_x[a]) + mass * v[a]

            each(tag, 1, n - 1, plane)

            def line(a):
                out = along_z(tag, src[a])
                for i in range(1, n - 1):
                    dst[a, SUB * i : SUB * i + SUB, :] += out[i]
                if after is not None:
                    after(a)

            each(tag, 1, p - 1, line)

        def apply(tag, name):
            level = FINE if tag == "f" else MID
            n, p = level.planes, level.points
            src, dst = s[name + tag], s["l" + tag]

            def plane(z):
                rows = plane_rows(z)
                v = src[:, rows, :]
                acc = along_y(tag, v)
                along_x = mix_even_odd(level.khat, [v[a] for a in range(p)])
                weight = s["dz" + tag][rows, :]
                mass = jnp.where(z == p - 1, 2.0 * SHIFT_MASS, SHIFT_MASS)
                for a in range(p):
                    dst[a, rows, :] = weight * (acc[a] + along_x[a]) + mass * v[a]

            loop(0, n, plane)

            def line(a):
                out = along_z(tag, src[a])
                for i in range(n):
                    dst[a, SUB * i : SUB * i + SUB, :] += out[i]

            loop(0, p, line)

        def update(tag, kind, c1=0.0, c2=0.0, last=False, residual="r"):
            level = FINE if tag == "f" else MID
            c = float(1.0 / level.theta)
            l, rhs, inv, x, r, d = (s[k + tag] for k in ("l", "rhs", "inv", "x", "r", "d"))
            old = s[residual + tag]

            def on(*sel):
                if kind == "zero":
                    res = l[sel]
                    rhs[sel] = res
                    upd = c * inv[sel] * res
                    d[sel] = upd
                    x[sel] = upd
                elif kind == "first":
                    res = rhs[sel] - l[sel]
                    r[sel] = res
                    upd = c * inv[sel] * res
                    d[sel] = upd
                    x[sel] = x[sel] + upd
                else:
                    res = old[sel] - l[sel]
                    upd = c1 * d[sel] + c2 * inv[sel] * res
                    if not last:
                        r[sel] = res
                        d[sel] = upd
                    x[sel] = x[sel] + upd

            return on

        def inner_update(tag, on):
            level = FINE if tag == "f" else MID

            def one(a):
                sum_y(tag, a, 1, level.planes - 2)
                on(a, slice(SUB, level.rows - SUB))

            return one

        def face_update(tag, on):
            level = FINE if tag == "f" else MID
            add_faces(tag)
            for a in (0, level.points - 1):
                sum_y(tag, a)
                on(a, slice(0, level.rows))
            for row in (0, level.rows - SUB):
                sum_y_planes(tag, row, slice(1, level.points - 1))
                on(slice(1, level.points - 1), slice(row, row + SUB))

        def raw_start_x(tag):
            level = FINE if tag == "f" else MID
            buf = s["l" + tag]
            for f, a in ((0, 0), (1, level.points - 1)):
                parts = [buf[a, SUB * z : SUB * z + SUB, :] for z in range(level.planes)]
                put(s["sx" + tag], f, pack(tag, parts))
            start_faces(tag, X_DIRS)

        def raw_start_z(tag):
            level = FINE if tag == "f" else MID
            buf, top = s["l" + tag], level.rows - SUB
            for side, row in ((0, 0), (1, top)):
                parts = [buf[a, row : row + SUB, :] for a in range(level.points)]
                put(s["sz" + tag], side, pack(tag, parts))
            start_faces(tag, Z_DIRS)

        def raw_finish(tag, on, before_faces, before_edges):
            level = FINE if tag == "f" else MID
            buf, last, top = s["l" + tag], level.points - 1, level.rows - SUB
            each(tag, 1, last, inner_update(tag, on))
            before_faces()
            par = add_faces(tag)
            for a in (0, last):
                sum_y(tag, a, 1, level.planes - 2)
                on(a, slice(SUB, top))
            for row in (0, top):
                sum_y_planes(tag, row, slice(1, last))
                on(slice(1, last), slice(row, row + SUB))
            before_edges()
            wait_some(lambda i: face_copy(tag, par, i), EDGE_DIRS)
            for k, (a, row) in enumerate(((0, 0), (0, top), (last, 0), (last, top))):
                rows = slice(row, row + SUB)
                buf[a, rows, :] += jnp.where(has_lo if a == 0 else has_hi, s["rc" + tag][par, k], 0.0)
                sum_y_planes(tag, row, a)
                on(a, rows)

        def steps(tag, count, residual, between, done=0):
            coefs = (FINE if tag == "f" else MID).steps(count)
            for index, (c1, c2) in enumerate(coefs):
                if index < done:
                    continue
                on = update(tag, "next", c1, c2, index == count - 2, residual)
                residual = "r"
                faces(tag, "d")
                interior(tag, "d", inner_update(tag, on))
                between[index]()
                face_update(tag, on)

        ones = [has_lo.astype(jnp.float32), 1.0, has_hi.astype(jnp.float32)]
        copies = [1.0 + ones[0], 1.0, 1.0 + ones[2]]
        def spread_row(row):
            return jnp.broadcast_to(row, (SUB, LANES))

        def patch_row(dx, k):
            dz, row = ((-1, 1), (0, 0), (0, 1), (1, 0))[k]
            ref = s["dsrc"] if (dx, dz) == (0, 0) else s["dhalo"].at[DIRS.index((dx, dz))]
            value = spread_row(ref[row : row + 1, :])
            if dx != 0:
                value = jnp.where(has_lo if dx < 0 else has_hi, value, 0.0)
            return value

        def patch(dx):
            return [patch_row(dx, k) for k in range(4)]

        def kinds_of(q):
            return [q[0] + q[1], q[1], q[1] + q[2], q[2], q[2] + q[3]]

        def kind_of(z, p):
            return {0: 0, p - 1: 2, 2 * p - 2: 4}.get(z, 1 if z < p else 3)

        def nodal(k, p):
            lo = k + jnp.where(lane > 0, pltpu.roll(k, 1, 1), 0.0)
            hi = k + jnp.where(lane < LANES - 1, pltpu.roll(k, LANES - 1, 1), 0.0)
            return jnp.where(sub == 0, lo, jnp.where(sub == p - 1, hi, k))

        def set_inverse(tag, level, a, xc, rows):
            row_k, _ = CONSTS.at["kzb" + tag]
            row_c, _ = CONSTS.at["cnt" + tag]
            kzb = s["cst"][row_k + rows.start : row_k + rows.stop, :]
            cnt = s["cst"][row_c + rows.start : row_c + rows.stop, :]
            diag = (float(level.kdiag[a]) + kzb) * s["cls" + tag][xc, rows, :]
            s["inv" + tag][a, rows, :] = 1.0 / (diag + copies[xc] * cnt)

        def set_class(tag, level, xc, kind, value):
            full = nodal(value, level.points)
            for z in range(level.planes):
                if kind_of(z, level.points) == kind:
                    s["cls" + tag][xc, SUB * z : SUB * z + SUB, :] = full

        def diagonals_inside(tag, level):
            first, second = patch_row(0, 1), patch_row(0, 2)
            kinds = [first, first, first + second, second, second]
            for z in range(level.planes):
                s["dz" + tag][SUB * z : SUB * z + SUB, :] = kinds[kind_of(z, level.points)]
            for kind in (1, 2, 3):
                set_class(tag, level, 1, kind, kinds[kind])
            for a in range(1, level.points - 1):
                set_inverse(tag, level, a, 1, slice(SUB, level.rows - SUB))

        def diagonals_x(tag, level):
            for xc, dx, a in ((0, -1, 0), (2, 1, level.points - 1)):
                first = patch_row(0, 1) + patch_row(dx, 1)
                second = patch_row(0, 2) + patch_row(dx, 2)
                for kind, value in ((1, first), (2, first + second), (3, second)):
                    set_class(tag, level, xc, kind, value)
                set_inverse(tag, level, a, xc, slice(SUB, level.rows - SUB))

        def diagonals_z(tag, level):
            set_class(tag, level, 1, 0, patch_row(0, 0) + patch_row(0, 1))
            set_class(tag, level, 1, 4, patch_row(0, 2) + patch_row(0, 3))
            for a in range(1, level.points - 1):
                set_inverse(tag, level, a, 1, slice(0, SUB))
                set_inverse(tag, level, a, 1, slice(level.rows - SUB, level.rows))

        def diagonals_edges(tag, level):
            for xc, dx, a in ((0, -1, 0), (2, 1, level.points - 1)):
                q = [u + v for u, v in zip(patch(0), patch(dx))]
                set_class(tag, level, xc, 0, q[0] + q[1])
                set_class(tag, level, xc, 4, q[2] + q[3])
                set_inverse(tag, level, a, xc, slice(0, SUB))
                set_inverse(tag, level, a, xc, slice(level.rows - SUB, level.rows))

        def side_diffusivity():
            q = [patch(-1), patch(0), patch(1)]
            for side in range(2):
                s["side"][side] = q[0][1 + side]
                s["side"][2 + side] = q[2][1 + side]
                s["side"][4 + side] = q[1][3 * side]

        def restrict_fine():
            def line(a):
                res = s["locf"][a] - s["lf"][a]
                parts = [res[SUB * i : SUB * i + SUB] for i in range(FINE.planes)]
                for i, t in enumerate(mix(R73Z.T, parts)):
                    s["tmpf"][a, SUB * i : SUB * i + SUB, :] = t

            loop(0, PF, line)

            def plane(z):
                rows = plane_rows(z)
                v = s["tmpf"][:, rows, :]
                t = jnp.stack(mix(R73, [v[a] for a in range(PF)]))
                acc = const("r73", 0) * t
                for shift in range(1, SUB):
                    acc = acc + const("r73", shift) * pltpu.roll(t, shift, 1)
                s["locm"][:, rows, :] = acc
                s["lm"][:, rows, :] = acc

            each("m", 0, MID.planes, plane)

        def prolong_fine():
            def plane(z):
                rows = plane_rows(z)
                v = s["xm"][:, rows, :]
                acc = const("j73", 0) * v
                for shift in range(1, SUB):
                    acc = acc + const("j73", shift) * pltpu.roll(v, shift, 1)
                for a, t in enumerate(mix(J73, [acc[i] for i in range(PM)])):
                    s["tmpf"][a, rows, :] = t

            each("m", 0, MID.planes, plane)

            def line(a):
                v = s["tmpf"][a]
                parts = [v[SUB * i : SUB * i + SUB] for i in range(MID.planes)]
                for i, t in enumerate(mix(J73Z, parts)):
                    s["xf"][a, SUB * i : SUB * i + SUB, :] += t

            loop(0, PF, line)

        def restrict_mid():
            for a in range(PM):
                res = s["locm"][a] - s["lm"][a]
                parts = [res[SUB * i : SUB * i + SUB] for i in range(MID.planes)]
                for i, t in enumerate(mix(R31Z.T, parts)):
                    s["tmpm"][a, SUB * i : SUB * i + SUB, :] = t
            spare = jnp.zeros((SUB, LANES), jnp.float32)
            for z in range(3):
                v = s["tmpm"][:, SUB * z : SUB * z + SUB, :]
                for a, t in enumerate(mix(R31, [v[i] for i in range(PM)])):
                    acc = const("r31", 0) * t
                    for shift in (1, 5, 6, 7):
                        acc = acc + const("r31", shift) * pltpu.roll(t, shift, 0)
                    up = pltpu.roll(pltpu.roll(acc, 1, 1), SUB - 1, 0)
                    node_row = acc + jnp.where(lane > 0, up, 0.0)
                    s["ga"][dev, 3 * a + z : 3 * a + z + 1, :] = node_row[0:1, :]
                    spare = spare + jnp.where(lane == z * nx + dev + a, up[0:1, 0:1], 0.0)
            s["ga"][dev, 6:7, :] = spare[0:1, :]
            s["ga"][dev, 7:8, :] = jnp.zeros((1, LANES), jnp.float32)

        def sum_x_low():
            flat = s["ga"]
            g = jnp.zeros((low_rows, LANES), jnp.float32)
            pad = lambda rows, before: jnp.pad(
                rows, ((before, low_rows - before - rows.shape[0]), (0, 0))
            )
            mine = s["gb"].at[
                pl.ds(pl.multiple_of(low_rows + node * low_rows, low_rows), low_rows)
            ]
            mine[...] = g
            for z in range(3):
                mine[z * nx : z * nx + n_dev, :] = flat[:, z, :]
                mine[z * nx + 1 : z * nx + nx, :] += flat[:, 3 + z, :]
            mine[3 * nx : 3 * nx + 1, :] = jnp.sum(flat[:, 6, :], axis=0, keepdims=True)

        low_lane = lax.broadcasted_iota(jnp.int32, (nz, LANES), 1)
        LAST = LANES - 1

        def ahead(v):
            return jnp.where(low_lane > 0, pltpu.roll(v, 1, 1), 0.0)

        def to_end(x, v):
            return jnp.where(low_lane == x, pltpu.roll(v, x + 1, 1), 0.0)

        def low_weights():
            up_z = lambda v: pltpu.roll(v, 1, 0)
            elem = lambda x: s["db"][pl.ds(x, nz, stride=n_dev), :]
            zero = jnp.zeros((nz, LANES), jnp.float32)
            y_copies = jnp.where(low_lane > 0, 2.0, 1.0)
            end_wx = end_wy = end_wz = zero
            for x in range(nx):
                lo = elem(x - 1) if x > 0 else zero
                hi = elem(x) if x < n_dev else zero
                both = lo + hi
                wy = 0.5 * (both + up_z(both))
                wym = ahead(wy)
                wz = 0.5 * (both + ahead(both))
                wzm = up_z(wz)
                hz = hi + up_z(hi)
                wx = 0.5 * (hz + ahead(hz))
                wxm = s["c_wx"][x - 1] if x > 0 else zero
                s["c_wy"][x] = wy
                s["c_wym"][x] = wym
                s["c_wz"][x] = wz
                s["c_wzm"][x] = wzm
                s["c_wx"][x] = wx
                x_copies = 1.0 if x in (0, n_dev) else 2.0
                s["c_dg"][x] = wx + wxm + wy + wym + wz + wzm + 2.0 * SHIFT_MASS * x_copies * y_copies
                end_wx = end_wx + to_end(x, 0.5 * hz)
                end_wy = end_wy + to_end(x, wy)
                end_wz = end_wz + to_end(x, 0.5 * both)
            end_wxm, end_wzm = ahead(end_wx), up_z(end_wz)
            x_copies = jnp.where((low_lane == 0) | (low_lane == n_dev), 1.0, 2.0)
            x_copies = jnp.where(low_lane < nx, x_copies, 0.0)
            s["c_wx"][nx] = end_wx
            s["c_wxm"][...] = end_wxm
            s["c_wy"][nx] = end_wy
            s["c_wz"][nx] = end_wz
            s["c_wzm"][nx] = end_wzm
            s["c_dg"][nx] = (
                end_wx + end_wxm + end_wy + end_wz + end_wzm + 2.0 * SHIFT_MASS * x_copies
            )

        def low_rhs():
            buf = s["gb"]
            buf[0:low_rows, :] = buf[n_node * low_rows : (n_node + 1) * low_rows, :]
            own = lambda row: buf[pl.ds(low_rows + row, n_node, stride=low_rows), :]
            before = lambda row: buf[pl.ds(row, n_node, stride=low_rows), :]
            at = lax.broadcasted_iota(jnp.int32, (n_node, LANES), 1)
            spare, spare_before = own(3 * nx), before(3 * nx)

            def pick(rows, first):
                moved = rows if first == 0 else pltpu.roll(rows, LANES - first, 1)
                return jnp.where(at < nx, moved, 0.0)

            even, odd = pl.ds(0, n_node, stride=2), pl.ds(1, n_node, stride=2)
            res, main = s["c_cr"], s["c_main"]
            for x in range(nx):
                main[even, :] = own(x) + before(2 * nx + x)
                main[odd, :] = own(nx + x)
                res[x] = main[...]
            main[even, :] = pick(spare, 0) + pick(spare_before, 2 * nx)
            main[odd, :] = pick(spare, nx)
            res[nx] = main[...]

        def fold(v):
            parts = [v[i : i + SUB] for i in range(0, v.shape[0], SUB)]
            while len(parts) > 1:
                parts = [u + w for u, w in zip(parts[::2], parts[1::2])] + (
                    [parts[-1]] if len(parts) % 2 else []
                )
            return parts[0]

        def total(v):
            return jnp.sum(v, axis=(0, 1), keepdims=True)

        def set_direction(x, value):
            p = s["c_p"]
            p[x, SUB : SUB + nz, :] = value
            p[x, 0:SUB, :] = value[nz - SUB : nz]
            p[x, SUB + nz : 2 * SUB + nz, :] = value[0:SUB]

        def coarse_solve():
            p, q, res, sol = s["c_p"], s["c_cq"], s["c_cr"], s["c_cx"]
            here = pl.ds(SUB, nz)
            norm = jnp.zeros((SUB, LANES), jnp.float32)
            for x in range(nx + 1):
                v = res[x]
                set_direction(x, v)
                sol[x] = jnp.zeros_like(v)
                norm = norm + fold(v * v)

            def along_pipe(x):
                out = s["c_wz"][x] * p[x, SUB + 1 : SUB + 1 + nz, :]
                return out + s["c_wzm"][x] * p[x, SUB - 1 : SUB - 1 + nz, :]

            def step_length(now):
                dot = jnp.zeros((SUB, LANES), jnp.float32)
                end = p[nx, here, :]
                last = jnp.zeros((nz, LANES), jnp.float32)
                for x in range(nx):
                    v = p[x, here, :]
                    out = s["c_dg"][x] * v
                    if x > 0:
                        out = out - s["c_wx"][x - 1] * p[x - 1, here, :]
                    if x < nx - 1:
                        out = out - s["c_wx"][x] * p[x + 1, here, :]
                    above = jnp.where(
                        low_lane == LAST, pltpu.roll(end, LAST - x, 1), pltpu.roll(v, LAST, 1)
                    )
                    below = pltpu.roll(v, 1, 1)
                    out = out - s["c_wy"][x] * above - s["c_wym"][x] * below
                    out = out - along_pipe(x)
                    q[x] = out
                    dot = dot + fold(v * out)
                    last = jnp.where(low_lane == x, pltpu.roll(v, x + 1, 1), last)
                out = s["c_dg"][nx] * end - s["c_wx"][nx] * pltpu.roll(end, LAST, 1)
                out = out - s["c_wxm"][...] * pltpu.roll(end, 1, 1)
                out = out - s["c_wy"][nx] * last - along_pipe(nx)
                q[nx] = out
                dot = dot + fold(end * out)
                return now / total(dot)

            def iteration(_, now):
                alpha = step_length(now)
                norm = jnp.zeros((SUB, LANES), jnp.float32)
                for x in range(nx + 1):
                    sol[x] += alpha * p[x, here, :]
                    v = res[x] - alpha * q[x]
                    res[x] = v
                    norm = norm + fold(v * v)
                new = total(norm)
                beta = new / now
                for x in range(nx + 1):
                    set_direction(x, res[x] + beta * p[x, here, :])
                return new

            alpha = step_length(lax.fori_loop(0, COARSE_ITERS - 1, iteration, total(norm)))
            for x in range(nx + 1):
                sol[x] += alpha * p[x, here, :]

        n3, edge_slope = MID.planes, float((MID.khat @ J31)[0, 0])

        def stacked(parts):
            return jnp.stack(list(parts))

        def exists(o):
            return (dev + o >= 0) & (dev + o < n_dev)

        def diff_at(o, k):
            x = jnp.clip(dev + o, 0, n_dev - 1)
            z = lax.rem(2 * node + k + nz, nz)
            row = spread_row(s["db"][pl.ds(z * n_dev + x, 1), :])
            return row if o == 0 else jnp.where(exists(o), row, 0.0)

        def over_planes(q):
            kinds = kinds_of(q)
            return stacked(kinds[kind_of(z, PM)] for z in range(n3))

        def column(o):
            return [diff_at(o, k) for k in (-1, 0, 1, 2)]

        def add_rows(p, q):
            return [u + v for u, v in zip(p, q)]

        def copies_at(o, a):
            if a == 0:
                return 1.0 + exists(o - 1).astype(jnp.float32)
            if a == PM - 1:
                return 1.0 + exists(o + 1).astype(jnp.float32)
            return 1.0

        def around(o, a):
            q = column(o)
            if a == 0:
                q = add_rows(q, column(o - 1))
            if a == PM - 1:
                q = add_rows(q, column(o + 1))
            return q

        def spread_low(i, k):
            x = jnp.clip(dev + i, 0, n_dev)
            z = lax.rem(2 * node + k + nz, nz)
            low = spread_row(s["c_cx"][x, pl.ds(z, 1), :])
            end = pltpu.roll(spread_row(s["c_cx"][nx, pl.ds(z, 1), :]), LAST - x, 1)
            high = jnp.where(lane < LAST, pltpu.roll(low, LAST, 1), end)
            return const("j31", 0) * low + const("j31", 1) * high

        def once(fn):
            seen = {}

            def get(*key):
                if key not in seen:
                    seen[key] = fn(*key)
                return seen[key]

            return get

        def y_summed(v):
            across, along = v.ndim - 1, v.ndim - 2
            up = pltpu.roll(pltpu.roll(v, 1, across), SUB - PM + 1, along)
            down = pltpu.roll(pltpu.roll(v, LANES - 1, across), PM - 1, along)
            v = v + jnp.where((sub == 0) & (lane > 0), up, 0.0)
            return v + jnp.where((sub == PM - 1) & (lane < LANES - 1), down, 0.0)

        def low_tools():
            node_at = once(spread_low)
            line_at = once(lambda i: stacked(mix(J31Z, [node_at(i, k) for k in (0, 1, 2)])))
            mass = const("mzfull").reshape(n3, SUB, LANES)
            h = edge_slope

            def along_line(o, a):
                pick = lambda f: mix(J31[a : a + 1], [f(o), f(o + 1)])[0]
                u = pick(line_at)
                before, after = pick(lambda i: node_at(i, -1)), pick(lambda i: node_at(i, 3))
                w = around(o, a)
                out = over_planes(w) * along_y("m", u) + copies_at(o, a) * mass * u
                f0, f1 = w[0] * (u[0] - before), w[1] * (u[PM - 1] - u[0])
                f2, f3 = w[2] * (u[n3 - 1] - u[PM - 1]), w[3] * (after - u[n3 - 1])
                zero = jnp.zeros((SUB, LANES), jnp.float32)
                flow = [zero] * n3
                flow[0], flow[PM - 1], flow[n3 - 1] = f0 - f1, f1 - f2, f2 - f3
                out = out + h * stacked(flow)
                if a in (0, PM - 1):
                    inner = line_at(o + 1) if a == 0 else line_at(o)
                    outer_o = o - 1 if a == 0 else o + 1
                    outer = line_at(o - 1) if a == 0 else line_at(o + 2)
                    out = out + h * (
                        over_planes(column(o)) * (u - inner)
                        + over_planes(column(outer_o)) * (u - outer)
                    )
                return u, out

            def beyond_z(side, c):
                k = -1 if side == 0 else 2
                far = c == (0 if side == 0 else PM - 1)
                other = k - 1 if side == 0 else k + 1
                at_x = once(lambda i: mix(J31[c : c + 1], [node_at(i, k), node_at(i, k + 1)])[0])
                across = lambda kk: stacked(mix(J31, [node_at(0, kk), node_at(1, kk)]))
                weights = once(lambda o: diff_at(o, k) + diff_at(o, other) if far else diff_at(o, k))
                u = stacked(mix(J31, [at_x(0), at_x(1)]))
                sums = lambda f: stacked(
                    [f(0) + f(-1), f(0), f(0), f(0) + f(1)]
                )
                total_w = sums(weights)
                copies3 = [copies_at(0, a) * (2.0 if far else 1.0) * SHIFT_MASS for a in range(PM)]
                out = total_w * along_y("m", u) + stacked(copies3[a] * u[a] for a in range(PM))
                zero = jnp.zeros((SUB, LANES), jnp.float32)
                flow = [zero] * PM
                flow[0] = weights(-1) * (u[0] - at_x(-1)) + weights(0) * (u[0] - u[PM - 1])
                flow[PM - 1] = weights(0) * (u[PM - 1] - u[0]) + weights(1) * (u[PM - 1] - at_x(2))
                out = out + h * stacked(flow)
                if far:
                    inner, outer = (across(k + 1), across(k - 1)) if side == 0 else (
                        across(k),
                        across(k + 2),
                    )
                    out = out + h * (
                        sums(lambda o: diff_at(o, k)) * (u - inner)
                        + sums(lambda o: diff_at(o, other)) * (u - outer)
                    )
                return out

            return along_line, beyond_z

        beyond_x = ((-1, (0, 1, 2), MID.khat[PM - 1]), (1, (1, 2, 3), MID.khat[0]))
        beyond_c = (((0, 1, 2), MID.khat[PM - 1]), ((1, 2, 3), MID.khat[0]))

        def ghost_diagonals():
            theta = MID.theta
            my = 1.0 + jnp.where(((sub == 0) & (lane > 0)) | ((sub == PM - 1) & (lane < LAST)), 1.0, 0.0)
            kb = mirrored_rows(MID.kdiag)
            kz = [float(v) for v in np.concatenate([MID.kdiag, MID.kdiag[1:]])]
            for side, (o, points, row) in enumerate(beyond_x):
                for index, a in enumerate(points):
                    kinds = [nodal(k, PM) for k in kinds_of(around(o, a))]
                    for z in range(n3):
                        diag = (float(MID.kdiag[a]) + kz[z] + kb) * kinds[kind_of(z, PM)]
                        diag = diag + (float(MID_COPIES[z]) * SHIFT_MASS * copies_at(o, a)) * my
                        s["ghost_x"][side, index, z] = float(row[a] / theta) / diag
            for side, (planes, row) in enumerate(beyond_c):
                k = -1 if side == 0 else 2
                other = k - 1 if side == 0 else k + 1
                for index, c in enumerate(planes):
                    far = c in (0, PM - 1)
                    weights = lambda o: diff_at(o, k) + diff_at(o, other) if far else diff_at(o, k)
                    for a in range(PM):
                        w = weights(0)
                        if a in (0, PM - 1):
                            w = w + weights(-1 if a == 0 else 1)
                        diag = (float(MID.kdiag[a] + MID.kdiag[c]) + kb) * nodal(w, PM)
                        scale = (2.0 if far else 1.0) * SHIFT_MASS * copies_at(0, a)
                        s["ghost_z"][side, index, a] = float(row[c] / theta) / (diag + scale * my)

        def mirrored_rows(values):
            out = jnp.zeros((SUB, LANES), jnp.float32)
            for i, v in enumerate(values):
                out = jnp.where(sub == i, float(v), out)
            return out

        def send_known_part():
            c = float(1.0 / MID.theta)
            for a in range(PM):
                sum_y("m", a)
                res = s["rhsm"][a] - s["lm"][a]
                s["rm"][a] = res
                s["dm"][a] = c * s["invm"][a] * res
            plane = lambda z: s["dm"][:, SUB * z : SUB * z + SUB, :]
            for side, (points, row) in enumerate(((range(1, PM), 0), (range(PM - 1), PM - 1))):
                rows = [s["dm"][a] for a in points]
                t = mix(MID.khat[row : row + 1, list(points)], rows)[0]
                put(s["sxm"], side, pack("m", [t[SUB * z : SUB * z + SUB] for z in range(n3)]))
                first = 0 if side == 0 else PM - 1
                t = mix(MID.khat[row : row + 1, list(points)], [plane(first + c) for c in points])[0]
                put(s["szm"], side, pack("m", [t[a] for a in range(PM)]))
            start_faces("m", X_DIRS + Z_DIRS)

        def after_coarse(c1, c2):
            c = float(1.0 / MID.theta)
            along_line, beyond_z = low_tools()
            shape = (n3, SUB, LANES)
            flat = (MID.rows, LANES)
            par = parity["m"]
            parity["m"] = 1 - par
            for a in range(PM):
                u, rho = along_line(0, a)
                res = s["rm"][a] - y_summed(rho).reshape(flat)
                upd = c * s["invm"][a] * res
                s["rm"][a] = res
                s["dm"][a] = upd
                s["xm"][a] = s["xm"][a] + u.reshape(flat) + upd
            for side, (o, points, row) in enumerate(beyond_x):
                acc = None
                for index, a in enumerate(points):
                    _, rho = along_line(o, a)
                    t = s["ghost_x"][side, index] * y_summed(rho)
                    acc = t if acc is None else acc + t
                s["tmpf"][side] = acc.reshape(flat)
            for side, (planes, row) in enumerate(beyond_c):
                acc = None
                for index, cc in enumerate(planes):
                    t = s["ghost_z"][side, index] * y_summed(beyond_z(side, cc))
                    acc = t if acc is None else acc + t
                s["tmpf"][2 + side, 0 : PM * SUB, :] = acc.reshape(PM * SUB, LANES)
            wait_some(lambda i: face_copy("m", par, i), X_DIRS + Z_DIRS)
            d = [s["dm"][a].reshape(shape) for a in range(PM)]
            own_x = mix_even_odd(MID.khat, d)
            last = float(MID.khat[PM - 1, PM - 1])
            terms_x = []
            for side, a in ((0, 0), (1, PM - 1)):
                t = stacked(unpack("m", s["rxm"][par, side], n3)) - s["tmpf"][side].reshape(shape)
                terms_x.append(t + last * d[a])
            terms_z = []
            for side, z in ((0, 0), (1, n3 - 1)):
                t = stacked(unpack("m", s["rzm"][par, side], PM))
                t = t - s["tmpf"][2 + side, 0 : PM * SUB, :].reshape(PM, SUB, LANES)
                terms_z.append(t + last * stacked(v[z] for v in d))
            mass = const("mzfull").reshape(shape)
            here = over_planes(column(0))
            for a in range(PM):
                w = around(0, a)
                out = over_planes(w) * along_y("m", d[a]) + copies_at(0, a) * mass * d[a]
                out = out + here * own_x[a]
                if a == 0:
                    out = out + over_planes(column(-1)) * terms_x[0]
                if a == PM - 1:
                    out = out + over_planes(column(1)) * terms_x[1]
                low = mix_even_odd(MID.khat, [d[a][z] for z in range(PM)])
                high = mix_even_odd(MID.khat, [d[a][z] for z in range(PM - 1, n3)])
                along = [w[1] * v for v in low] + [w[2] * v for v in high[1:]]
                along[PM - 1] = along[PM - 1] + w[2] * high[0]
                along[0] = along[0] + w[0] * terms_z[0][a]
                along[n3 - 1] = along[n3 - 1] + w[3] * terms_z[1][a]
                out = y_summed(out + stacked(along)).reshape(flat)
                res = s["rm"][a] - out
                upd = c1 * s["dm"][a] + c2 * s["invm"][a] * res
                s["lm"][a] = res
                s["locm"][a] = upd
            for a in range(PM):
                s["rm"][a] = s["lm"][a]
                s["dm"][a] = s["locm"][a]
                s["xm"][a] = s["xm"][a] + s["locm"][a]

        nothing = lambda: None
        load_diff.wait()
        s["da"][dev] = s["dsrc"][...]
        wz = np.concatenate([FINE.w, FINE.w[1:]])

        def mirrored(index, values):
            out = jnp.float32(values[0])
            for i in range(1, PF // 2):
                out = jnp.where((index == i) | (index == PF - 1 - i), float(values[i]), out)
            return out

        across_y = mirrored(sub, 1.0 / FINE.w)

        def load_line(a):
            planes = []
            for e in range(2):
                for c in range(PF):
                    start = a * chunk + 2 * c + e
                    planes.append(s["ein"][pl.ds(start, SUB, stride=2 * PF), :])
            merged = planes[: PF - 1] + [planes[PF - 1] + planes[PF]] + planes[PF + 1 :]
            scale = across_y * mirrored(jnp.int32(a), 1.0 / FINE.w)
            for z, v in enumerate(merged):
                t = scale * v * float(1.0 / wz[z])
                s["locf"][a, SUB * z : SUB * z + SUB, :] = t
                s["lf"][a, SUB * z : SUB * z + SUB, :] = t

        for a in (0, PF - 1):
            load_in(a).wait()
            load_line(a)
        wait_barrier()
        start_some(halo_copy, range(8))
        start_faces("f", EDGE_DIRS)
        raw_start_x("f")
        for a in range(1, PF - 1):
            load_in(a).wait()
        loop(1, PF - 1, load_line)
        raw_start_z("f")
        load_cst.wait()
        diagonals_inside("f", FINE)
        diagonals_inside("m", MID)

        def halo_sides():
            start_a("d")
            wait_some(halo_copy, X_DIRS)
            diagonals_x("f", FINE)
            wait_some(halo_copy, Z_DIRS)
            diagonals_z("f", FINE)

        def halo_edges():
            wait_some(halo_copy, EDGE_DIRS)
            diagonals_edges("f", FINE)

        def diff_stage_b():
            wait_a("d")
            mine = slot("d", node)
            for e in range(2):
                mine[e * n_dev : (e + 1) * n_dev, :] = s["da"][:, e, :]
            start_b("d")

        raw_finish("f", update("f", "zero"), halo_sides, halo_edges)
        side_diffusivity()
        steps("f", SMOOTH_FINE, "rhs", [diff_stage_b, lambda: forward_b("d")])
        apply("f", "x")
        restrict_fine()

        start_faces("m", EDGE_DIRS)
        raw_start_z("m")
        raw_start_x("m")

        def order3_faces():
            diagonals_x("m", MID)
            diagonals_z("m", MID)
            diagonals_edges("m", MID)
            wait_b("d")

        raw_finish("m", update("m", "zero"), order3_faces, nothing)
        steps("m", SMOOTH_MID, "rhs", [low_weights, ghost_diagonals])
        faces("m", "x")
        interior("m", "x")
        restrict_mid()
        start_a("g")
        add_faces("m")
        send_known_part()
        wait_a("g")
        sum_x_low()
        start_b("g")
        forward_b("g")
        wait_b("g")
        low_rhs()
        coarse_solve()
        coefs = MID.steps(SMOOTH_MID)
        after_coarse(*coefs[0])
        steps("m", SMOOTH_MID, "r", [nothing, nothing], 1)
        prolong_fine()
        first = update("f", "first")
        faces("f", "x")
        interior("f", "x", inner_update("f", first))
        face_update("f", first)
        steps("f", SMOOTH_FINE, "r", [nothing, nothing])

        def store_line(a):
            for e in range(2):
                for c in range(PF):
                    z = e * (PF - 1) + c
                    start = a * chunk + 2 * c + e
                    out_ref[pl.ds(start, SUB, stride=2 * PF), :] = s["xf"][
                        a, SUB * z : SUB * z + SUB, :
                    ]

        loop(0, PF, store_line)

    return kernel


def solution(mesh):
    n_node, n_dev = mesh.shape["node"], mesh.shape["dev"]
    shapes, low_rows = scratch_shapes(n_node, n_dev)
    kernel = make_kernel(n_node, n_dev, list(shapes), low_rows)
    rows = PF * PF * PF * 2

    def local(element_load, diffusivity):
        out = pl.pallas_call(
            kernel,
            out_shape=pltpu.VMEM((rows, LANES), jnp.float32),
            in_specs=[pl.BlockSpec(memory_space=pltpu.HBM)] * 3,
            out_specs=pl.BlockSpec(memory_space=pltpu.VMEM),
            scratch_shapes=list(shapes.values()),
            compiler_params=pltpu.CompilerParams(
                collective_id=0, has_side_effects=True, vmem_limit_bytes=48 * 1024 * 1024
            ),
        )(
            pltpu.with_memory_space_constraint(element_load.reshape(rows, LANES), pltpu.HBM),
            pltpu.with_memory_space_constraint(diffusivity.reshape(2, LANES), pltpu.HBM),
            pltpu.with_memory_space_constraint(jnp.asarray(CONSTS.array()), pltpu.HBM),
        )
        return out.reshape(element_load.shape)

    return jax.shard_map(
        local,
        mesh=mesh,
        in_specs=(P(None, None, None, "dev", "node", None), P("dev", "node", None)),
        out_specs=P(None, None, None, "dev", "node", None),
        check_vma=False,
    )
```
